128 devices in a mesh: slab: 32 (over y, z, core), sub: 4 (over x).
Axes of the slice: x: 4, y: 4, z: 4, core: 2. Of those that a mesh axis runs over, the one named last changes fastest.
Arguments:
- positions: float32 [3, 786432], P(None, ('slab', 'sub')), may hold values from 0 to 128, as said below
- forces: float32 [12, 786432], P(None, ('slab', 'sub')), may hold values from -30 to 30
- tile_rows: int32 [16384], P(('slab', 'sub')), may hold values from 0 to 4095, as said below
- tile_cols: int32 [16384], P(('slab', 'sub')), may hold values from 0 to 4095, as said below
- tile_count: int32 [128], P(('slab', 'sub')), may hold values from 1 to 128, as said below
Outputs:
- first_vectors: float32 [12, 786432], P(None, ('slab', 'sub'))
- second_vectors: float32 [12, 786432], P(None, ('slab', 'sub'))
The draws below stay inside these ranges and needn't reach their ends.
Inputs may be any that keep to these rules, and one draw needn't show every extreme that they name: `tile_rows`: slot t names a block of the device that holds slot t: t div 128 times 32 plus 0 to 31. `tile_cols`: slot t names a block whose slab (the block divided by 128, rounded down) is the slab of slot t's device or one of the two beside it. `tile_count`: some device has all 128 slots live. `positions`: the first coordinate of a bead of slab s lies in [4 s, 4 s + 4), the others in [0, 6).
All inputs are finite; a program needn't handle non-finite values.
Results may differ from the reference program's by a relative error of at most 0.0003.
Values sent between devices are 32-bit elements; how exact they have to be, the bound alone decides.
A program may use at most 128 MiB of HBM per device.

```python
import jax
import jax.numpy as jnp
from jax import lax

BLOCK = 192
BLOCKS_DEV = 32
TILES_DEV = 128
N_SLAB = 32
N_SUB = 4


def draw_positions(key, part):
    key = jax.random.fold_in(key, 1)
    bead_total = BLOCK * BLOCKS_DEV * N_SLAB * N_SUB
    along_key, across_key = jax.random.split(key)
    slab_of = (jnp.arange(bead_total, dtype=jnp.int32) // (BLOCK * BLOCKS_DEV * N_SUB)).astype(jnp.float32)
    along_coord = jax.random.uniform(along_key, (bead_total,), jnp.float32, 0.0, 4.0) + 4.0 * slab_of
    across = jax.random.uniform(across_key, (2, bead_total), jnp.float32, 0.0, 6.0)
    return jnp.concatenate([along_coord[None], across], axis=0)


def draw_forces(key, part):
    key = jax.random.fold_in(key, 2)
    bead_total = BLOCK * BLOCKS_DEV * N_SLAB * N_SUB
    rising = 1.0 + 2.0 * jnp.arange(bead_total, dtype=jnp.float32) / bead_total
    return jnp.clip(jax.random.normal(key, (12, bead_total), jnp.float32), -6.0, 6.0) * rising


def draw_tile_rows(key, part):
    key = jax.random.fold_in(key, 4)
    slot_total = TILES_DEV * N_SLAB * N_SUB
    slot_dev = jnp.arange(slot_total, dtype=jnp.int32) // TILES_DEV
    local_pick = jax.random.randint(key, (slot_total,), 0, BLOCKS_DEV)
    return (slot_dev * BLOCKS_DEV + local_pick).astype(jnp.int32)


def draw_tile_cols(key, part):
    key = jax.random.fold_in(key, 5)
    slot_total = TILES_DEV * N_SLAB * N_SUB
    slot_dev = jnp.arange(slot_total, dtype=jnp.int32) // TILES_DEV
    slab_key, sub_key, local_key = jax.random.split(key, 3)
    slab_of = slot_dev // N_SUB
    target = jnp.clip(slab_of + jax.random.randint(slab_key, (slot_total,), -1, 2), 0, N_SLAB - 1)
    sub_pick = jax.random.randint(sub_key, (slot_total,), 0, N_SUB)
    local_pick = jax.random.randint(local_key, (slot_total,), 0, BLOCKS_DEV)
    return ((target * N_SUB + sub_pick) * BLOCKS_DEV + local_pick).astype(jnp.int32)


def draw_tile_count(key, part):
    key = jax.random.fold_in(key, 3)
    device_total = N_SLAB * N_SUB
    light_key, heavy_key, slab_key, pick_key = jax.random.split(key, 4)
    light_load = jax.random.randint(light_key, (device_total,), max(TILES_DEV // 8, 1), TILES_DEV // 2 + 1)
    heavy_load = jax.random.randint(heavy_key, (device_total,), TILES_DEV * 3 // 4, TILES_DEV + 1)
    dense_slab = jax.random.randint(slab_key, (), 0, N_SLAB)
    slab_of = jnp.arange(device_total, dtype=jnp.int32) // N_SUB
    counts = jnp.where(slab_of == dense_slab, heavy_load, light_load)
    fullest = dense_slab * N_SUB + jax.random.randint(pick_key, (), 0, N_SUB)
    return jnp.where(jnp.arange(device_total, dtype=jnp.int32) == fullest, TILES_DEV, counts).astype(jnp.int32)


def setup_inputs(seed: int = 0) -> dict:
    splits = jax.random.split(jax.random.key(seed), 6)
    positions = draw_positions(jax.random.fold_in(splits[5], 71), 0)
    forces = draw_forces(jax.random.fold_in(splits[5], 71), 0)
    tile_rows = draw_tile_rows(jax.random.fold_in(splits[5], 71), 0)
    tile_cols = draw_tile_cols(jax.random.fold_in(splits[5], 71), 0)
    tile_count = draw_tile_count(jax.random.fold_in(splits[5], 71), 0)
    return dict(positions=positions, forces=forces, tile_rows=tile_rows, tile_cols=tile_cols, tile_count=tile_count)


cutoff_sq = 64.0
group_size = 8

def mobility_tile(pos_row, pos_col):
    offset = pos_row[:, :, None] - pos_col[:, None, :]
    dist_sq = lax.optimization_barrier(jnp.sum(offset * offset, axis=0))
    radius = jnp.sqrt(jnp.maximum(dist_sq, 1e-12))
    inverse = 1.0 / radius
    inverse_sq = inverse * inverse
    far_iso = 0.75 * inverse * (1.0 + inverse_sq * (2.0 / 3.0))
    far_dyad = 0.75 * inverse * (1.0 - 2.0 * inverse_sq) * inverse_sq
    near_iso = 1.0 - radius * (9.0 / 32.0)
    near_dyad = inverse * (3.0 / 32.0)
    touching = dist_sq < 4.0
    tapering = jnp.square(jnp.maximum(1.0 - dist_sq / cutoff_sq, 0.0))
    isotropic = jnp.where(touching, near_iso, far_iso) * tapering
    dyadic = jnp.where(touching, near_dyad, far_dyad) * tapering
    identity = jnp.eye(3, dtype=pos_row.dtype)
    return identity[:, :, None, None] * isotropic + offset[:, None] * offset[None, :] * dyadic

def apply_mobility(positions, columns, tile_rows, tile_cols, tile_count):
    block_total = positions.shape[1] // BLOCK
    pos_blocks = positions.reshape(3, block_total, BLOCK)
    col_blocks = columns.reshape(12, block_total, BLOCK)
    slot_total = TILES_DEV * N_SLAB * N_SUB
    slot_ids = jnp.arange(slot_total, dtype=jnp.int32)
    alive_weight = (slot_ids % TILES_DEV < tile_count[slot_ids // TILES_DEV]).astype(columns.dtype)
    group_total = slot_total // group_size

    def tile_group(totals, packet):
        row_pick, col_pick, weight = packet
        tile_blocks = jax.vmap(mobility_tile, in_axes=(1, 1))(jnp.take(pos_blocks, row_pick, axis=1), jnp.take(pos_blocks, col_pick, axis=1))
        force_row = (jnp.take(col_blocks, row_pick, axis=1) * weight[None, :, None]).reshape(4, 3, group_size, BLOCK)
        force_col = (jnp.take(col_blocks, col_pick, axis=1) * weight[None, :, None]).reshape(4, 3, group_size, BLOCK)
        to_rows = jnp.einsum('kbgj,gabij->kagi', force_col, tile_blocks, precision=lax.Precision.HIGHEST)
        to_cols = jnp.einsum('kagi,gabij->kbgj', force_row, tile_blocks, precision=lax.Precision.HIGHEST)
        totals = totals.at[:, row_pick].add(to_rows.reshape(12, group_size, BLOCK))
        totals = totals.at[:, col_pick].add(to_cols.reshape(12, group_size, BLOCK))
        return (totals, None)
    packets = (tile_rows.reshape(group_total, group_size), tile_cols.reshape(group_total, group_size), alive_weight.reshape(group_total, group_size))
    totals, _ = lax.scan(tile_group, col_blocks, packets)
    return totals.reshape(12, block_total * BLOCK)

def normalize(values):
    grouped = values.reshape(4, -1)
    mean_sq = lax.optimization_barrier(jnp.sum(grouped * grouped, axis=1)) / grouped.shape[1]
    scales = lax.rsqrt(mean_sq + 1e-06)
    return (grouped * scales[:, None]).reshape(values.shape)

def reference(positions, forces, tile_rows, tile_cols, tile_count):
    first_sweep = apply_mobility(positions, forces, tile_rows, tile_cols, tile_count)
    first_vectors = normalize(first_sweep)
    second_sweep = apply_mobility(positions, first_vectors, tile_rows, tile_cols, tile_count)
    second_vectors = normalize(second_sweep)
    return (first_vectors, second_vectors)
```

```python
import functools

import jax
import jax.numpy as jnp
from jax import lax
from jax.experimental import pallas as pl
from jax.experimental.pallas import tpu as pltpu
from jax.sharding import PartitionSpec as P

f32, bf16, i32 = jnp.float32, jnp.bfloat16, jnp.int32
BLOCK = 192
WIDE = 256
CHUNK = 16
SPAN = 32
HALF = SPAN // 2 * BLOCK
NEAR = 6 * SPAN
N_SUB = 4
N_SLAB = 32
LIST = 6 * 128
MESH = pl.DeviceIdType.MESH
VMEM = pl.BlockSpec(memory_space=pltpu.VMEM)
SMEM = pl.BlockSpec(memory_space=pltpu.SMEM)


def place():
    return lax.axis_index("slab"), lax.axis_index("sub")


def other(slab, sub):
    return (lax.rem(slab + N_SLAB, N_SLAB), lax.rem(sub, N_SUB))


def push(src, dst, send, recv, to):
    copy = pltpu.make_async_remote_copy(
        src_ref=src, dst_ref=dst, send_sem=send, recv_sem=recv, device_id=to, device_id_type=MESH
    )
    copy.start()
    return copy


def greet(peers):
    barrier = pltpu.get_barrier_semaphore()
    for peer in peers:
        pl.semaphore_signal(barrier, inc=1, device_id=peer, device_id_type=MESH)
    pl.semaphore_wait(barrier, len(peers))


def spread(slab, sub, src, near, send, recv):
    copies = []
    for d in range(1, N_SUB):
        copies.append(push(src, near.at[sub], send.at[d - 1], recv.at[sub], other(slab, sub + d)))
    copies.append(push(src, near.at[4], send.at[3], recv.at[4], other(slab + 1, sub)))
    copies.append(push(src, near.at[5], send.at[4], recv.at[5], other(slab - 1, sub)))
    return copies


def arrived(sub, src, near, send, recv, me):
    for d in range(1, N_SUB):
        at = lax.rem(sub + d, N_SUB)
        pltpu.make_async_remote_copy(
            src_ref=src, dst_ref=near.at[at], send_sem=send.at[d - 1], recv_sem=recv.at[at],
            device_id=me, device_id_type=MESH).wait_recv()
    for at in (4, 5):
        pltpu.make_async_remote_copy(
            src_ref=src, dst_ref=near.at[at], send_sem=send.at[at - 1], recv_sem=recv.at[at],
            device_id=me, device_id_type=MESH).wait_recv()


def gather_kernel(x, near, table, mine, send, recv, tsend, trecv, wsend, wrecv):
    slab, sub = place()
    greet([other(slab, sub + d) for d in range(1, N_SUB)]
          + [other(slab + d, sub) for d in (1, -1, 2, -2)])
    copies = spread(slab, sub, x, near, send, recv)
    col, live = x[30:31, 128:256], x[30:31, 256:384]
    upper = jnp.sum(jnp.where(col >= 256.0, live, 0.0), axis=1, keepdims=True)
    lower = jnp.sum(jnp.where(col < 128.0, live, 0.0), axis=1, keepdims=True)
    whole = jnp.sum(live, axis=1, keepdims=True)
    row = lax.broadcasted_iota(i32, (8, 128), 0)
    mine[...] = jnp.where(row == 0, upper, jnp.where(row == 1, lower, jnp.where(row == 2, whole, 0.0)))
    own = pl.ds(pl.multiple_of(sub * 8, 8), 8)
    copies += [push(mine, table.at[2, own], tsend.at[d - 1], trecv.at[sub], other(slab, sub + d))
               for d in range(1, N_SUB)]
    table[2, own, :] = mine[...]
    for d in range(1, N_SUB):
        at = lax.rem(sub + d, N_SUB)
        pltpu.make_async_remote_copy(
            src_ref=mine, dst_ref=table.at[2, pl.ds(pl.multiple_of(at * 8, 8), 8)], send_sem=tsend.at[d - 1],
            recv_sem=trecv.at[at], device_id=(slab, sub), device_id_type=MESH).wait_recv()
    steps = (1, -1, 2, -2)
    for n, d in enumerate(steps):
        copies.append(push(table.at[2], table.at[2 - d], wsend.at[n], wrecv.at[n], other(slab + d, sub)))
    near[sub, :, :] = x[...]
    for n, d in enumerate(steps):
        copies[-4 + n].wait_recv()
    arrived(sub, x, near, send, recv, (slab, sub))
    for copy in copies:
        copy.wait_send()


def gather(x):
    return pl.pallas_call(
        gather_kernel,
        out_shape=(jax.ShapeDtypeStruct((6, 32, HALF), f32), jax.ShapeDtypeStruct((5, 32, 128), f32)),
        in_specs=[VMEM],
        out_specs=(VMEM, VMEM),
        scratch_shapes=[pltpu.VMEM((8, 128), f32)] + [pltpu.SemaphoreType.DMA((n,)) for n in (5, 6, 3, 4, 4, 4)],
        compiler_params=pltpu.CompilerParams(collective_id=0, has_side_effects=True, vmem_limit_bytes=40 * 2**20),
        name="gather_all",
    )(x)


def given(flow, counts):
    total = counts[0] + counts[1] + counts[2] + counts[3]
    whole = jnp.minimum(jnp.floor(jnp.maximum(flow, 0.0)), total)
    part = whole / jnp.maximum(total, 1.0)
    return [jnp.minimum(jnp.floor(part * n), n) for n in counts]


def plan_kernel(table, lists, out):
    slab, sub = place()
    at = lambda rel, sub_at, kind: table[rel + 2, 8 * sub_at + kind:8 * sub_at + kind + 1, :]
    subs = range(N_SUB)
    total = {rel: sum(at(rel, v, 2) for v in subs) for rel in range(-2, 3)}
    first, last = slab == 0, slab == N_SLAB - 1

    def flow(a, b, c, d):
        return (a - d + 2.0 * (b - c)) * 0.2

    before = flow(jnp.where(slab == 1, total[-1], total[-2]), total[-1], total[0],
                  jnp.where(last, total[0], total[1]))
    after = flow(jnp.where(first, total[0], total[-1]), total[0], total[1],
                 jnp.where(slab == N_SLAB - 2, total[1], total[2]))
    before = jnp.where(first, 0.0, before)
    after = jnp.where(last, 0.0, after)
    ups = [at(0, v, 0) for v in subs]
    downs = [at(0, v, 1) for v in subs]
    up_given = given(after, ups)
    down_given = given(-before, downs)
    from_before = given(before, [at(-1, v, 0) for v in subs])
    from_after = given(-after, [at(1, v, 1) for v in subs])

    col = lists[:, 128:256]
    alive = lists[:, 256:384] > 0.5
    row_local = lists[:, :128]
    is_up = alive & (col >= 256.0)
    is_down = alive & (col < 128.0)
    is_own = alive & (col >= 128.0) & (col < 256.0)
    within = col - jnp.where(col >= 256.0, 256.0, jnp.where(col >= 128.0, 128.0, 0.0))
    col_sub = jnp.floor(within * (1.0 / SPAN))
    col_local = within - SPAN * col_sub
    masks = jnp.concatenate([m.astype(f32) for m in (is_up, is_down, is_own)], axis=0)
    lane_a = lax.broadcasted_iota(i32, (128, 128), 0)
    lane_b = lax.broadcasted_iota(i32, (128, 128), 1)
    ahead = (lane_a < lane_b).astype(bf16)
    rank = jnp.dot(masks.astype(bf16), ahead, preferred_element_type=f32)
    up_rank, down_rank, own_rank = rank[0:8], rank[8:16], rank[16:24]

    seat = lax.broadcasted_iota(i32, (8, 128), 0)

    def rows(values):
        full = jnp.zeros((8, 128), f32)
        for n, value in enumerate(values):
            full = jnp.where(seat == n, value, full)
        return full

    pick = lambda values: sum(jnp.where(sub == v, values[v], 0.0) for v in subs)
    up_limit = rows(up_given + [pick(from_before), jnp.zeros((1, 128), f32)])
    down_limit = rows(down_given + [jnp.zeros((1, 128), f32), pick(from_after)])
    up_sent = is_up & (up_rank < up_limit)
    down_sent = is_down & (down_rank < down_limit)
    in_slab = seat < 4
    crossing = in_slab & ((is_up & ~up_sent) | (is_down & ~down_sent))
    fixed = []
    for v in subs:
        kept = jnp.where(crossing & (col_sub == float(v)), 1.0, 0.0)
        fixed.append(jnp.sum(jnp.sum(kept, axis=0, keepdims=True), axis=1, keepdims=True)
                     + from_before[v] + from_after[v])
    own_counts = [at(0, v, 2) - ups[v] - downs[v] for v in subs]
    own_total = sum(own_counts)
    level = (sum(fixed) + own_total) * 0.25
    wish = [jnp.maximum(level - have, 0.0) for have in fixed]
    scale = own_total / jnp.maximum(sum(wish), 1.0)
    edges = [jnp.zeros((1, 128), f32)]
    run = jnp.zeros((1, 128), f32)
    for v in range(3):
        run = run + wish[v] * scale
        edges.append(jnp.minimum(jnp.floor(run + 0.5), own_total))
    edges.append(own_total)
    begin = pick(edges[:4])
    end = pick(edges[1:])
    start, offsets = jnp.zeros((1, 128), f32), []
    for v in subs:
        offsets.append(start)
        start = start + own_counts[v]
    place_own = own_rank + rows(offsets)
    mine = (crossing & (col_sub == sub.astype(f32))) | (
        in_slab & is_own & (place_own >= begin) & (place_own < end))
    mine = mine | ((seat == 4) & up_sent) | ((seat == 5) & down_sent)
    mine_value = mine.astype(f32)
    slot = jnp.dot(mine_value.astype(bf16), ahead, preferred_element_type=f32)
    counted = jnp.sum(mine_value, axis=1, keepdims=True)
    start, offsets = jnp.zeros((1, 1), f32), []
    for n in range(6):
        offsets.append(start)
        start = start + counted[n:n + 1]
    slot = slot + rows(offsets)
    slot = jnp.where(mine, slot, -1.0)
    row_near = row_local + SPAN * seat.astype(f32)
    inside = SPAN * col_sub + col_local
    col_near = jnp.where(in_slab, jnp.where(is_up, 160.0 + col_local, jnp.where(is_down, 128.0 + col_local, inside)),
                         inside)
    slot_t = jnp.transpose(slot, (1, 0))
    target = lax.broadcasted_iota(i32, (128, LIST), 1).astype(f32)
    result = jnp.zeros((16, LIST), f32)
    pad = jnp.zeros((14, 128), f32)
    for n in range(6):
        chosen = (slot_t[:, n:n + 1] == target).astype(bf16)
        values = jnp.concatenate([row_near[n:n + 1], col_near[n:n + 1], pad], axis=0).astype(bf16)
        result = result + jnp.dot(values, chosen, preferred_element_type=f32)
    seat_wide = lax.broadcasted_iota(i32, (8, LIST), 0)
    out[...] = jnp.where(seat_wide == 2, start, result[0:8]).astype(i32)


def plan(table, lists):
    return pl.pallas_call(
        plan_kernel,
        out_shape=jax.ShapeDtypeStruct((8, LIST), i32),
        in_specs=[VMEM, VMEM],
        out_specs=VMEM,
        compiler_params=pltpu.CompilerParams(vmem_limit_bytes=40 * 2**20),
        name="plan_tiles",
    )(table, lists)


def mobility(xi, yi, zi, xj, yj, zj):
    dx, dy, dz = xi - xj, yi - yj, zi - zj
    q = jnp.maximum(dx * dx + dy * dy + dz * dz, 1e-12 / 64.0)
    inverse = lax.rsqrt(q)
    root = (0.75 / 8.0) ** 0.5
    taper = jnp.maximum(root - root * q, 0.0)
    weight = taper * taper * inverse
    square = inverse * inverse
    radius = q * inverse
    near = radius * (32.0 / 3.0 - 24.0 * radius)
    far = 1.0 + square * (1.0 / 96.0)
    iso = weight * jnp.where(q < 4.0 / 64.0, near, far)
    capped = jnp.minimum(square, 16.0)
    dyad = weight * (capped * (1.0 - capped * (1.0 / 32.0)))
    return iso, dyad * dx, dyad * dy, dyad * dz


def block_pieces(ref, at, pair, rows):
    lanes = pl.ds(pl.multiple_of(pair * 2 * BLOCK, 128), 2 * BLOCK)
    return ref[at, rows, lanes]


def prepare(values, spots, pos, vec):
    pad = jnp.zeros((12, WIDE - BLOCK), f32)

    def pair_body(n, _):
        at, pair = n // 8, n % 8
        lanes = pl.ds(pl.multiple_of(pair * 2 * BLOCK, 128), 2 * BLOCK)
        both = values[at, 0:24, lanes]
        spot = spots[at, :, lanes]
        for half in range(2):
            for side in range(2):
                block = at * SPAN + half * 16 + pair * 2 + side
                v = jnp.concatenate([both[12 * half:12 * half + 12, BLOCK * side:BLOCK * side + BLOCK], pad], axis=1)
                p = jnp.concatenate([spot[3 * half:3 * half + 3, BLOCK * side:BLOCK * side + BLOCK], pad[:3]], axis=1)
                s = v[0:4] * p[0:1] + v[4:8] * p[1:2] + v[8:12] * p[2:3]
                full = jnp.concatenate([v, s], axis=0)
                high = full.astype(bf16)
                vec[block, 0:16, :] = high
                vec[block, 16:32, :] = (full - high.astype(f32)).astype(bf16)
                pos[block, 0:3, :] = p
        return 0

    lax.fori_loop(0, 48, pair_body, 0)


def sweep_kernel(plan_ref, values, spots, out, pos, vec, acc, high, low, turned):
    prepare(values, spots, pos, vec)
    acc[...] = jnp.zeros_like(acc)

    def finish(parts, spot, sign):
        parts = [part[:16] + part[16:] for part in parts]
        x, y, z = (spot[n:n + 1] for n in range(3))
        row = lax.broadcasted_iota(i32, (8, WIDE), 0)
        upper = jnp.where(row < 4, x, y) * sign
        under = jnp.where(row < 4, z, -1.0) * sign
        sums = []
        for a in range(1, 4):
            t = parts[a][:8] * upper + parts[a][8:] * under
            sums.append(t + pltpu.roll(t, 4, 0))
        return parts[0][:8] + jnp.where(row < 4, sums[0], sums[1]), parts[0][8:] + sums[2]

    def tile(t, _):
        p, c = plan_ref[0, t], plan_ref[1, t]
        turned[...] = jnp.transpose(pos[p], (1, 0))
        xj, yj, zj = (pos[c, n:n + 1, :] for n in range(3))
        for r in range(0, BLOCK, CHUNK):
            xi, yi, zi = (turned[r:r + CHUNK, n:n + 1] for n in range(3))
            for m, value in enumerate(mobility(xi, yi, zi, xj, yj, zj)):
                part = value.astype(bf16)
                high[m, r:r + CHUNK, :] = part
                low[m, r:r + CHUNK, :] = (value - part.astype(f32)).astype(bf16)
        col_vec, row_vec = vec[c], vec[p, :, :BLOCK]
        to_rows, to_cols = [], []
        across = (((1,), (1,)), ((), ()))
        for m in range(4):
            h, l = high[m], low[m]
            side = (lax.dot_general(col_vec, h, across, preferred_element_type=f32)
                    + lax.dot_general(col_vec, l, across, preferred_element_type=f32))
            to_rows.append(jnp.concatenate([side, jnp.zeros((32, WIDE - BLOCK), f32)], axis=1))
            to_cols.append(jnp.dot(row_vec, h, preferred_element_type=f32)
                           + jnp.dot(row_vec, l, preferred_element_type=f32))
        upper, under = finish(to_rows, pos[p], 1.0)
        acc[p, 0:8, :] += upper
        acc[p, 8:16, :] += under
        upper, under = finish(to_cols, pos[c], -1.0)
        acc[c, 0:8, :] += upper
        acc[c, 8:16, :] += under
        return 0

    lax.fori_loop(0, plan_ref[2, 0], tile, 0)

    def pair_body(n, _):
        at, pair = n // 8, n % 8
        lanes = pl.ds(pl.multiple_of(pair * 2 * BLOCK, 128), 2 * BLOCK)
        halves = []
        for half in range(2):
            block = at * SPAN + half * 16 + pair * 2
            halves.append(jnp.concatenate([acc[block, 0:12, :BLOCK], acc[block + 1, 0:12, :BLOCK]], axis=1))
        out[at, :, lanes] = jnp.concatenate(halves, axis=0)
        return 0

    lax.fori_loop(0, 48, pair_body, 0)


def sweep(plan_list, values, spots):
    return pl.pallas_call(
        sweep_kernel,
        out_shape=jax.ShapeDtypeStruct((6, 24, HALF), f32),
        in_specs=[SMEM, VMEM, VMEM],
        out_specs=VMEM,
        scratch_shapes=[
            pltpu.VMEM((NEAR, 8, WIDE), f32),
            pltpu.VMEM((NEAR, 32, WIDE), bf16),
            pltpu.VMEM((NEAR, 16, WIDE), f32),
            pltpu.VMEM((4, BLOCK, WIDE), bf16),
            pltpu.VMEM((4, BLOCK, WIDE), bf16),
            pltpu.VMEM((WIDE, 8), f32),
        ],
        compiler_params=pltpu.CompilerParams(vmem_limit_bytes=48 * 2**20),
        name="sweep_tiles",
    )(plan_list, values, spots)


def collect(slab, sub, parts, own, inbox, send, recv):
    copies = []
    for d in range(1, N_SUB):
        at = lax.rem(sub + d, N_SUB)
        copies.append(push(parts.at[at], inbox.at[sub], send.at[d - 1], recv.at[sub], other(slab, sub + d)))
    copies.append(push(parts.at[4], inbox.at[5], send.at[3], recv.at[5], other(slab - 1, sub)))
    copies.append(push(parts.at[5], inbox.at[4], send.at[4], recv.at[4], other(slab + 1, sub)))
    arrived(sub, own, inbox, send, recv, (slab, sub))
    total = own[...] + parts[sub]
    for d in range(1, N_SUB):
        total = total + inbox[lax.rem(sub + d, N_SUB)]
    return copies, total + inbox[4] + inbox[5]


def greet_near(slab, sub, more=()):
    greet([other(slab, sub + d) for d in range(1, N_SUB)] + [other(slab + d, sub) for d in (1, -1)] + list(more))


def turn_kernel(parts, own, near, inbox, total, send, recv, gsend, grecv):
    slab, sub = place()
    greet_near(slab, sub)
    copies, value = collect(slab, sub, parts, own, inbox, send, recv)
    total[...] = value
    copies += spread(slab, sub, total, near, gsend, grecv)
    near[sub, :, :] = total[...]
    arrived(sub, total, near, gsend, grecv, (slab, sub))
    for copy in copies:
        copy.wait_send()


def turn(parts, own):
    return pl.pallas_call(
        turn_kernel,
        out_shape=jax.ShapeDtypeStruct((6, 24, HALF), f32),
        in_specs=[VMEM, VMEM],
        out_specs=VMEM,
        scratch_shapes=[pltpu.VMEM((6, 24, HALF), f32), pltpu.VMEM((24, HALF), f32)]
        + [pltpu.SemaphoreType.DMA((n,)) for n in (5, 6, 5, 6)],
        compiler_params=pltpu.CompilerParams(collective_id=1, has_side_effects=True, vmem_limit_bytes=40 * 2**20),
        name="turn_around",
    )(parts, own)


def squares(value):
    sq = value * value
    folded = sq[0:8] + sq[8:16] + sq[16:24]
    lanes = folded[:, 0:128]
    for n in range(1, HALF // 128):
        lanes = lanes + folded[:, 128 * n:128 * n + 128]
    return lanes


def finish_kernel(parts, first, out_first, out_second, inbox, box, send, recv, ssend, srecv):
    slab, sub = place()
    core = lax.rem(slab, 2)
    z = lax.rem(slab // 2, 4)
    y = slab // 8
    groups = [[other(slab, sub + d) for d in range(1, 4)],
              [(slab + 1 - 2 * core, sub)],
              [(y * 8 + lax.rem(z + d, 4) * 2 + core, sub) for d in range(1, 4)],
              [(lax.rem(y + d, 4) * 8 + z * 2 + core, sub) for d in range(1, 4)]]
    greet_near(slab, sub, groups[2] + groups[3])
    copies, value = collect(slab, sub, parts, first, inbox, send, recv)
    out_second[...] = value
    box[0, 0, 0:8, :] = squares(first[...])
    box[0, 0, 8:16, :] = squares(value)
    for n, group in enumerate(groups):
        turns = []
        for m, peer in enumerate(group):
            turns.append(push(box.at[n, 0], box.at[n, m + 1], ssend.at[3 * n + m], srecv.at[3 * n + m], peer))
        for copy in turns:
            copy.wait_recv()
        copies += turns
        now = box[n, 0]
        for m in range(len(group)):
            now = now + box[n, m + 1]
        box[n + 1, 0, :, :] = now
    total = jnp.sum(box[4, 0], axis=1, keepdims=True)
    per = 1.0 / (3.0 * BLOCK * SPAN * N_SUB * N_SLAB)
    one, two = total[0:8], total[8:16]
    one = (one + pltpu.roll(jnp.broadcast_to(one, (8, 128)), 4, 0)) * per
    two = (two + pltpu.roll(jnp.broadcast_to(two, (8, 128)), 4, 0)) * per
    scale_one = lax.rsqrt(one + 1e-6)
    scale_two = scale_one * lax.rsqrt(scale_one * scale_one * two + 1e-6)
    for r in range(0, 24, 8):
        out_first[r:r + 8, :] = first[r:r + 8, :] * scale_one[:, 0:1]
        out_second[r:r + 8, :] = out_second[r:r + 8, :] * scale_two[:, 0:1]
    for copy in copies:
        copy.wait_send()


def finish_all(parts, first):
    return pl.pallas_call(
        finish_kernel,
        out_shape=(jax.ShapeDtypeStruct((24, HALF), f32),) * 2,
        in_specs=[VMEM, VMEM],
        out_specs=(VMEM, VMEM),
        scratch_shapes=[pltpu.VMEM((6, 24, HALF), f32), pltpu.VMEM((5, 4, 16, 128), f32)]
        + [pltpu.SemaphoreType.DMA((n,)) for n in (5, 6, 12, 12)],
        compiler_params=pltpu.CompilerParams(collective_id=2, has_side_effects=True, vmem_limit_bytes=40 * 2**20),
        name="finish_all",
    )(parts, first)


def body(positions, forces, tile_rows, tile_cols, tile_count):
    slab, sub = place()
    device = slab * N_SUB + sub
    centre = jnp.stack([4.0 * slab.astype(f32) + 2.0, jnp.float32(3.0), jnp.float32(3.0)])
    packed = forces.reshape(4, 3, 2, HALF).transpose(2, 1, 0, 3).reshape(24, HALF)
    spots = positions.reshape(3, 2, HALF).transpose(1, 0, 2).reshape(6, HALF)
    row_local = tile_rows - device * SPAN
    col_rel = tile_cols - (slab - 1) * (N_SUB * SPAN)
    live = jnp.arange(128, dtype=i32) < tile_count[0]
    lists = jnp.concatenate([row_local.astype(f32), col_rel.astype(f32), live.astype(f32),
                             jnp.zeros((HALF - 384,), f32)])[None]
    x = jnp.concatenate([packed, spots, lists, jnp.zeros((1, HALF), f32)], axis=0)
    near, table = gather(x)
    lists_near = jnp.concatenate([near[:, 30, :384], jnp.zeros((2, 384), f32)], axis=0)
    spots_near = (near[:, 24:32] - jnp.concatenate([centre, centre, jnp.zeros((2,), f32)])[None, :, None]) * 0.125
    plan_list = plan(table, lists_near)
    parts = sweep(plan_list, near, spots_near)
    near_second = turn(parts, packed)
    parts = sweep(plan_list, near_second, spots_near)
    first = lax.dynamic_index_in_dim(near_second, sub, 0, keepdims=False)
    outs = finish_all(parts, first)
    return tuple(o.reshape(2, 3, 4, HALF).transpose(2, 1, 0, 3).reshape(12, 2 * HALF) for o in outs)


def solution(mesh):
    placed = (
        P(None, ("slab", "sub")),
        P(None, ("slab", "sub")),
        P(("slab", "sub")),
        P(("slab", "sub")),
        P(("slab", "sub")),
    )
    return jax.shard_map(
        body,
        mesh=mesh,
        in_specs=placed,
        out_specs=(P(None, ("slab", "sub")), P(None, ("slab", "sub"))),
        check_vma=False,
    )
```

```python
import functools

import jax
import jax.numpy as jnp
from jax import lax
from jax.experimental import pallas as pl
from jax.experimental.pallas import tpu as pltpu
from jax.sharding import PartitionSpec as P

f32, bf16, i32 = jnp.float32, jnp.bfloat16, jnp.int32
BLOCK = 192
WIDE = 256
CHUNK = 16
SPAN = 32
HALF = SPAN // 2 * BLOCK
NEAR = 6 * SPAN
N_SUB = 4
N_SLAB = 32
LIST = 6 * 128 + 128
MESH = pl.DeviceIdType.MESH
VMEM = pl.BlockSpec(memory_space=pltpu.VMEM)
SMEM = pl.BlockSpec(memory_space=pltpu.SMEM)


def place():
    return lax.axis_index("slab"), lax.axis_index("sub")


def other(slab, sub):
    return (lax.rem(slab + N_SLAB, N_SLAB), lax.rem(sub, N_SUB))


def push(src, dst, send, recv, to):
    copy = pltpu.make_async_remote_copy(
        src_ref=src, dst_ref=dst, send_sem=send, recv_sem=recv, device_id=to, device_id_type=MESH
    )
    copy.start()
    return copy


def greet(peers):
    barrier = pltpu.get_barrier_semaphore()
    for peer in peers:
        pl.semaphore_signal(barrier, inc=1, device_id=peer, device_id_type=MESH)
    pl.semaphore_wait(barrier, len(peers))


def spread(slab, sub, src, near, send, recv):
    copies = []
    for d in range(1, N_SUB):
        copies.append(push(src, near.at[sub], send.at[d - 1], recv.at[sub], other(slab, sub + d)))
    copies.append(push(src, near.at[4], send.at[3], recv.at[4], other(slab + 1, sub)))
    copies.append(push(src, near.at[5], send.at[4], recv.at[5], other(slab - 1, sub)))
    return copies


def arrived(sub, src, near, send, recv, me):
    for d in range(1, N_SUB):
        at = lax.rem(sub + d, N_SUB)
        pltpu.make_async_remote_copy(
            src_ref=src, dst_ref=near.at[at], send_sem=send.at[d - 1], recv_sem=recv.at[at],
            device_id=me, device_id_type=MESH).wait_recv()
    for at in (4, 5):
        pltpu.make_async_remote_copy(
            src_ref=src, dst_ref=near.at[at], send_sem=send.at[at - 1], recv_sem=recv.at[at],
            device_id=me, device_id_type=MESH).wait_recv()


def gather_kernel(x, near, table, mine, send, recv, tsend, trecv, wsend, wrecv):
    slab, sub = place()
    greet([other(slab, sub + d) for d in range(1, N_SUB)]
          + [other(slab + d, sub) for d in (1, -1, 2, -2)])
    copies = spread(slab, sub, x, near, send, recv)
    col, live = x[30:31, 128:256], x[30:31, 256:384]
    upper = jnp.sum(jnp.where(col >= 256.0, live, 0.0), axis=1, keepdims=True)
    lower = jnp.sum(jnp.where(col < 128.0, live, 0.0), axis=1, keepdims=True)
    whole = jnp.sum(live, axis=1, keepdims=True)
    row = lax.broadcasted_iota(i32, (8, 128), 0)
    mine[...] = jnp.where(row == 0, upper, jnp.where(row == 1, lower, jnp.where(row == 2, whole, 0.0)))
    own = pl.ds(pl.multiple_of(sub * 8, 8), 8)
    copies += [push(mine, table.at[2, own], tsend.at[d - 1], trecv.at[sub], other(slab, sub + d))
               for d in range(1, N_SUB)]
    table[2, own, :] = mine[...]
    for d in range(1, N_SUB):
        at = lax.rem(sub + d, N_SUB)
        pltpu.make_async_remote_copy(
            src_ref=mine, dst_ref=table.at[2, pl.ds(pl.multiple_of(at * 8, 8), 8)], send_sem=tsend.at[d - 1],
            recv_sem=trecv.at[at], device_id=(slab, sub), device_id_type=MESH).wait_recv()
    steps = (1, -1, 2, -2)
    for n, d in enumerate(steps):
        copies.append(push(table.at[2], table.at[2 - d], wsend.at[n], wrecv.at[n], other(slab + d, sub)))
    near[sub, :, :] = x[...]
    for n, d in enumerate(steps):
        copies[-4 + n].wait_recv()
    arrived(sub, x, near, send, recv, (slab, sub))
    for copy in copies:
        copy.wait_send()


def gather(x):
    return pl.pallas_call(
        gather_kernel,
        out_shape=(jax.ShapeDtypeStruct((6, 32, HALF), f32), jax.ShapeDtypeStruct((5, 32, 128), f32)),
        in_specs=[VMEM],
        out_specs=(VMEM, VMEM),
        scratch_shapes=[pltpu.VMEM((8, 128), f32)] + [pltpu.SemaphoreType.DMA((n,)) for n in (5, 6, 3, 4, 4, 4)],
        compiler_params=pltpu.CompilerParams(collective_id=0, has_side_effects=True, vmem_limit_bytes=40 * 2**20),
        name="gather_all",
    )(x)


def given(flow, counts):
    total = counts[0] + counts[1] + counts[2] + counts[3]
    whole = jnp.minimum(jnp.floor(jnp.maximum(flow, 0.0)), total)
    part = whole / jnp.maximum(total, 1.0)
    return [jnp.minimum(jnp.floor(part * n), n) for n in counts]


def plan_kernel(table, lists, out):
    slab, sub = place()
    at = lambda rel, sub_at, kind: table[rel + 2, 8 * sub_at + kind:8 * sub_at + kind + 1, :]
    subs = range(N_SUB)
    total = {rel: sum(at(rel, v, 2) for v in subs) for rel in range(-2, 3)}
    first, last = slab == 0, slab == N_SLAB - 1

    def flow(a, b, c, d):
        return (a - d + 2.0 * (b - c)) * 0.2

    before = flow(jnp.where(slab == 1, total[-1], total[-2]), total[-1], total[0],
                  jnp.where(last, total[0], total[1]))
    after = flow(jnp.where(first, total[0], total[-1]), total[0], total[1],
                 jnp.where(slab == N_SLAB - 2, total[1], total[2]))
    before = jnp.where(first, 0.0, before)
    after = jnp.where(last, 0.0, after)
    ups = [at(0, v, 0) for v in subs]
    downs = [at(0, v, 1) for v in subs]
    up_given = given(after, ups)
    down_given = given(-before, downs)
    from_before = given(before, [at(-1, v, 0) for v in subs])
    from_after = given(-after, [at(1, v, 1) for v in subs])

    col = lists[:, 128:256]
    alive = lists[:, 256:384] > 0.5
    row_local = lists[:, :128]
    is_up = alive & (col >= 256.0)
    is_down = alive & (col < 128.0)
    is_own = alive & (col >= 128.0) & (col < 256.0)
    within = col - jnp.where(col >= 256.0, 256.0, jnp.where(col >= 128.0, 128.0, 0.0))
    col_sub = jnp.floor(within * (1.0 / SPAN))
    col_local = within - SPAN * col_sub
    masks = jnp.concatenate([m.astype(f32) for m in (is_up, is_down, is_own)], axis=0)
    lane_a = lax.broadcasted_iota(i32, (128, 128), 0)
    lane_b = lax.broadcasted_iota(i32, (128, 128), 1)
    ahead = (lane_a < lane_b).astype(bf16)
    rank = jnp.dot(masks.astype(bf16), ahead, preferred_element_type=f32)
    up_rank, down_rank, own_rank = rank[0:8], rank[8:16], rank[16:24]

    seat = lax.broadcasted_iota(i32, (8, 128), 0)

    def rows(values):
        full = jnp.zeros((8, 128), f32)
        for n, value in enumerate(values):
            full = jnp.where(seat == n, value, full)
        return full

    pick = lambda values: sum(jnp.where(sub == v, values[v], 0.0) for v in subs)
    up_limit = rows(up_given + [pick(from_before), jnp.zeros((1, 128), f32)])
    down_limit = rows(down_given + [jnp.zeros((1, 128), f32), pick(from_after)])
    up_sent = is_up & (up_rank < up_limit)
    down_sent = is_down & (down_rank < down_limit)
    in_slab = seat < 4
    crossing = in_slab & ((is_up & ~up_sent) | (is_down & ~down_sent))
    fixed = []
    for v in subs:
        kept = jnp.where(crossing & (col_sub == float(v)), 1.0, 0.0)
        fixed.append(jnp.sum(jnp.sum(kept, axis=0, keepdims=True), axis=1, keepdims=True)
                     + from_before[v] + from_after[v])
    own_counts = [at(0, v, 2) - ups[v] - downs[v] for v in subs]
    own_total = sum(own_counts)
    level = (sum(fixed) + own_total) * 0.25
    wish = [jnp.maximum(level - have, 0.0) for have in fixed]
    scale = own_total / jnp.maximum(sum(wish), 1.0)
    edges = [jnp.zeros((1, 128), f32)]
    run = jnp.zeros((1, 128), f32)
    for v in range(3):
        run = run + wish[v] * scale
        edges.append(jnp.minimum(jnp.floor(run + 0.5), own_total))
    edges.append(own_total)
    begin = pick(edges[:4])
    end = pick(edges[1:])
    start, offsets = jnp.zeros((1, 128), f32), []
    for v in subs:
        offsets.append(start)
        start = start + own_counts[v]
    place_own = own_rank + rows(offsets)
    mine = (crossing & (col_sub == sub.astype(f32))) | (
        in_slab & is_own & (place_own >= begin) & (place_own < end))
    mine = mine | ((seat == 4) & up_sent) | ((seat == 5) & down_sent)
    mine_value = mine.astype(f32)
    slot = jnp.dot(mine_value.astype(bf16), ahead, preferred_element_type=f32)
    counted = jnp.sum(mine_value, axis=1, keepdims=True)
    start, offsets = jnp.zeros((1, 1), f32), []
    for n in range(6):
        offsets.append(start)
        start = start + counted[n:n + 1]
    slot = slot + rows(offsets)
    slot = jnp.where(mine, slot, -1.0)
    row_near = row_local + SPAN * seat.astype(f32)
    inside = SPAN * col_sub + col_local
    col_near = jnp.where(in_slab, jnp.where(is_up, 160.0 + col_local, jnp.where(is_down, 128.0 + col_local, inside)),
                         inside)
    slot_t = jnp.transpose(slot, (1, 0))
    target = lax.broadcasted_iota(i32, (128, LIST), 1).astype(f32)
    result = jnp.zeros((16, LIST), f32)
    pad = jnp.zeros((14, 128), f32)
    for n in range(6):
        chosen = (slot_t[:, n:n + 1] == target).astype(bf16)
        values = jnp.concatenate([row_near[n:n + 1], col_near[n:n + 1], pad], axis=0).astype(bf16)
        result = result + jnp.dot(values, chosen, preferred_element_type=f32)
    seat_wide = lax.broadcasted_iota(i32, (8, LIST), 0)
    lane_wide = lax.broadcasted_iota(i32, (8, LIST), 1).astype(f32)
    spare = jnp.where(lane_wide < start, result[0:8], float(NEAR))
    out[...] = jnp.where(seat_wide == 2, start, spare).astype(i32)


def plan(table, lists):
    return pl.pallas_call(
        plan_kernel,
        out_shape=jax.ShapeDtypeStruct((8, LIST), i32),
        in_specs=[VMEM, VMEM],
        out_specs=VMEM,
        compiler_params=pltpu.CompilerParams(vmem_limit_bytes=40 * 2**20),
        name="plan_tiles",
    )(table, lists)


UNIT = 0.5 ** 0.5
ISO = 0.25 * UNIT / (64.0 * UNIT**2) ** 2
DYAD = 3.0 * ISO


def mobility(xi, yi, zi, xj, yj, zj):
    dx, dy, dz = xi - xj, yi - yj, zi - zj
    q = jnp.maximum(dx * dx + dy * dy + dz * dz, 1e-12 * UNIT**2)
    inverse = lax.rsqrt(q)
    taper = jnp.maximum(64.0 * UNIT**2 - q, 0.0)
    weight = taper * taper
    square = inverse * inverse
    near = 4.0 / UNIT - 9.0 / 8.0 / UNIT**2 * (q * inverse)
    far = inverse * (3.0 + square)
    iso = weight * jnp.where(q < 4.0 * UNIT**2, near, far)
    capped = jnp.minimum(square, 0.5)
    dyad = weight * (capped * (1.0 - capped))
    return iso, dyad, (dx, dy, dz), inverse, q


CLOSE = 1.0 / (2e-3 * UNIT)


def two_parts(value):
    high = value.astype(bf16)
    return high, (value - high.astype(f32)).astype(bf16)


def unpack(values, spots, raw, pos):
    row = lax.broadcasted_iota(i32, (8, 128), 0)
    lane = lax.broadcasted_iota(i32, (8, 128), 1)

    def pair_body(n, _):
        at, pair = n // 8, n % 8
        start = pl.multiple_of(pair * 2 * BLOCK, 128)
        for j in range(3):
            lanes = pl.ds(start + 128 * j, 128)
            x, y, z = (values[at, 8 * a:8 * a + 8, lanes] for a in range(3))
            spot = spots[at, :, lanes]
            for half in range(2):
                if half == 0:
                    first, second = jnp.where(row < 4, x, pltpu.roll(y, 4, 0)), z
                else:
                    first, second = jnp.where(row < 4, pltpu.roll(x, 4, 0), y), pltpu.roll(z, 4, 0)
                place_of = spot if half == 0 else pltpu.roll(spot, 7, 0)
                block = at * SPAN + half * 16 + pair * 2
                for ref, r, value in ((raw, 0, first), (raw, 8, second), (pos, 0, place_of)):
                    if j == 0:
                        ref[block, r:r + 8, 0:128] = value
                    elif j == 2:
                        ref[block + 1, r:r + 8, 0:128] = value
                    else:
                        swapped = pltpu.roll(value, 64, 1)
                        ref[block, r:r + 8, 128:256] = jnp.where(lane < 64, value, swapped)
                        ref[block + 1, r:r + 8, 128:256] = jnp.where(lane < 64, swapped, value)
        return 0

    lax.fori_loop(0, 48, pair_body, 0, unroll=4)


def repack(acc, out):
    row = lax.broadcasted_iota(i32, (8, 128), 0)
    lane = lax.broadcasted_iota(i32, (8, 128), 1)

    def pair_body(n, _):
        at, pair = n // 8, n % 8
        start = pl.multiple_of(pair * 2 * BLOCK, 128)
        for j in range(3):
            got = []
            for half in range(2):
                block = at * SPAN + half * 16 + pair * 2
                for r in (0, 8):
                    if j == 0:
                        got.append(acc[block, r:r + 8, 0:128])
                    elif j == 2:
                        got.append(acc[block + 1, r:r + 8, 0:128])
                    else:
                        even, odd = acc[block, r:r + 8, 128:256], acc[block + 1, r:r + 8, 128:256]
                        got.append(jnp.where(lane < 64, even, odd)
                                   + pltpu.roll(jnp.where(lane < 64, odd, even), 64, 1))
            a0, a1, b0, b1 = got
            lanes = pl.ds(start + 128 * j, 128)
            out[at, 0:8, lanes] = jnp.where(row < 4, a0, pltpu.roll(b0, 4, 0))
            out[at, 8:16, lanes] = jnp.where(row < 4, pltpu.roll(a0, 4, 0), b0)
            out[at, 16:24, lanes] = jnp.where(row < 4, a1, pltpu.roll(b1, 4, 0))
        return 0

    lax.fori_loop(0, 48, pair_body, 0, unroll=4)


def sweep_kernel(plan_ref, values, spots, out, raw, pos, acc, *scratch):
    matrices, extra, turned, nearest = (scratch[0:4], scratch[4:8]), scratch[8:10], scratch[10:12], scratch[12]
    nearest[...] = jnp.full((8, 128), 64.0, f32)
    raw[NEAR, :, :] = jnp.zeros((16, WIDE), f32)
    pos[NEAR, :, :] = jnp.zeros((8, WIDE), f32)
    for part in matrices[0] + matrices[1]:
        part[:, 128:] = jnp.zeros((BLOCK, WIDE - 128), bf16)
    unpack(values, spots, raw, pos)
    acc[...] = jnp.zeros_like(acc)
    row = lax.broadcasted_iota(i32, (8, WIDE), 0)
    across = (((1,), (1,)), ((), ()))

    def tile_of(t):
        return plan_ref[0, t], plan_ref[1, t]

    def build(t, slot):
        p, c = tile_of(t)
        turn_ref = turned[slot]
        turn_ref[...] = jnp.transpose(pos[p], (1, 0))
        xj, yj, zj = (pos[c, n:n + 1, :] for n in (0, 2, 4))
        least = jnp.full((8, 128), 64.0, f32)
        side = lax.broadcasted_iota(i32, (CHUNK, 128), 1) < BLOCK - 128
        main, rest = slice(0, 128), slice(128, WIDE)

        def put(m, value, r):
            if r < BLOCK:
                matrices[slot][m][r:r + CHUNK, main] = value
            else:
                r -= BLOCK
                matrices[slot][m][r:r + CHUNK, 128:BLOCK] = value[:, :BLOCK - 128]
                matrices[slot][m][r + BLOCK // 2:r + BLOCK // 2 + CHUNK, BLOCK:] = value[:, BLOCK - 128:]

        for u in range(0, BLOCK // 2, CHUNK):
            w = u + BLOCK // 2
            there = [[jnp.broadcast_to(turn_ref[v:v + CHUNK, n:n + 1], (CHUNK, 128)) for n in (0, 2, 4)]
                     for v in (u, w)]
            there.append([jnp.where(side, one, two) for one, two in zip(*there)])
            for r, at, lanes in zip((u, w, u + BLOCK), there, (main, main, rest)):
                iso, dyad, _, inverse, q = mobility(*at, xj[:, lanes], yj[:, lanes], zj[:, lanes])
                for m, value in enumerate((iso, dyad * jnp.minimum(inverse, CLOSE))):
                    high, low = two_parts(value)
                    put(2 * m, high, r)
                    put(2 * m + 1, low, r)
                least = jnp.minimum(least, jnp.minimum(q[:8], q[8:]))
                yield
        nearest[...] = jnp.minimum(nearest[...], jnp.where(p == c, 64.0, least))

    def patterns(block):
        x, y, z = (pos[block, n:n + 1, :] for n in (0, 2, 4))
        return x, y, z, jnp.where(row < 4, x, y)

    def columns(block):
        x, y, z, both = patterns(block)
        first, second = raw[block, 0:8, :], raw[block, 8:16, :]
        t = first * both
        s = t + pltpu.roll(t, 4, 0) + pltpu.roll(second * z, 4, 0)
        second = jnp.where(row < 4, second, s)
        full = jnp.concatenate([first, second] + [part * scale for scale in (x, y, z) for part in (first, second)], axis=0)
        high = full.astype(bf16)
        rest = full - high.astype(f32)
        middle, low = two_parts(rest)
        return high, middle, low

    def finish(iso, dyad, block):
        x, y, z, both = patterns(block)
        last = jnp.where(row < 4, z, -1.0)
        iso = iso[0:16] + iso[16:32] + iso[32:48]
        dyad = dyad[0:64] + dyad[64:128] + dyad[128:192]

        def folded(r):
            t = dyad[r:r + 8] * both + dyad[r + 8:r + 16] * last
            return t + pltpu.roll(t, 4, 0)

        along = folded(0)
        upper = both * along - jnp.where(row < 4, folded(16), folded(32))
        under = z * along - folded(48)
        return ISO * iso[0:8] + DYAD * upper, ISO * iso[8:16] + DYAD * under

    def apply(t, slot):
        p, c = tile_of(t)
        iso_high, iso_low, dyad_high, dyad_low = matrices[slot]
        dot = lambda a, b: jnp.dot(a, b, preferred_element_type=f32)
        dot_across = lambda a, b: lax.dot_general(a, b, across, preferred_element_type=f32)
        parts = columns(c)
        wide = jnp.concatenate(parts, axis=0)
        slim = jnp.concatenate([part[:16] for part in parts], axis=0)
        yield
        pad = jnp.zeros((192, WIDE - BLOCK), f32)
        dyad = dot_across(wide, dyad_high[...])
        yield
        dyad = dyad + dot_across(wide, dyad_low[...])
        yield
        iso = dot_across(slim, iso_high[...]) + dot_across(slim, iso_low[...])
        yield
        upper, under = finish(jnp.concatenate([iso, pad[:48]], axis=1), jnp.concatenate([dyad, pad], axis=1), p)
        acc[p, 0:8, :] += upper
        acc[p, 8:16, :] += under
        yield
        parts = columns(p)
        wide = jnp.concatenate(parts, axis=0)[:, :BLOCK]
        slim = jnp.concatenate([part[:16] for part in parts], axis=0)[:, :BLOCK]
        yield
        dyad = dot(wide, dyad_high[...])
        yield
        dyad = dyad + dot(wide, dyad_low[...])
        yield
        iso = dot(slim, iso_high[...]) + dot(slim, iso_low[...])
        yield
        upper, under = finish(iso, dyad, c)
        acc[c, 0:8, :] += upper
        acc[c, 8:16, :] += under
        yield

    def close_pairs(t):
        p, c = tile_of(t)
        slot = 0
        turned[slot][...] = jnp.transpose(pos[p], (1, 0))
        single = lax.broadcasted_iota(i32, (1, WIDE), 1) < BLOCK
        xj, yj, zj = (pos[c, n:n + 1, :] for n in (0, 2, 4))
        col_parts, row_parts = columns(c), columns(p)
        col_vec = jnp.concatenate([col_parts[0][:16], col_parts[1][:16]], axis=0)
        row_vec = jnp.concatenate([row_parts[0][:16], row_parts[1][:16]], axis=0)[:, :BLOCK]

        col_vec = jnp.where(single, col_vec, jnp.zeros_like(col_vec))

        def one(n, _):
            for r in range(0, BLOCK, CHUNK):
                xi, yi, zi = (turned[slot][r:r + CHUNK, m:m + 1] for m in (0, 2, 4))
                _, dyad, offset, inverse, _ = mobility(xi, yi, zi, xj, yj, zj)
                rest = dyad * jnp.maximum(inverse - CLOSE, 0.0)
                along = jnp.where(n == 0, offset[0], jnp.where(n == 1, offset[1], offset[2]))
                high, low = two_parts(rest * along)
                extra[0][r:r + CHUNK, :] = high
                extra[1][r:r + CHUNK, :] = low
            h, l = extra[0][...], extra[1][...]
            to_row = (lax.dot_general(col_vec, h, across, preferred_element_type=f32)
                      + lax.dot_general(col_vec, l, across, preferred_element_type=f32))
            to_row = jnp.concatenate([to_row, jnp.zeros((32, WIDE - BLOCK), f32)], axis=1)
            to_col = (jnp.dot(row_vec, h, preferred_element_type=f32)
                      + jnp.dot(row_vec, l, preferred_element_type=f32))
            for block, got, sign in ((p, to_row, 1.0), (c, to_col, -1.0)):
                x, y, z, both = patterns(block)
                last = jnp.where(row < 4, z, -1.0)
                got = got[:16] + got[16:]
                folded = got[:8] * both + got[8:] * last
                folded = sign * DYAD * (folded + pltpu.roll(folded, 4, 0)) * single
                acc[block, 0:8, :] += jnp.where(row // 4 == n, folded, 0.0)
                acc[block, 8:16, :] += jnp.where(row // 4 + 2 == n, folded, 0.0)
            return 0

        lax.fori_loop(0, 3, one, 0)

    def drain(*steps):
        steps = list(steps)
        while steps:
            for step in list(steps):
                if next(step, steps) is steps:
                    steps.remove(step)

    count = plan_ref[2, 0]
    drain(build(0, 0))

    def body(n, _):
        for slot in range(2):
            t = 2 * n + slot
            drain(apply(t, slot), build(t + 1, 1 - slot))
        return 0

    lax.fori_loop(0, (count + 1) // 2, body, 0)

    found = jnp.min(nearest[...]) < 1.01 / CLOSE**2

    def look(t, _):
        p, c = tile_of(t)

        @pl.when(found | (p == c))
        def _():
            close_pairs(t)
        return 0

    lax.fori_loop(0, count, look, 0)

    repack(acc, out)


def sweep(plan_list, values, spots):
    tile = pltpu.VMEM((BLOCK, WIDE), bf16)
    return pl.pallas_call(
        sweep_kernel,
        out_shape=jax.ShapeDtypeStruct((6, 24, HALF), f32),
        in_specs=[SMEM, VMEM, VMEM],
        out_specs=VMEM,
        scratch_shapes=[
            pltpu.VMEM((NEAR + 1, 16, WIDE), f32),
            pltpu.VMEM((NEAR + 1, 8, WIDE), f32),
            pltpu.VMEM((NEAR + 1, 16, WIDE), f32),
        ]
        + [tile] * 10
        + [pltpu.VMEM((WIDE, 8), f32)] * 2
        + [pltpu.VMEM((8, 128), f32)],
        compiler_params=pltpu.CompilerParams(vmem_limit_bytes=48 * 2**20),
        name="sweep_tiles",
    )(plan_list, values, spots)


def collect(slab, sub, parts, own, inbox, send, recv):
    copies = []
    for d in range(1, N_SUB):
        at = lax.rem(sub + d, N_SUB)
        copies.append(push(parts.at[at], inbox.at[sub], send.at[d - 1], recv.at[sub], other(slab, sub + d)))
    copies.append(push(parts.at[4], inbox.at[5], send.at[3], recv.at[5], other(slab - 1, sub)))
    copies.append(push(parts.at[5], inbox.at[4], send.at[4], recv.at[4], other(slab + 1, sub)))
    arrived(sub, own, inbox, send, recv, (slab, sub))
    total = own[...] + parts[sub]
    for d in range(1, N_SUB):
        total = total + inbox[lax.rem(sub + d, N_SUB)]
    return copies, total + inbox[4] + inbox[5]


def greet_near(slab, sub, more=()):
    greet([other(slab, sub + d) for d in range(1, N_SUB)] + [other(slab + d, sub) for d in (1, -1)] + list(more))


def turn_kernel(parts, own, near, inbox, total, send, recv, gsend, grecv):
    slab, sub = place()
    greet_near(slab, sub)
    copies, value = collect(slab, sub, parts, own, inbox, send, recv)
    total[...] = value
    copies += spread(slab, sub, total, near, gsend, grecv)
    near[sub, :, :] = total[...]
    arrived(sub, total, near, gsend, grecv, (slab, sub))
    for copy in copies:
        copy.wait_send()


def turn(parts, own):
    return pl.pallas_call(
        turn_kernel,
        out_shape=jax.ShapeDtypeStruct((6, 24, HALF), f32),
        in_specs=[VMEM, VMEM],
        out_specs=VMEM,
        scratch_shapes=[pltpu.VMEM((6, 24, HALF), f32), pltpu.VMEM((24, HALF), f32)]
        + [pltpu.SemaphoreType.DMA((n,)) for n in (5, 6, 5, 6)],
        compiler_params=pltpu.CompilerParams(collective_id=1, has_side_effects=True, vmem_limit_bytes=40 * 2**20),
        name="turn_around",
    )(parts, own)


def squares(value):
    sq = value * value
    folded = sq[0:8] + sq[8:16] + sq[16:24]
    lanes = folded[:, 0:128]
    for n in range(1, HALF // 128):
        lanes = lanes + folded[:, 128 * n:128 * n + 128]
    return lanes


def finish_kernel(parts, first, out_first, out_second, inbox, box, send, recv, ssend, srecv):
    slab, sub = place()
    core = lax.rem(slab, 2)
    z = lax.rem(slab // 2, 4)
    y = slab // 8
    groups = [[other(slab, sub + d) for d in range(1, 4)],
              [(slab + 1 - 2 * core, sub)],
              [(y * 8 + lax.rem(z + d, 4) * 2 + core, sub) for d in range(1, 4)],
              [(lax.rem(y + d, 4) * 8 + z * 2 + core, sub) for d in range(1, 4)]]
    greet_near(slab, sub, groups[2] + groups[3])
    copies, value = collect(slab, sub, parts, first, inbox, send, recv)
    out_second[...] = value
    box[0, 0, 0:8, :] = squares(first[...])
    box[0, 0, 8:16, :] = squares(value)
    for n, group in enumerate(groups):
        turns = []
        for m, peer in enumerate(group):
            turns.append(push(box.at[n, 0], box.at[n, m + 1], ssend.at[3 * n + m], srecv.at[3 * n + m], peer))
        for copy in turns:
            copy.wait_recv()
        copies += turns
        now = box[n, 0]
        for m in range(len(group)):
            now = now + box[n, m + 1]
        box[n + 1, 0, :, :] = now
    total = jnp.sum(box[4, 0], axis=1, keepdims=True)
    per = 1.0 / (3.0 * BLOCK * SPAN * N_SUB * N_SLAB)
    one, two = total[0:8], total[8:16]
    one = (one + pltpu.roll(jnp.broadcast_to(one, (8, 128)), 4, 0)) * per
    two = (two + pltpu.roll(jnp.broadcast_to(two, (8, 128)), 4, 0)) * per
    scale_one = lax.rsqrt(one + 1e-6)
    scale_two = scale_one * lax.rsqrt(scale_one * scale_one * two + 1e-6)
    for r in range(0, 24, 8):
        out_first[r:r + 8, :] = first[r:r + 8, :] * scale_one[:, 0:1]
        out_second[r:r + 8, :] = out_second[r:r + 8, :] * scale_two[:, 0:1]
    for copy in copies:
        copy.wait_send()


def finish_all(parts, first):
    return pl.pallas_call(
        finish_kernel,
        out_shape=(jax.ShapeDtypeStruct((24, HALF), f32),) * 2,
        in_specs=[VMEM, VMEM],
        out_specs=(VMEM, VMEM),
        scratch_shapes=[pltpu.VMEM((6, 24, HALF), f32), pltpu.VMEM((5, 4, 16, 128), f32)]
        + [pltpu.SemaphoreType.DMA((n,)) for n in (5, 6, 12, 12)],
        compiler_params=pltpu.CompilerParams(collective_id=2, has_side_effects=True, vmem_limit_bytes=40 * 2**20),
        name="finish_all",
    )(parts, first)


def body(positions, forces, tile_rows, tile_cols, tile_count):
    slab, sub = place()
    device = slab * N_SUB + sub
    centre = jnp.stack([4.0 * slab.astype(f32) + 2.0, jnp.float32(3.0), jnp.float32(3.0)])
    packed = forces.reshape(4, 3, 2, HALF).transpose(1, 2, 0, 3).reshape(24, HALF)
    spots = positions.reshape(6, HALF)
    row_local = tile_rows - device * SPAN
    col_rel = tile_cols - (slab - 1) * (N_SUB * SPAN)
    live = jnp.arange(128, dtype=i32) < tile_count[0]
    lists = jnp.concatenate([row_local.astype(f32), col_rel.astype(f32), live.astype(f32),
                             jnp.zeros((HALF - 384,), f32)])[None]
    x = jnp.concatenate([packed, spots, lists, jnp.zeros((1, HALF), f32)], axis=0)
    near, table = gather(x)
    lists_near = jnp.concatenate([near[:, 30, :384], jnp.zeros((2, 384), f32)], axis=0)
    spots_near = (near[:, 24:32] - jnp.concatenate([jnp.repeat(centre, 2), jnp.zeros((2,), f32)])[None, :, None]) * UNIT
    plan_list = plan(table, lists_near)
    parts = sweep(plan_list, near, spots_near)
    near_second = turn(parts, packed)
    parts = sweep(plan_list, near_second, spots_near)
    first = lax.dynamic_index_in_dim(near_second, sub, 0, keepdims=False)
    outs = finish_all(parts, first)
    return tuple(o.reshape(3, 2, 4, HALF).transpose(2, 0, 1, 3).reshape(12, 2 * HALF) for o in outs)


def solution(mesh):
    placed = (
        P(None, ("slab", "sub")),
        P(None, ("slab", "sub")),
        P(("slab", "sub")),
        P(("slab", "sub")),
        P(("slab", "sub")),
    )
    return jax.shard_map(
        body,
        mesh=mesh,
        in_specs=placed,
        out_specs=(P(None, ("slab", "sub")), P(None, ("slab", "sub"))),
        check_vma=False,
    )
```

```python
import functools

import jax
import jax.numpy as jnp
from jax import lax
from jax.experimental import pallas as pl
from jax.experimental.pallas import tpu as pltpu
from jax.sharding import PartitionSpec as P

f32, bf16, i32 = jnp.float32, jnp.bfloat16, jnp.int32
BLOCK = 192
WIDE = 256
CHUNK = 16
SPAN = 32
HALF = SPAN // 2 * BLOCK
NEAR = 6 * SPAN
N_SUB = 4
N_SLAB = 32
LIST = 6 * 128 + 128
MESH = pl.DeviceIdType.MESH
VMEM = pl.BlockSpec(memory_space=pltpu.VMEM)
SMEM = pl.BlockSpec(memory_space=pltpu.SMEM)


def place():
    return lax.axis_index("slab"), lax.axis_index("sub")


def other(slab, sub):
    return (lax.rem(slab + N_SLAB, N_SLAB), lax.rem(sub, N_SUB))


def push(src, dst, send, recv, to):
    copy = pltpu.make_async_remote_copy(
        src_ref=src, dst_ref=dst, send_sem=send, recv_sem=recv, device_id=to, device_id_type=MESH
    )
    copy.start()
    return copy


def greet(peers):
    barrier = pltpu.get_barrier_semaphore()
    for peer in peers:
        pl.semaphore_signal(barrier, inc=1, device_id=peer, device_id_type=MESH)
    pl.semaphore_wait(barrier, len(peers))


WIDTH = HALF // 2
EARLY, LATE = slice(0, WIDTH), slice(WIDTH, HALF)


def wait_for(ref, sem, me):
    pltpu.make_async_remote_copy(
        src_ref=ref, dst_ref=ref, send_sem=sem, recv_sem=sem, device_id=me, device_id_type=MESH
    ).wait_recv()


def spread(slab, sub, src, near, send, recv):
    right, left = other(slab, sub + 1), other(slab, sub + 3)
    one, two, three = (lax.rem(sub + d, N_SUB) for d in range(1, 4))
    copies = []

    def half(what, at, lanes, to, n):
        copies.append(push(what.at[:, lanes], near.at[at, :, lanes], send.at[n],
                           recv.at[2 * at + (lanes is LATE)], to))

    half(src, sub, EARLY, right, 0)
    half(src, sub, LATE, left, 1)
    copies.append(push(src, near.at[4], send.at[2], recv.at[8], other(slab + 1, sub)))
    copies.append(push(src, near.at[5], send.at[3], recv.at[10], other(slab - 1, sub)))
    half(src, sub, LATE, right, 4)
    half(src, sub, EARLY, left, 5)
    near[sub, :, :] = src[...]

    def wait_half(at, lanes):
        wait_for(near.at[at, :, lanes], recv.at[2 * at + (lanes is LATE)], (slab, sub))

    wait_half(three, EARLY)
    half(near.at[three], three, EARLY, right, 6)
    wait_half(one, LATE)
    half(near.at[one], one, LATE, left, 7)
    for at, lanes in ((three, LATE), (one, EARLY), (two, EARLY), (two, LATE)):
        wait_half(at, lanes)
    wait_for(near.at[4], recv.at[8], (slab, sub))
    wait_for(near.at[5], recv.at[10], (slab, sub))
    return copies


def gather_kernel(x, y, near, spots, table, mine, send, recv, ysend, yrecv, tsend, trecv, wsend, wrecv):
    slab, sub = place()
    greet([other(slab, sub + d) for d in range(1, N_SUB)]
          + [other(slab + d, sub) for d in (1, -1, 2, -2)])
    copies = []
    for d in range(1, N_SUB):
        copies.append(push(y, spots.at[sub], ysend.at[d - 1], yrecv.at[sub], other(slab, sub + d)))
    copies.append(push(y, spots.at[4], ysend.at[3], yrecv.at[4], other(slab + 1, sub)))
    copies.append(push(y, spots.at[5], ysend.at[4], yrecv.at[5], other(slab - 1, sub)))
    col, live = y[6:7, 128:256], y[6:7, 256:384]
    upper = jnp.sum(jnp.where(col >= 256.0, live, 0.0), axis=1, keepdims=True)
    lower = jnp.sum(jnp.where(col < 128.0, live, 0.0), axis=1, keepdims=True)
    whole = jnp.sum(live, axis=1, keepdims=True)
    row = lax.broadcasted_iota(i32, (8, 128), 0)
    mine[...] = jnp.where(row == 0, upper, jnp.where(row == 1, lower, jnp.where(row == 2, whole, 0.0)))
    own = pl.ds(pl.multiple_of(sub * 8, 8), 8)
    copies += [push(mine, table.at[2, own], tsend.at[d - 1], trecv.at[sub], other(slab, sub + d))
               for d in range(1, N_SUB)]
    table[2, own, :] = mine[...]
    for d in range(1, N_SUB):
        at = lax.rem(sub + d, N_SUB)
        wait_for(table.at[2, pl.ds(pl.multiple_of(at * 8, 8), 8)], trecv.at[at], (slab, sub))
    turns = [push(table.at[2], table.at[2 - d], wsend.at[n], wrecv.at[n], other(slab + d, sub))
             for n, d in enumerate((1, -1, 2, -2))]
    copies += spread(slab, sub, x, near, send, recv)
    spots[sub, :, :] = y[...]
    for copy in turns:
        copy.wait_recv()
    for d in range(1, N_SUB):
        at = lax.rem(sub + d, N_SUB)
        wait_for(spots.at[at], yrecv.at[at], (slab, sub))
    for at in (4, 5):
        wait_for(spots.at[at], yrecv.at[at], (slab, sub))
    for copy in copies + turns:
        copy.wait_send()


def gather(x, y):
    return pl.pallas_call(
        gather_kernel,
        out_shape=(jax.ShapeDtypeStruct((6, 24, HALF), f32), jax.ShapeDtypeStruct((6, 8, HALF), f32),
                   jax.ShapeDtypeStruct((5, 32, 128), f32)),
        in_specs=[VMEM, VMEM],
        out_specs=(VMEM, VMEM, VMEM),
        scratch_shapes=[pltpu.VMEM((8, 128), f32)]
        + [pltpu.SemaphoreType.DMA((n,)) for n in (8, 12, 5, 6, 3, 4, 4, 4)],
        compiler_params=pltpu.CompilerParams(collective_id=0, has_side_effects=True, vmem_limit_bytes=40 * 2**20),
        name="gather_all",
    )(x, y)


def given(flow, counts):
    total = counts[0] + counts[1] + counts[2] + counts[3]
    whole = jnp.minimum(jnp.floor(jnp.maximum(flow, 0.0)), total)
    part = whole / jnp.maximum(total, 1.0)
    return [jnp.minimum(jnp.floor(part * n), n) for n in counts]


def plan_kernel(table, spots, out):
    slab, sub = place()
    lists = jnp.concatenate([spots[n, 6:7, 0:384] for n in range(6)] + [jnp.zeros((2, 384), f32)], axis=0)
    at = lambda rel, sub_at, kind: table[rel + 2, 8 * sub_at + kind:8 * sub_at + kind + 1, :]
    subs = range(N_SUB)
    total = {rel: sum(at(rel, v, 2) for v in subs) for rel in range(-2, 3)}
    first, last = slab == 0, slab == N_SLAB - 1

    def flow(a, b, c, d):
        return (a - d + 2.0 * (b - c)) * 0.2

    before = flow(jnp.where(slab == 1, total[-1], total[-2]), total[-1], total[0],
                  jnp.where(last, total[0], total[1]))
    after = flow(jnp.where(first, total[0], total[-1]), total[0], total[1],
                 jnp.where(slab == N_SLAB - 2, total[1], total[2]))
    before = jnp.where(first, 0.0, before)
    after = jnp.where(last, 0.0, after)
    ups = [at(0, v, 0) for v in subs]
    downs = [at(0, v, 1) for v in subs]
    up_given = given(after, ups)
    down_given = given(-before, downs)
    from_before = given(before, [at(-1, v, 0) for v in subs])
    from_after = given(-after, [at(1, v, 1) for v in subs])

    col = lists[:, 128:256]
    alive = lists[:, 256:384] > 0.5
    row_local = lists[:, :128]
    is_up = alive & (col >= 256.0)
    is_down = alive & (col < 128.0)
    is_own = alive & (col >= 128.0) & (col < 256.0)
    within = col - jnp.where(col >= 256.0, 256.0, jnp.where(col >= 128.0, 128.0, 0.0))
    col_sub = jnp.floor(within * (1.0 / SPAN))
    col_local = within - SPAN * col_sub
    masks = jnp.concatenate([m.astype(f32) for m in (is_up, is_down, is_own)], axis=0)
    lane_a = lax.broadcasted_iota(i32, (128, 128), 0)
    lane_b = lax.broadcasted_iota(i32, (128, 128), 1)
    ahead = (lane_a < lane_b).astype(bf16)
    rank = jnp.dot(masks.astype(bf16), ahead, preferred_element_type=f32)
    up_rank, down_rank, own_rank = rank[0:8], rank[8:16], rank[16:24]

    seat = lax.broadcasted_iota(i32, (8, 128), 0)

    def rows(values):
        full = jnp.zeros((8, 128), f32)
        for n, value in enumerate(values):
            full = jnp.where(seat == n, value, full)
        return full

    pick = lambda values: sum(jnp.where(sub == v, values[v], 0.0) for v in subs)
    up_limit = rows(up_given + [pick(from_before), jnp.zeros((1, 128), f32)])
    down_limit = rows(down_given + [jnp.zeros((1, 128), f32), pick(from_after)])
    up_sent = is_up & (up_rank < up_limit)
    down_sent = is_down & (down_rank < down_limit)
    in_slab = seat < 4
    crossing = in_slab & ((is_up & ~up_sent) | (is_down & ~down_sent))
    fixed = []
    for v in subs:
        kept = jnp.where(crossing & (col_sub == float(v)), 1.0, 0.0)
        fixed.append(jnp.sum(jnp.sum(kept, axis=0, keepdims=True), axis=1, keepdims=True)
                     + from_before[v] + from_after[v])
    own_counts = [at(0, v, 2) - ups[v] - downs[v] for v in subs]
    own_total = sum(own_counts)
    level = (sum(fixed) + own_total) * 0.25
    wish = [jnp.maximum(level - have, 0.0) for have in fixed]
    scale = own_total / jnp.maximum(sum(wish), 1.0)
    edges = [jnp.zeros((1, 128), f32)]
    run = jnp.zeros((1, 128), f32)
    for v in range(3):
        run = run + wish[v] * scale
        edges.append(jnp.minimum(jnp.floor(run + 0.5), own_total))
    edges.append(own_total)
    begin = pick(edges[:4])
    end = pick(edges[1:])
    start, offsets = jnp.zeros((1, 128), f32), []
    for v in subs:
        offsets.append(start)
        start = start + own_counts[v]
    place_own = own_rank + rows(offsets)
    mine = (crossing & (col_sub == sub.astype(f32))) | (
        in_slab & is_own & (place_own >= begin) & (place_own < end))
    mine = mine | ((seat == 4) & up_sent) | ((seat == 5) & down_sent)
    mine_value = mine.astype(f32)
    slot = jnp.dot(mine_value.astype(bf16), ahead, preferred_element_type=f32)
    counted = jnp.sum(mine_value, axis=1, keepdims=True)
    start, offsets = jnp.zeros((1, 1), f32), []
    for n in range(6):
        offsets.append(start)
        start = start + counted[n:n + 1]
    slot = slot + rows(offsets)
    slot = jnp.where(mine, slot, -1.0)
    row_near = row_local + SPAN * seat.astype(f32)
    inside = SPAN * col_sub + col_local
    col_near = jnp.where(in_slab, jnp.where(is_up, 160.0 + col_local, jnp.where(is_down, 128.0 + col_local, inside)),
                         inside)
    slot_t = jnp.transpose(slot, (1, 0))
    target = lax.broadcasted_iota(i32, (128, LIST), 1).astype(f32)
    result = jnp.zeros((16, LIST), f32)
    pad = jnp.zeros((14, 128), f32)
    for n in range(6):
        chosen = (slot_t[:, n:n + 1] == target).astype(bf16)
        values = jnp.concatenate([row_near[n:n + 1], col_near[n:n + 1], pad], axis=0).astype(bf16)
        result = result + jnp.dot(values, chosen, preferred_element_type=f32)
    lane_wide = lax.broadcasted_iota(i32, (1, LIST), 1).astype(f32)
    packed = jnp.where(lane_wide < start, result[0:1] * 256.0 + result[1:2], NEAR * 257.0)
    last_row = jnp.where(lane_b[0:1] == 0, start, 4.0 * slab.astype(f32) + 2.0)
    out[...] = jnp.concatenate([packed[:, 128 * n:128 * n + 128] for n in range(7)] + [last_row], axis=0).astype(i32)


def plan(table, spots):
    return pl.pallas_call(
        plan_kernel,
        out_shape=jax.ShapeDtypeStruct((8, 128), i32),
        in_specs=[VMEM, VMEM],
        out_specs=VMEM,
        compiler_params=pltpu.CompilerParams(vmem_limit_bytes=40 * 2**20),
        name="plan_tiles",
    )(table, spots)


UNIT = 0.5 ** 0.5
ISO = 0.25 * UNIT / (64.0 * UNIT**2) ** 2
DYAD = 3.0 * ISO


def mobility(xi, yi, zi, xj, yj, zj):
    dx, dy, dz = xi - xj, yi - yj, zi - zj
    q = jnp.maximum(dx * dx + dy * dy + dz * dz, 1e-12 * UNIT**2)
    inverse = lax.rsqrt(q)
    taper = jnp.maximum(64.0 * UNIT**2 - q, 0.0)
    weight = taper * taper
    square = inverse * inverse
    near = 4.0 / UNIT - 9.0 / 8.0 / UNIT**2 * (q * inverse)
    far = inverse * (3.0 + square)
    iso = weight * jnp.where(q < 4.0 * UNIT**2, near, far)
    capped = jnp.minimum(square, 0.5)
    dyad = weight * (capped * (1.0 - capped))
    return iso, dyad, (dx, dy, dz), inverse, q


CLOSE = 1.0 / (2e-3 * UNIT)


def two_parts(value):
    high = value.astype(bf16)
    return high, (value - high.astype(f32)).astype(bf16)


def unpack(values, spots, raw, pos, centre):
    row = lax.broadcasted_iota(i32, (8, 128), 0)
    lane = lax.broadcasted_iota(i32, (8, 128), 1)
    middle = jnp.where(row < 2, centre, 3.0)

    def pair_body(n, _):
        at, pair = n // 8, n % 8
        start = pl.multiple_of(pair * 2 * BLOCK, 128)
        for j in range(3):
            lanes = pl.ds(start + 128 * j, 128)
            x, y, z = (values[at, 8 * a:8 * a + 8, lanes] for a in range(3))
            spot = (spots[at, :, lanes] - middle) * UNIT
            for half in range(2):
                if half == 0:
                    first, second = jnp.where(row < 4, x, pltpu.roll(y, 4, 0)), z
                else:
                    first, second = jnp.where(row < 4, pltpu.roll(x, 4, 0), y), pltpu.roll(z, 4, 0)
                place_of = spot if half == 0 else pltpu.roll(spot, 7, 0)
                block = at * SPAN + half * 16 + pair * 2
                for ref, r, value in ((raw, 0, first), (raw, 8, second), (pos, 0, place_of)):
                    if j == 0:
                        ref[block, r:r + 8, 0:128] = value
                    elif j == 2:
                        ref[block + 1, r:r + 8, 0:128] = value
                    else:
                        swapped = pltpu.roll(value, 64, 1)
                        ref[block, r:r + 8, 128:256] = jnp.where(lane < 64, value, swapped)
                        ref[block + 1, r:r + 8, 128:256] = jnp.where(lane < 64, swapped, value)
        return 0

    lax.fori_loop(0, 48, pair_body, 0, unroll=4)


def repack(acc, out):
    row = lax.broadcasted_iota(i32, (8, 128), 0)
    lane = lax.broadcasted_iota(i32, (8, 128), 1)

    def pair_body(n, _):
        at, pair = n // 8, n % 8
        start = pl.multiple_of(pair * 2 * BLOCK, 128)
        for j in range(3):
            got = []
            for half in range(2):
                block = at * SPAN + half * 16 + pair * 2
                for r in (0, 8):
                    if j == 0:
                        got.append(acc[block, r:r + 8, 0:128])
                    elif j == 2:
                        got.append(acc[block + 1, r:r + 8, 0:128])
                    else:
                        even, odd = acc[block, r:r + 8, 128:256], acc[block + 1, r:r + 8, 128:256]
                        got.append(jnp.where(lane < 64, even, odd)
                                   + pltpu.roll(jnp.where(lane < 64, odd, even), 64, 1))
            a0, a1, b0, b1 = got
            lanes = pl.ds(start + 128 * j, 128)
            out[at, 0:8, lanes] = jnp.where(row < 4, a0, pltpu.roll(b0, 4, 0))
            out[at, 8:16, lanes] = jnp.where(row < 4, pltpu.roll(a0, 4, 0), b0)
            out[at, 16:24, lanes] = jnp.where(row < 4, a1, pltpu.roll(b1, 4, 0))
        return 0

    lax.fori_loop(0, 48, pair_body, 0, unroll=4)


def sweep_kernel(plan_ref, values, spots, out, raw, pos, acc, *scratch):
    matrices, extra, turned, nearest = (scratch[0:4], scratch[4:8]), scratch[8:10], scratch[10:12], scratch[12]
    sides = (scratch[13:15], scratch[15:17])
    nearest[...] = jnp.full((8, 128), 64.0, f32)
    raw[NEAR, :, :] = jnp.zeros((16, WIDE), f32)
    pos[NEAR, :, :] = jnp.zeros((8, WIDE), f32)
    for part in matrices[0] + matrices[1]:
        part[:, 128:] = jnp.zeros((BLOCK, WIDE - 128), bf16)
    unpack(values, spots, raw, pos, plan_ref[7, 1].astype(f32))
    acc[...] = jnp.zeros_like(acc)
    row = lax.broadcasted_iota(i32, (8, WIDE), 0)
    across = (((1,), (1,)), ((), ()))

    def tile_of(t):
        packed = plan_ref[t // 128, t % 128]
        return packed // 256, packed % 256

    def build(t, slot):
        p, c = tile_of(t)
        turn_ref = turned[slot]
        xj, yj, zj = (pos[c, n:n + 1, :] for n in (0, 2, 4))
        least = jnp.full((8, 128), 64.0, f32)
        side = lax.broadcasted_iota(i32, (CHUNK, 128), 1) < BLOCK - 128
        main, rest = slice(0, 128), slice(128, WIDE)

        def put(m, value, r):
            if r < BLOCK:
                matrices[slot][m][r:r + CHUNK, main] = value
            else:
                r -= BLOCK
                matrices[slot][m][r:r + CHUNK, 128:BLOCK] = value[:, :BLOCK - 128]
                matrices[slot][m][r + BLOCK // 2:r + BLOCK // 2 + CHUNK, BLOCK:] = value[:, BLOCK - 128:]

        for u in range(0, BLOCK // 2, CHUNK):
            w = u + BLOCK // 2
            there = [[jnp.broadcast_to(turn_ref[v:v + CHUNK, n:n + 1], (CHUNK, 128)) for n in (0, 2, 4)]
                     for v in (u, w)]
            there.append([jnp.where(side, one, two) for one, two in zip(*there)])
            for r, at, lanes in zip((u, w, u + BLOCK), there, (main, main, rest)):
                iso, dyad, _, inverse, q = mobility(*at, xj[:, lanes], yj[:, lanes], zj[:, lanes])
                for m, value in enumerate((iso, dyad * jnp.minimum(inverse, CLOSE))):
                    high, low = two_parts(value)
                    put(2 * m, high, r)
                    put(2 * m + 1, low, r)
                least = jnp.minimum(least, jnp.minimum(q[:8], q[8:]))
                yield
        nearest[...] = jnp.minimum(nearest[...], jnp.where(p == c, 64.0, least))

    def patterns(block):
        x, y, z = (pos[block, n:n + 1, :] for n in (0, 2, 4))
        return x, y, z, jnp.where(row < 4, x, y)

    def columns(block):
        x, y, z, both = patterns(block)
        first, second = raw[block, 0:8, :], raw[block, 8:16, :]
        t = first * both
        s = t + pltpu.roll(t, 4, 0) + pltpu.roll(second * z, 4, 0)
        second = jnp.where(row < 4, second, s)
        full = jnp.concatenate([first, second] + [part * scale for scale in (x, y, z) for part in (first, second)], axis=0)
        high = full.astype(bf16)
        rest = full - high.astype(f32)
        middle, low = two_parts(rest)
        return high, middle, low

    def finish(iso, dyad, block):
        x, y, z, both = patterns(block)
        last = jnp.where(row < 4, z, -1.0)
        iso = iso[0:16] + iso[16:32] + iso[32:48]
        dyad = dyad[0:64] + dyad[64:128] + dyad[128:192]

        def folded(r):
            t = dyad[r:r + 8] * both + dyad[r + 8:r + 16] * last
            return t + pltpu.roll(t, 4, 0)

        along = folded(0)
        upper = both * along - jnp.where(row < 4, folded(16), folded(32))
        under = z * along - folded(48)
        return ISO * iso[0:8] + DYAD * upper, ISO * iso[8:16] + DYAD * under

    def ready(t, slot):
        for side, block in zip(sides[slot], reversed(tile_of(t))):
            for n, part in enumerate(columns(block)):
                side[64 * n:64 * n + 64, :] = part
                yield

    def turn_rows(t, slot):
        turned[slot][...] = jnp.transpose(pos[tile_of(t)[0]], (1, 0))
        yield

    def apply(t, slot):
        p, c = tile_of(t)
        iso_high, iso_low, dyad_high, dyad_low = matrices[slot]
        dot = lambda a, b: jnp.dot(a, b, preferred_element_type=f32)
        dot_across = lambda a, b: lax.dot_general(a, b, across, preferred_element_type=f32)
        wide = sides[slot][0][...]
        slim = jnp.concatenate([wide[n:n + 16] for n in (0, 64, 128)], axis=0)
        pad = jnp.zeros((192, WIDE - BLOCK), f32)
        dyad = dot_across(wide, dyad_high[...])
        yield
        dyad = dyad + dot_across(wide, dyad_low[...])
        yield
        iso = dot_across(slim, iso_high[...]) + dot_across(slim, iso_low[...])
        yield
        upper, under = finish(jnp.concatenate([iso, pad[:48]], axis=1), jnp.concatenate([dyad, pad], axis=1), p)
        acc[p, 0:8, :] += upper
        acc[p, 8:16, :] += under
        yield
        wide = sides[slot][1][:, :BLOCK]
        slim = jnp.concatenate([wide[n:n + 16] for n in (0, 64, 128)], axis=0)
        dyad = dot(wide, dyad_high[...])
        yield
        dyad = dyad + dot(wide, dyad_low[...])
        yield
        iso = dot(slim, iso_high[...]) + dot(slim, iso_low[...])
        yield
        upper, under = finish(iso, dyad, c)
        acc[c, 0:8, :] += upper
        acc[c, 8:16, :] += under
        yield

    def close_pairs(t):
        p, c = tile_of(t)
        slot = 0
        turned[slot][...] = jnp.transpose(pos[p], (1, 0))
        single = lax.broadcasted_iota(i32, (1, WIDE), 1) < BLOCK
        xj, yj, zj = (pos[c, n:n + 1, :] for n in (0, 2, 4))
        col_parts, row_parts = columns(c), columns(p)
        col_vec = jnp.concatenate([col_parts[0][:16], col_parts[1][:16]], axis=0)
        row_vec = jnp.concatenate([row_parts[0][:16], row_parts[1][:16]], axis=0)[:, :BLOCK]

        col_vec = jnp.where(single, col_vec, jnp.zeros_like(col_vec))

        def one(n, _):
            for r in range(0, BLOCK, CHUNK):
                xi, yi, zi = (turned[slot][r:r + CHUNK, m:m + 1] for m in (0, 2, 4))
                _, dyad, offset, inverse, _ = mobility(xi, yi, zi, xj, yj, zj)
                rest = dyad * jnp.maximum(inverse - CLOSE, 0.0)
                along = jnp.where(n == 0, offset[0], jnp.where(n == 1, offset[1], offset[2]))
                high, low = two_parts(rest * along)
                extra[0][r:r + CHUNK, :] = high
                extra[1][r:r + CHUNK, :] = low
            h, l = extra[0][...], extra[1][...]
            to_row = (lax.dot_general(col_vec, h, across, preferred_element_type=f32)
                      + lax.dot_general(col_vec, l, across, preferred_element_type=f32))
            to_row = jnp.concatenate([to_row, jnp.zeros((32, WIDE - BLOCK), f32)], axis=1)
            to_col = (jnp.dot(row_vec, h, preferred_element_type=f32)
                      + jnp.dot(row_vec, l, preferred_element_type=f32))
            for block, got, sign in ((p, to_row, 1.0), (c, to_col, -1.0)):
                x, y, z, both = patterns(block)
                last = jnp.where(row < 4, z, -1.0)
                got = got[:16] + got[16:]
                folded = got[:8] * both + got[8:] * last
                folded = sign * DYAD * (folded + pltpu.roll(folded, 4, 0)) * single
                acc[block, 0:8, :] += jnp.where(row // 4 == n, folded, 0.0)
                acc[block, 8:16, :] += jnp.where(row // 4 + 2 == n, folded, 0.0)
            return 0

        lax.fori_loop(0, 3, one, 0)

    def drain(*steps):
        steps = list(steps)
        while steps:
            for step in list(steps):
                if next(step, steps) is steps:
                    steps.remove(step)

    count = plan_ref[7, 0]
    drain(turn_rows(0, 0), turn_rows(1, 1))
    drain(build(0, 0), ready(0, 0))

    def body(n, selves):
        for slot in range(2):
            t = 2 * n + slot
            p, c = tile_of(t)
            selves = selves + (p == c).astype(i32)
            drain(apply(t, slot), build(t + 1, 1 - slot), turn_rows(t + 2, slot), ready(t + 1, 1 - slot))
        return selves

    selves = lax.fori_loop(0, (count + 1) // 2, body, 0)
    found = jnp.min(nearest[...]) < 1.01 / CLOSE**2

    def look(t, _):
        p, c = tile_of(t)

        @pl.when(found | (p == c))
        def _():
            close_pairs(t)
        return 0

    lax.fori_loop(0, jnp.where(found | (selves > 0), count, 0), look, 0)

    repack(acc, out)


def sweep(plan_list, values, spots):
    tile = pltpu.VMEM((BLOCK, WIDE), bf16)
    return pl.pallas_call(
        sweep_kernel,
        out_shape=jax.ShapeDtypeStruct((6, 24, HALF), f32),
        in_specs=[SMEM, VMEM, VMEM],
        out_specs=VMEM,
        scratch_shapes=[
            pltpu.VMEM((NEAR + 1, 16, WIDE), f32),
            pltpu.VMEM((NEAR + 1, 8, WIDE), f32),
            pltpu.VMEM((NEAR + 1, 16, WIDE), f32),
        ]
        + [tile] * 10
        + [pltpu.VMEM((WIDE, 8), f32)] * 2
        + [pltpu.VMEM((8, 128), f32)]
        + [tile] * 4,
        compiler_params=pltpu.CompilerParams(vmem_limit_bytes=48 * 2**20),
        name="sweep_tiles",
    )(plan_list, values, spots)


def collect(slab, sub, parts, own, inbox, stage, send, recv):
    right, left = other(slab, sub + 1), other(slab, sub + 3)
    one, two, three = (lax.rem(sub + d, N_SUB) for d in range(1, 4))
    copies = []

    def half(what, at, lanes, to, n):
        copies.append(push(what, inbox.at[at, :, lanes], send.at[n], recv.at[2 * at + (lanes is LATE)], to))

    def wait_half(at, lanes):
        wait_for(inbox.at[at, :, lanes], recv.at[2 * at + (lanes is LATE)], (slab, sub))

    half(parts.at[two, :, EARLY], 0, EARLY, right, 0)
    half(parts.at[two, :, LATE], 1, LATE, left, 1)
    copies.append(push(parts.at[4], inbox.at[5], send.at[2], recv.at[10], other(slab - 1, sub)))
    copies.append(push(parts.at[5], inbox.at[4], send.at[3], recv.at[8], other(slab + 1, sub)))
    half(parts.at[one, :, LATE], 2, LATE, right, 4)
    half(parts.at[three, :, EARLY], 3, EARLY, left, 5)
    wait_half(0, EARLY)
    stage[0, :, :] = parts[one, :, EARLY] + inbox[0, :, EARLY]
    half(stage.at[0], 2, EARLY, right, 6)
    wait_half(1, LATE)
    stage[1, :, :] = parts[three, :, LATE] + inbox[1, :, LATE]
    half(stage.at[1], 3, LATE, left, 7)
    wait_for(inbox.at[4], recv.at[8], (slab, sub))
    wait_for(inbox.at[5], recv.at[10], (slab, sub))
    total = own[...] + parts[sub] + inbox[4] + inbox[5]
    for at in (2, 3):
        for lanes in (EARLY, LATE):
            wait_half(at, lanes)
    return copies, total + inbox[2] + inbox[3]


def greet_near(slab, sub, more=()):
    greet([other(slab, sub + d) for d in range(1, N_SUB)] + [other(slab + d, sub) for d in (1, -1)] + list(more))


def turn_kernel(parts, own, near, inbox, stage, total, send, recv, gsend, grecv):
    slab, sub = place()
    greet_near(slab, sub)
    copies, value = collect(slab, sub, parts, own, inbox, stage, send, recv)
    total[...] = value
    copies += spread(slab, sub, total, near, gsend, grecv)
    for copy in copies:
        copy.wait_send()


def turn(parts, own):
    return pl.pallas_call(
        turn_kernel,
        out_shape=jax.ShapeDtypeStruct((6, 24, HALF), f32),
        in_specs=[VMEM, VMEM],
        out_specs=VMEM,
        scratch_shapes=[pltpu.VMEM((6, 24, HALF), f32), pltpu.VMEM((2, 24, WIDTH), f32), pltpu.VMEM((24, HALF), f32)]
        + [pltpu.SemaphoreType.DMA((n,)) for n in (8, 12, 8, 12)],
        compiler_params=pltpu.CompilerParams(collective_id=1, has_side_effects=True, vmem_limit_bytes=40 * 2**20),
        name="turn_around",
    )(parts, own)


def squares(value):
    sq = value * value
    folded = sq[0:8] + sq[8:16] + sq[16:24]
    lanes = folded[:, 0:128]
    for n in range(1, HALF // 128):
        lanes = lanes + folded[:, 128 * n:128 * n + 128]
    return lanes


def finish_kernel(parts, first, out_first, out_second, inbox, stage, box, send, recv, ssend, srecv):
    slab, sub = place()
    core = lax.rem(slab, 2)
    z = lax.rem(slab // 2, 4)
    y = slab // 8
    groups = [[other(slab, sub + d) for d in range(1, 4)],
              [(slab + 1 - 2 * core, sub)],
              [(y * 8 + lax.rem(z + d, 4) * 2 + core, sub) for d in range(1, 4)],
              [(lax.rem(y + d, 4) * 8 + z * 2 + core, sub) for d in range(1, 4)]]
    greet_near(slab, sub, groups[2] + groups[3])
    copies, value = collect(slab, sub, parts, first, inbox, stage, send, recv)
    out_second[...] = value
    box[0, 0, 0:8, :] = squares(first[...])
    box[0, 0, 8:16, :] = squares(value)
    for n, group in enumerate(groups):
        turns = []
        for m, peer in enumerate(group):
            turns.append(push(box.at[n, 0], box.at[n, m + 1], ssend.at[3 * n + m], srecv.at[3 * n + m], peer))
        for copy in turns:
            copy.wait_recv()
        copies += turns
        now = box[n, 0]
        for m in range(len(group)):
            now = now + box[n, m + 1]
        box[n + 1, 0, :, :] = now
    total = jnp.sum(box[4, 0], axis=1, keepdims=True)
    per = 1.0 / (3.0 * BLOCK * SPAN * N_SUB * N_SLAB)
    one, two = total[0:8], total[8:16]
    one = (one + pltpu.roll(jnp.broadcast_to(one, (8, 128)), 4, 0)) * per
    two = (two + pltpu.roll(jnp.broadcast_to(two, (8, 128)), 4, 0)) * per
    scale_one = lax.rsqrt(one + 1e-6)
    scale_two = scale_one * lax.rsqrt(scale_one * scale_one * two + 1e-6)
    for r in range(0, 24, 8):
        out_first[r:r + 8, :] = first[r:r + 8, :] * scale_one[:, 0:1]
        out_second[r:r + 8, :] = out_second[r:r + 8, :] * scale_two[:, 0:1]
    for copy in copies:
        copy.wait_send()


def finish_all(parts, first):
    return pl.pallas_call(
        finish_kernel,
        out_shape=(jax.ShapeDtypeStruct((24, HALF), f32),) * 2,
        in_specs=[VMEM, VMEM],
        out_specs=(VMEM, VMEM),
        scratch_shapes=[pltpu.VMEM((6, 24, HALF), f32), pltpu.VMEM((2, 24, WIDTH), f32), pltpu.VMEM((5, 4, 16, 128), f32)]
        + [pltpu.SemaphoreType.DMA((n,)) for n in (8, 12, 12, 12)],
        compiler_params=pltpu.CompilerParams(collective_id=2, has_side_effects=True, vmem_limit_bytes=40 * 2**20),
        name="finish_all",
    )(parts, first)


def body(positions, forces, tile_rows, tile_cols, tile_count):
    slab, sub = place()
    device = slab * N_SUB + sub
    packed = forces.reshape(4, 3, 2, HALF).transpose(1, 2, 0, 3).reshape(24, HALF)
    spots = positions.reshape(6, HALF)
    row_local = tile_rows - device * SPAN
    col_rel = tile_cols - (slab - 1) * (N_SUB * SPAN)
    live = jnp.arange(128, dtype=i32) < tile_count[0]
    lists = jnp.concatenate([row_local.astype(f32), col_rel.astype(f32), live.astype(f32),
                             jnp.zeros((HALF - 384,), f32)])[None]
    y = jnp.concatenate([spots, lists, jnp.zeros((1, HALF), f32)], axis=0)
    near, spots_near, table = gather(packed, y)
    plan_list = plan(table, spots_near)
    parts = sweep(plan_list, near, spots_near)
    near_second = turn(parts, packed)
    parts = sweep(plan_list, near_second, spots_near)
    first = lax.dynamic_index_in_dim(near_second, sub, 0, keepdims=False)
    outs = finish_all(parts, first)
    return tuple(o.reshape(3, 2, 4, HALF).transpose(2, 0, 1, 3).reshape(12, 2 * HALF) for o in outs)


def solution(mesh):
    placed = (
        P(None, ("slab", "sub")),
        P(None, ("slab", "sub")),
        P(("slab", "sub")),
        P(("slab", "sub")),
        P(("slab", "sub")),
    )
    return jax.shard_map(
        body,
        mesh=mesh,
        in_specs=placed,
        out_specs=(P(None, ("slab", "sub")), P(None, ("slab", "sub"))),
        check_vma=False,
    )
```

```python
import functools
import types

import jax
import jax.numpy as jnp
from jax import lax
from jax.experimental import pallas as pl
from jax.experimental.pallas import tpu as pltpu
from jax.sharding import PartitionSpec as P

f32, bf16, i32 = jnp.float32, jnp.bfloat16, jnp.int32
BLOCK = 192
WIDE = 256
CHUNK = 16
SPAN = 32
HALF = SPAN // 2 * BLOCK
NEAR = 6 * SPAN
N_SUB = 4
N_SLAB = 32
LIST = 6 * 128 + 128
MESH = pl.DeviceIdType.MESH
VMEM = pl.BlockSpec(memory_space=pltpu.VMEM)
SMEM = pl.BlockSpec(memory_space=pltpu.SMEM)


def place():
    return lax.axis_index("slab"), lax.axis_index("sub")


def other(slab, sub):
    return (lax.rem(slab + N_SLAB, N_SLAB), lax.rem(sub, N_SUB))


def push(src, dst, send, recv, to):
    copy = pltpu.make_async_remote_copy(
        src_ref=src, dst_ref=dst, send_sem=send, recv_sem=recv, device_id=to, device_id_type=MESH
    )
    copy.start()
    return copy


def greet(peers):
    barrier = pltpu.get_barrier_semaphore()
    for peer in peers:
        pl.semaphore_signal(barrier, inc=1, device_id=peer, device_id_type=MESH)
    pl.semaphore_wait(barrier, len(peers))


WIDTH = HALF // 2
EARLY, LATE = slice(0, WIDTH), slice(WIDTH, HALF)


def wait_for(ref, sem, me):
    pltpu.make_async_remote_copy(
        src_ref=ref, dst_ref=ref, send_sem=sem, recv_sem=sem, device_id=me, device_id_type=MESH
    ).wait_recv()


def spread(slab, sub, src, near, send, recv):
    right, left = other(slab, sub + 1), other(slab, sub + 3)
    one, two, three = (lax.rem(sub + d, N_SUB) for d in range(1, 4))
    copies = []

    def half(what, at, lanes, to, n):
        copies.append(push(what.at[:, lanes], near.at[at, :, lanes], send.at[n],
                           recv.at[2 * at + (lanes is LATE)], to))

    half(src, sub, EARLY, right, 0)
    half(src, sub, LATE, left, 1)
    copies.append(push(src, near.at[4], send.at[2], recv.at[8], other(slab + 1, sub)))
    copies.append(push(src, near.at[5], send.at[3], recv.at[10], other(slab - 1, sub)))
    half(src, sub, LATE, right, 4)
    half(src, sub, EARLY, left, 5)
    near[sub, :, :] = src[...]

    def wait_half(at, lanes):
        wait_for(near.at[at, :, lanes], recv.at[2 * at + (lanes is LATE)], (slab, sub))

    wait_half(three, EARLY)
    half(near.at[three], three, EARLY, right, 6)
    wait_half(one, LATE)
    half(near.at[one], one, LATE, left, 7)
    for at, lanes in ((three, LATE), (one, EARLY), (two, EARLY), (two, LATE)):
        wait_half(at, lanes)
    wait_for(near.at[4], recv.at[8], (slab, sub))
    wait_for(near.at[5], recv.at[10], (slab, sub))
    return copies


def gather_kernel(forces, positions, rows, cols, count, values, spots, own, table, near, x, mine, send, recv, tsend, trecv, wsend, wrecv):
    slab, sub = place()
    x[30:32, :] = jnp.zeros((2, HALF), f32)
    col = (cols[...] - (slab - 1) * (N_SUB * SPAN)).astype(f32)
    live = jnp.where(lax.broadcasted_iota(i32, (1, 128), 1) < count[0], 1.0, 0.0)
    x[30:31, 0:128] = (rows[...] - (slab * N_SUB + sub) * SPAN).astype(f32)
    x[30:31, 128:256] = col
    x[30:31, 256:384] = live
    upper = jnp.sum(jnp.where(col >= 256.0, live, 0.0), axis=1, keepdims=True)
    lower = jnp.sum(jnp.where(col < 128.0, live, 0.0), axis=1, keepdims=True)
    whole = jnp.sum(live, axis=1, keepdims=True)
    row = lax.broadcasted_iota(i32, (8, 128), 0)
    mine[...] = jnp.where(row == 0, upper, jnp.where(row == 1, lower, jnp.where(row == 2, whole, 0.0)))
    for a in range(3):
        for half in range(2):
            lanes = slice(half * HALF, half * HALF + HALF)
            for k in range(4):
                x[a * 8 + half * 4 + k:a * 8 + half * 4 + k + 1, :] = forces[3 * k + a:3 * k + a + 1, lanes]
            x[24 + 2 * a + half:25 + 2 * a + half, :] = positions[a:a + 1, lanes]
    greet([other(slab, sub + d) for d in range(1, N_SUB)]
          + [other(slab + d, sub) for d in (1, -1, 2, -2)])
    at_own = pl.ds(pl.multiple_of(sub * 8, 8), 8)
    copies = [push(mine, table.at[2, at_own], tsend.at[d - 1], trecv.at[sub], other(slab, sub + d))
              for d in range(1, N_SUB)]
    table[2, at_own, :] = mine[...]
    for d in range(1, N_SUB):
        at = lax.rem(sub + d, N_SUB)
        wait_for(table.at[2, pl.ds(pl.multiple_of(at * 8, 8), 8)], trecv.at[at], (slab, sub))
    turns = [push(table.at[2], table.at[2 - d], wsend.at[n], wrecv.at[n], other(slab + d, sub))
             for n, d in enumerate((1, -1, 2, -2))]
    own[...] = x[0:24, :]
    copies += spread(slab, sub, x, near, send, recv)
    for n in range(6):
        values[n, :, :] = near[n, 0:24, :]
        spots[n, :, :] = near[n, 24:32, :]
    for copy in turns:
        copy.wait_recv()
    for copy in copies + turns:
        copy.wait_send()


def gather(forces, positions, rows, cols, count):
    return pl.pallas_call(
        gather_kernel,
        out_shape=(jax.ShapeDtypeStruct((6, 24, HALF), f32), jax.ShapeDtypeStruct((6, 8, HALF), f32),
                   jax.ShapeDtypeStruct((24, HALF), f32), jax.ShapeDtypeStruct((5, 32, 128), f32)),
        in_specs=[VMEM] * 4 + [SMEM],
        out_specs=(VMEM,) * 4,
        scratch_shapes=[pltpu.VMEM((6, 32, HALF), f32), pltpu.VMEM((32, HALF), f32), pltpu.VMEM((8, 128), f32)]
        + [pltpu.SemaphoreType.DMA((n,)) for n in (8, 12, 3, 4, 4, 4)],
        compiler_params=pltpu.CompilerParams(collective_id=0, has_side_effects=True, vmem_limit_bytes=60 * 2**20),
        name="gather_all",
    )(forces, positions, rows, cols, count)


def given(flow, counts):
    total = counts[0] + counts[1] + counts[2] + counts[3]
    whole = jnp.minimum(jnp.floor(jnp.maximum(flow, 0.0)), total)
    part = whole / jnp.maximum(total, 1.0)
    return [jnp.minimum(jnp.floor(part * n), n) for n in counts]


def plan_kernel(table, spots, out):
    slab, sub = place()
    lists = jnp.concatenate([spots[n, 6:7, 0:384] for n in range(6)] + [jnp.zeros((2, 384), f32)], axis=0)
    at = lambda rel, sub_at, kind: table[rel + 2, 8 * sub_at + kind:8 * sub_at + kind + 1, :]
    subs = range(N_SUB)
    total = {rel: sum(at(rel, v, 2) for v in subs) for rel in range(-2, 3)}
    first, last = slab == 0, slab == N_SLAB - 1

    def flow(a, b, c, d):
        return (a - d + 2.0 * (b - c)) * 0.2

    before = flow(jnp.where(slab == 1, total[-1], total[-2]), total[-1], total[0],
                  jnp.where(last, total[0], total[1]))
    after = flow(jnp.where(first, total[0], total[-1]), total[0], total[1],
                 jnp.where(slab == N_SLAB - 2, total[1], total[2]))
    before = jnp.where(first, 0.0, before)
    after = jnp.where(last, 0.0, after)
    ups = [at(0, v, 0) for v in subs]
    downs = [at(0, v, 1) for v in subs]
    up_given = given(after, ups)
    down_given = given(-before, downs)
    from_before = given(before, [at(-1, v, 0) for v in subs])
    from_after = given(-after, [at(1, v, 1) for v in subs])

    col = lists[:, 128:256]
    alive = lists[:, 256:384] > 0.5
    row_local = lists[:, :128]
    is_up = alive & (col >= 256.0)
    is_down = alive & (col < 128.0)
    is_own = alive & (col >= 128.0) & (col < 256.0)
    within = col - jnp.where(col >= 256.0, 256.0, jnp.where(col >= 128.0, 128.0, 0.0))
    col_sub = jnp.floor(within * (1.0 / SPAN))
    col_local = within - SPAN * col_sub
    masks = jnp.concatenate([m.astype(f32) for m in (is_up, is_down, is_own)], axis=0)
    lane_a = lax.broadcasted_iota(i32, (128, 128), 0)
    lane_b = lax.broadcasted_iota(i32, (128, 128), 1)
    ahead = (lane_a < lane_b).astype(bf16)
    rank = jnp.dot(masks.astype(bf16), ahead, preferred_element_type=f32)
    up_rank, down_rank, own_rank = rank[0:8], rank[8:16], rank[16:24]

    seat = lax.broadcasted_iota(i32, (8, 128), 0)

    def rows(values):
        full = jnp.zeros((8, 128), f32)
        for n, value in enumerate(values):
            full = jnp.where(seat == n, value, full)
        return full

    pick = lambda values: sum(jnp.where(sub == v, values[v], 0.0) for v in subs)
    up_limit = rows(up_given + [pick(from_before), jnp.zeros((1, 128), f32)])
    down_limit = rows(down_given + [jnp.zeros((1, 128), f32), pick(from_after)])
    up_sent = is_up & (up_rank < up_limit)
    down_sent = is_down & (down_rank < down_limit)
    in_slab = seat < 4
    crossing = in_slab & ((is_up & ~up_sent) | (is_down & ~down_sent))
    fixed = []
    for v in subs:
        kept = jnp.where(crossing & (col_sub == float(v)), 1.0, 0.0)
        fixed.append(jnp.sum(jnp.sum(kept, axis=0, keepdims=True), axis=1, keepdims=True)
                     + from_before[v] + from_after[v])
    own_counts = [at(0, v, 2) - ups[v] - downs[v] for v in subs]
    own_total = sum(own_counts)
    level = (sum(fixed) + own_total) * 0.25
    wish = [jnp.maximum(level - have, 0.0) for have in fixed]
    scale = own_total / jnp.maximum(sum(wish), 1.0)
    edges = [jnp.zeros((1, 128), f32)]
    run = jnp.zeros((1, 128), f32)
    for v in range(3):
        run = run + wish[v] * scale
        edges.append(jnp.minimum(jnp.floor(run + 0.5), own_total))
    edges.append(own_total)
    begin = pick(edges[:4])
    end = pick(edges[1:])
    start, offsets = jnp.zeros((1, 128), f32), []
    for v in subs:
        offsets.append(start)
        start = start + own_counts[v]
    place_own = own_rank + rows(offsets)
    mine = (crossing & (col_sub == sub.astype(f32))) | (
        in_slab & is_own & (place_own >= begin) & (place_own < end))
    mine = mine | ((seat == 4) & up_sent) | ((seat == 5) & down_sent)
    mine_value = mine.astype(f32)
    slot = jnp.dot(mine_value.astype(bf16), ahead, preferred_element_type=f32)
    counted = jnp.sum(mine_value, axis=1, keepdims=True)
    start, offsets = jnp.zeros((1, 1), f32), []
    for n in range(6):
        offsets.append(start)
        start = start + counted[n:n + 1]
    slot = slot + rows(offsets)
    slot = jnp.where(mine, slot, -1.0)
    row_near = row_local + SPAN * seat.astype(f32)
    inside = SPAN * col_sub + col_local
    col_near = jnp.where(in_slab, jnp.where(is_up, 160.0 + col_local, jnp.where(is_down, 128.0 + col_local, inside)),
                         inside)
    slot_t = jnp.transpose(slot, (1, 0))
    target = lax.broadcasted_iota(i32, (128, LIST), 1).astype(f32)
    result = jnp.zeros((16, LIST), f32)
    pad = jnp.zeros((14, 128), f32)
    for n in range(6):
        chosen = (slot_t[:, n:n + 1] == target).astype(bf16)
        values = jnp.concatenate([row_near[n:n + 1], col_near[n:n + 1], pad], axis=0).astype(bf16)
        result = result + jnp.dot(values, chosen, preferred_element_type=f32)
    lane_wide = lax.broadcasted_iota(i32, (1, LIST), 1).astype(f32)
    packed = jnp.where(lane_wide < start, result[0:1] * 256.0 + result[1:2], NEAR * 257.0)
    last_row = jnp.where(lane_b[0:1] == 0, start, 4.0 * slab.astype(f32) + 2.0)
    out[...] = jnp.concatenate([packed[:, 128 * n:128 * n + 128] for n in range(7)] + [last_row], axis=0).astype(i32)


def plan(table, spots):
    return pl.pallas_call(
        plan_kernel,
        out_shape=jax.ShapeDtypeStruct((8, 128), i32),
        in_specs=[VMEM, VMEM],
        out_specs=VMEM,
        compiler_params=pltpu.CompilerParams(vmem_limit_bytes=60 * 2**20),
        name="plan_tiles",
    )(table, spots)


UNIT = 0.5 ** 0.5
ISO = 0.25 * UNIT / (64.0 * UNIT**2) ** 2
DYAD = 3.0 * ISO


def mobility(xi, yi, zi, xj, yj, zj):
    dx, dy, dz = xi - xj, yi - yj, zi - zj
    q = jnp.maximum(dx * dx + dy * dy + dz * dz, 1e-12 * UNIT**2)
    inverse = lax.rsqrt(q)
    taper = jnp.maximum(64.0 * UNIT**2 - q, 0.0)
    weight = taper * taper
    square = inverse * inverse
    near = 4.0 / UNIT - 9.0 / 8.0 / UNIT**2 * (q * inverse)
    far = inverse * (3.0 + square)
    iso = weight * jnp.where(q < 4.0 * UNIT**2, near, far)
    capped = jnp.minimum(square, 0.5)
    dyad = weight * (capped * (1.0 - capped))
    return iso, dyad, (dx, dy, dz), inverse, q


CLOSE = 1.0 / (2e-3 * UNIT)


def two_parts(value):
    high = value.astype(bf16)
    return high, (value - high.astype(f32)).astype(bf16)


def block_store(ref, block, r, j, value, lane):
    if j == 0:
        ref[block, r:r + 8, 0:128] = value
    elif j == 2:
        ref[block + 1, r:r + 8, 0:128] = value
    else:
        swapped = pltpu.roll(value, 64, 1)
        ref[block, r:r + 8, 128:256] = jnp.where(lane < 64, value, swapped)
        ref[block + 1, r:r + 8, 128:256] = jnp.where(lane < 64, swapped, value)


def unpack_spots(spots, pos, centre):
    row = lax.broadcasted_iota(i32, (8, 128), 0)
    lane = lax.broadcasted_iota(i32, (8, 128), 1)
    middle = jnp.where(row < 2, centre, 3.0)
    pos[NEAR, :, :] = jnp.zeros((8, WIDE), f32)

    def pair_body(n, _):
        at, pair = n // 8, n % 8
        start = pl.multiple_of(pair * 2 * BLOCK, 128)
        for j in range(3):
            spot = (spots[at, :, pl.ds(start + 128 * j, 128)] - middle) * UNIT
            for half in range(2):
                block = at * SPAN + half * 16 + pair * 2
                block_store(pos, block, 0, j, spot if half == 0 else pltpu.roll(spot, 7, 0), lane)
        return 0

    lax.fori_loop(0, 48, pair_body, 0, unroll=4)


def unpack_values(sources, raw):
    row = lax.broadcasted_iota(i32, (8, 128), 0)
    lane = lax.broadcasted_iota(i32, (8, 128), 1)
    raw[NEAR, :, :] = jnp.zeros((16, WIDE), f32)

    def pair_body(pair, _):
        start = pl.multiple_of(pair * 2 * BLOCK, 128)
        for view, at in sources:
            for j in range(3):
                x, y, z = (view[8 * a:8 * a + 8, pl.ds(start + 128 * j, 128)] for a in range(3))
                for half in range(2):
                    if half == 0:
                        first, second = jnp.where(row < 4, x, pltpu.roll(y, 4, 0)), z
                    else:
                        first, second = jnp.where(row < 4, pltpu.roll(x, 4, 0), y), pltpu.roll(z, 4, 0)
                    block = at * SPAN + half * 16 + pair * 2
                    block_store(raw, block, 0, j, first, lane)
                    block_store(raw, block, 8, j, second, lane)
        return 0

    lax.fori_loop(0, 8, pair_body, 0)


def repack(acc, out):
    row = lax.broadcasted_iota(i32, (8, 128), 0)
    lane = lax.broadcasted_iota(i32, (8, 128), 1)

    def pair_body(n, _):
        at, pair = n // 8, n % 8
        start = pl.multiple_of(pair * 2 * BLOCK, 128)
        for j in range(3):
            got = []
            for half in range(2):
                block = at * SPAN + half * 16 + pair * 2
                for r in (0, 8):
                    if j == 0:
                        got.append(acc[block, r:r + 8, 0:128])
                    elif j == 2:
                        got.append(acc[block + 1, r:r + 8, 0:128])
                    else:
                        even, odd = acc[block, r:r + 8, 128:256], acc[block + 1, r:r + 8, 128:256]
                        got.append(jnp.where(lane < 64, even, odd)
                                   + pltpu.roll(jnp.where(lane < 64, odd, even), 64, 1))
            a0, a1, b0, b1 = got
            lanes = pl.ds(start + 128 * j, 128)
            out[at, 0:8, lanes] = jnp.where(row < 4, a0, pltpu.roll(b0, 4, 0))
            out[at, 8:16, lanes] = jnp.where(row < 4, pltpu.roll(a0, 4, 0), b0)
            out[at, 16:24, lanes] = jnp.where(row < 4, a1, pltpu.roll(b1, 4, 0))
        return 0

    lax.fori_loop(0, 48, pair_body, 0, unroll=4)


def worker(plan_ref, pos, nearest, turned, raw=None, acc=None, sides=None, extra=None):
    row = lax.broadcasted_iota(i32, (8, WIDE), 0)
    across = (((1,), (1,)), ((), ()))

    def tile_of(t):
        packed = plan_ref[t // 128, t % 128]
        return packed // 256, packed % 256

    def build(t, turn_ref, matrices):
        p, c = tile_of(t)
        xj, yj, zj = (pos[c, n:n + 1, :] for n in (0, 2, 4))
        least = jnp.full((8, 128), 64.0, f32)
        side = lax.broadcasted_iota(i32, (CHUNK, 128), 1) < BLOCK - 128
        main, rest = slice(0, 128), slice(128, WIDE)

        for u in range(0, BLOCK // 2, CHUNK):
            w = u + BLOCK // 2
            there = [[jnp.broadcast_to(turn_ref[v:v + CHUNK, n:n + 1], (CHUNK, 128)) for n in (0, 2, 4)]
                     for v in (u, w)]
            there.append([jnp.where(side, one, two) for one, two in zip(*there)])
            for r, at, lanes in zip((u, w, u + BLOCK), there, (main, main, rest)):
                iso, dyad, _, inverse, q = mobility(*at, xj[:, lanes], yj[:, lanes], zj[:, lanes])
                for m, value in enumerate((iso, dyad * jnp.minimum(inverse, CLOSE))):
                    high, low = two_parts(value)
                    matrices[2 * m, r:r + CHUNK, :] = high
                    matrices[2 * m + 1, r:r + CHUNK, :] = low
                least = jnp.minimum(least, jnp.minimum(q[:8], q[8:]))
                yield
        nearest[...] = jnp.minimum(nearest[...], jnp.where(p == c, 64.0, least))

    def patterns(block):
        x, y, z = (pos[block, n:n + 1, :] for n in (0, 2, 4))
        return x, y, z, jnp.where(row < 4, x, y)

    def columns(block):
        x, y, z, both = patterns(block)
        first, second = raw[block, 0:8, :], raw[block, 8:16, :]
        t = first * both
        s = t + pltpu.roll(t, 4, 0) + pltpu.roll(second * z, 4, 0)
        second = jnp.where(row < 4, second, s)
        full = jnp.concatenate([first, second] + [part * scale for scale in (x, y, z) for part in (first, second)], axis=0)
        high = full.astype(bf16)
        rest = full - high.astype(f32)
        middle, low = two_parts(rest)
        return high, middle, low

    def finish(iso, dyad, block):
        x, y, z, both = patterns(block)
        last = jnp.where(row < 4, z, -1.0)

        def folded(r):
            t = dyad[r:r + 8] * both + dyad[r + 8:r + 16] * last
            return t + pltpu.roll(t, 4, 0)

        along = folded(0)
        upper = both * along - jnp.where(row < 4, folded(16), folded(32))
        under = z * along - folded(48)
        return ISO * iso[0:8] + DYAD * upper, ISO * iso[8:16] + DYAD * under

    def ready(t, slot):
        for side, block in zip(sides[slot], reversed(tile_of(t))):
            for n, part in enumerate(columns(block)):
                side[64 * n:64 * n + 64, :] = part
                yield

    def turn_rows(t, turn_ref):
        turn_ref[...] = jnp.transpose(pos[tile_of(t)[0]], (1, 0))
        yield

    def summed(by_high, by_low):
        return (by_high[0:64] + by_low[0:64]) + (by_high[64:128] + by_low[64:128]) + by_high[128:192]

    def apply(t, slot, matrices):
        p, c = tile_of(t)
        side = lax.broadcasted_iota(i32, (1, 128), 1) < BLOCK - 128
        none = jnp.zeros((BLOCK // 2, 128), bf16)

        def whole(m):
            rest = matrices[m, BLOCK:, :]
            rest = jnp.concatenate([jnp.where(side, rest, none), jnp.where(side, none, rest)], axis=0)
            return jnp.concatenate([matrices[m, 0:BLOCK, :], rest], axis=1)

        iso_high, iso_low, dyad_high, dyad_low = (whole(m) for m in range(4))
        dot = lambda a, b: jnp.dot(a, b, preferred_element_type=f32)
        dot_across = lambda a, b: lax.dot_general(a, b, across, preferred_element_type=f32)
        wide = sides[slot][0][...]
        slim = jnp.concatenate([wide[n:n + 16] for n in (0, 64)], axis=0)
        pad = jnp.zeros((64, WIDE - BLOCK), f32)
        dyad = dot_across(wide, dyad_high)
        yield
        dyad = summed(dyad, dot_across(wide[:128], dyad_low))
        yield
        iso = dot_across(slim, iso_high) + dot_across(slim, iso_low)
        yield
        upper, under = finish(jnp.concatenate([iso[:16] + iso[16:], pad[:16]], axis=1), jnp.concatenate([dyad, pad], axis=1), p)
        acc[p, 0:8, :] += upper
        acc[p, 8:16, :] += under
        yield
        wide = sides[slot][1][:, :BLOCK]
        slim = jnp.concatenate([wide[n:n + 16] for n in (0, 64)], axis=0)
        dyad = dot(wide, dyad_high)
        yield
        dyad = summed(dyad, dot(wide[:128], dyad_low))
        yield
        iso = dot(slim, iso_high) + dot(slim, iso_low)
        yield
        upper, under = finish(iso[:16] + iso[16:], dyad, c)
        acc[c, 0:8, :] += upper
        acc[c, 8:16, :] += under
        yield

    def close_pairs(t):
        p, c = tile_of(t)
        turned[0][...] = jnp.transpose(pos[p], (1, 0))
        single = lax.broadcasted_iota(i32, (1, WIDE), 1) < BLOCK
        xj, yj, zj = (pos[c, n:n + 1, :] for n in (0, 2, 4))
        col_parts, row_parts = columns(c), columns(p)
        col_vec = jnp.concatenate([col_parts[0][:16], col_parts[1][:16]], axis=0)
        row_vec = jnp.concatenate([row_parts[0][:16], row_parts[1][:16]], axis=0)[:, :BLOCK]

        col_vec = jnp.where(single, col_vec, jnp.zeros_like(col_vec))

        def one(n, _):
            for r in range(0, BLOCK, CHUNK):
                xi, yi, zi = (turned[0][r:r + CHUNK, m:m + 1] for m in (0, 2, 4))
                _, dyad, offset, inverse, _ = mobility(xi, yi, zi, xj, yj, zj)
                rest = dyad * jnp.maximum(inverse - CLOSE, 0.0)
                along = jnp.where(n == 0, offset[0], jnp.where(n == 1, offset[1], offset[2]))
                high, low = two_parts(rest * along)
                extra[0][r:r + CHUNK, :] = high
                extra[1][r:r + CHUNK, :] = low
            h, l = extra[0][...], extra[1][...]
            to_row = (lax.dot_general(col_vec, h, across, preferred_element_type=f32)
                      + lax.dot_general(col_vec, l, across, preferred_element_type=f32))
            to_row = jnp.concatenate([to_row, jnp.zeros((32, WIDE - BLOCK), f32)], axis=1)
            to_col = (jnp.dot(row_vec, h, preferred_element_type=f32)
                      + jnp.dot(row_vec, l, preferred_element_type=f32))
            for block, got, sign in ((p, to_row, 1.0), (c, to_col, -1.0)):
                x, y, z, both = patterns(block)
                last = jnp.where(row < 4, z, -1.0)
                got = got[:16] + got[16:]
                folded = got[:8] * both + got[8:] * last
                folded = sign * DYAD * (folded + pltpu.roll(folded, 4, 0)) * single
                acc[block, 0:8, :] += jnp.where(row // 4 == n, folded, 0.0)
                acc[block, 8:16, :] += jnp.where(row // 4 + 2 == n, folded, 0.0)
            return 0

        lax.fori_loop(0, 3, one, 0)

    def drain(*steps):
        steps = list(steps)
        while steps:
            for step in list(steps):
                if next(step, steps) is steps:
                    steps.remove(step)

    return types.SimpleNamespace(tile_of=tile_of, build=build, ready=ready, turn_rows=turn_rows, apply=apply,
                                 close_pairs=close_pairs, drain=drain)


KEPT = 128
DEEP = 8


def finish_sweep(work, plan_ref, nearest, selves, acc, out):
    count = plan_ref[7, 0]
    found = jnp.min(nearest[...]) < 1.01 / CLOSE**2

    def look(t, _):
        p, c = work.tile_of(t)

        @pl.when(found | (p == c))
        def _():
            work.close_pairs(t)
        return 0

    lax.fori_loop(0, jnp.where(found | (selves > 0) | (count > KEPT), count, 0), look, 0)
    repack(acc, out)


def begin_sweep(plan_ref, values, spots, raw, pos, acc):
    unpack_values([(values.at[n], n) for n in range(6)], raw)
    unpack_spots(spots, pos, plan_ref[7, 1].astype(f32))
    acc[...] = jnp.zeros_like(acc)


def first_kernel(plan_ref, values, spots, out, kept, nearest, raw, pos, acc, store, sem, *scratch):
    turned, sides, extra = scratch[0:2], (scratch[2:4], scratch[4:6]), scratch[6:8]
    work = worker(plan_ref, pos, nearest, turned, raw, acc, sides, extra)
    nearest[...] = jnp.full((8, 128), 64.0, f32)
    begin_sweep(plan_ref, values, spots, raw, pos, acc)
    count = plan_ref[7, 0]
    pairs = (count + 1) // 2

    def out_copy(t):
        slot = lax.rem(t, DEEP)
        return pltpu.make_async_copy(store.at[slot], kept.at[t], sem.at[slot])

    def wait_out(t):
        @pl.when((t >= 0) & (t < KEPT))
        def _():
            out_copy(t).wait()

    work.drain(work.turn_rows(0, turned[0]), work.turn_rows(1, turned[1]))
    work.drain(work.build(0, turned[0], store.at[0]), work.ready(0, 0))
    out_copy(0).start()

    def body(n, selves):
        t = 2 * n
        for k in range(2):
            wait_out(t + 1 + k - DEEP)
        for k in range(2):
            p, c = work.tile_of(t + k)
            selves = selves + (p == c).astype(i32)
            work.drain(work.apply(t + k, k, store.at[lax.rem(t + k, DEEP)]),
                       work.build(t + k + 1, turned[1 - k], store.at[lax.rem(t + k + 1, DEEP)]),
                       work.turn_rows(t + k + 2, turned[k]), work.ready(t + k + 1, 1 - k))
        for k in range(2):
            @pl.when(t + 1 + k < KEPT)
            def _():
                out_copy(t + 1 + k).start()
        return selves

    selves = lax.fori_loop(0, pairs, body, 0)
    finish_sweep(work, plan_ref, nearest, selves, acc, out)
    for k in range(DEEP):
        wait_out(2 * pairs + 1 - DEEP + k)


TILE = (4, BLOCK + BLOCK // 2, 128)


def first_sweep(plan_list, values, spots):
    side = pltpu.VMEM((BLOCK, WIDE), bf16)
    return pl.pallas_call(
        first_kernel,
        out_shape=(jax.ShapeDtypeStruct((6, 24, HALF), f32), jax.ShapeDtypeStruct((KEPT,) + TILE, bf16),
                   jax.ShapeDtypeStruct((8, 128), f32)),
        in_specs=[SMEM, VMEM, VMEM],
        out_specs=(VMEM, pl.BlockSpec(memory_space=pl.ANY), VMEM),
        scratch_shapes=[
            pltpu.VMEM((NEAR + 1, 16, WIDE), f32),
            pltpu.VMEM((NEAR + 1, 8, WIDE), f32),
            pltpu.VMEM((NEAR + 1, 16, WIDE), f32),
            pltpu.VMEM((DEEP,) + TILE, bf16),
            pltpu.SemaphoreType.DMA((DEEP,)),
        ]
        + [pltpu.VMEM((WIDE, 8), f32)] * 2
        + [side] * 6,
        compiler_params=pltpu.CompilerParams(vmem_limit_bytes=60 * 2**20),
        name="first_sweep",
    )(plan_list, values, spots)


def second_kernel(plan_ref, values, spots, kept, least, out, raw, pos, acc, store, sem, *scratch):
    turned, sides, extra, nearest = scratch[0:2], (scratch[2:4], scratch[4:6]), scratch[6:8], scratch[8]
    work = worker(plan_ref, pos, nearest, turned, raw, acc, sides, extra)
    count = plan_ref[7, 0]
    pairs = (jnp.minimum(count, KEPT) + 1) // 2

    def in_copy(t):
        slot = lax.rem(t, DEEP)
        return pltpu.make_async_copy(kept.at[t], store.at[slot], sem.at[slot])

    for t in range(DEEP):
        @pl.when(t < 2 * pairs)
        def _():
            in_copy(t).start()

    nearest[...] = least[...]
    begin_sweep(plan_ref, values, spots, raw, pos, acc)
    work.drain(work.ready(0, 0))

    def body(n, selves):
        t = 2 * n
        for k in range(2):
            in_copy(t + k).wait()
        for k in range(2):
            p, c = work.tile_of(t + k)
            selves = selves + (p == c).astype(i32)
            work.drain(work.apply(t + k, k, store.at[lax.rem(t + k, DEEP)]), work.ready(t + k + 1, 1 - k))

        @pl.when(n + DEEP // 2 < pairs)
        def _():
            for k in range(2):
                in_copy(t + k + DEEP).start()
        return selves

    selves = lax.fori_loop(0, pairs, body, 0)

    @pl.when(count > KEPT)
    def _():
        def more(t, _):
            work.drain(work.turn_rows(t, turned[0]), work.ready(t, 0))
            work.drain(work.build(t, turned[0], store.at[0]))
            work.drain(work.apply(t, 0, store.at[0]))
            return 0

        lax.fori_loop(KEPT, count, more, 0)

    finish_sweep(work, plan_ref, nearest, selves, acc, out)


def second_sweep(plan_list, values, spots, kept, least):
    side = pltpu.VMEM((BLOCK, WIDE), bf16)
    return pl.pallas_call(
        second_kernel,
        out_shape=jax.ShapeDtypeStruct((6, 24, HALF), f32),
        in_specs=[SMEM, VMEM, VMEM, pl.BlockSpec(memory_space=pl.ANY), VMEM],
        out_specs=VMEM,
        scratch_shapes=[
            pltpu.VMEM((NEAR + 1, 16, WIDE), f32),
            pltpu.VMEM((NEAR + 1, 8, WIDE), f32),
            pltpu.VMEM((NEAR + 1, 16, WIDE), f32),
            pltpu.VMEM((DEEP,) + TILE, bf16),
            pltpu.SemaphoreType.DMA((DEEP,)),
        ]
        + [pltpu.VMEM((WIDE, 8), f32)] * 2
        + [side] * 6
        + [pltpu.VMEM((8, 128), f32)],
        compiler_params=pltpu.CompilerParams(vmem_limit_bytes=60 * 2**20),
        name="second_sweep",
    )(plan_list, values, spots, kept, least)


def collect(slab, sub, parts, own, inbox, stage, send, recv):
    right, left = other(slab, sub + 1), other(slab, sub + 3)
    one, two, three = (lax.rem(sub + d, N_SUB) for d in range(1, 4))
    copies = []

    def half(what, at, lanes, to, n):
        copies.append(push(what, inbox.at[at, :, lanes], send.at[n], recv.at[2 * at + (lanes is LATE)], to))

    def wait_half(at, lanes):
        wait_for(inbox.at[at, :, lanes], recv.at[2 * at + (lanes is LATE)], (slab, sub))

    half(parts.at[two, :, EARLY], 0, EARLY, right, 0)
    half(parts.at[two, :, LATE], 1, LATE, left, 1)
    copies.append(push(parts.at[4], inbox.at[5], send.at[2], recv.at[10], other(slab - 1, sub)))
    copies.append(push(parts.at[5], inbox.at[4], send.at[3], recv.at[8], other(slab + 1, sub)))
    half(parts.at[one, :, LATE], 2, LATE, right, 4)
    half(parts.at[three, :, EARLY], 3, EARLY, left, 5)
    wait_half(0, EARLY)
    stage[0, :, :] = parts[one, :, EARLY] + inbox[0, :, EARLY]
    half(stage.at[0], 2, EARLY, right, 6)
    wait_half(1, LATE)
    stage[1, :, :] = parts[three, :, LATE] + inbox[1, :, LATE]
    half(stage.at[1], 3, LATE, left, 7)
    wait_for(inbox.at[4], recv.at[8], (slab, sub))
    wait_for(inbox.at[5], recv.at[10], (slab, sub))
    total = own[...] + parts[sub] + inbox[4] + inbox[5]
    for at in (2, 3):
        for lanes in (EARLY, LATE):
            wait_half(at, lanes)
    return copies, total + inbox[2] + inbox[3]


def greet_near(slab, sub, more=()):
    greet([other(slab, sub + d) for d in range(1, N_SUB)] + [other(slab + d, sub) for d in (1, -1)] + list(more))


def turn_kernel(parts, own, near, inbox, stage, total, send, recv, gsend, grecv):
    slab, sub = place()
    greet_near(slab, sub)
    copies, value = collect(slab, sub, parts, own, inbox, stage, send, recv)
    total[...] = value
    copies += spread(slab, sub, total, near, gsend, grecv)
    for copy in copies:
        copy.wait_send()


def turn(parts, own):
    return pl.pallas_call(
        turn_kernel,
        out_shape=jax.ShapeDtypeStruct((6, 24, HALF), f32),
        in_specs=[VMEM, VMEM],
        out_specs=VMEM,
        scratch_shapes=[pltpu.VMEM((6, 24, HALF), f32), pltpu.VMEM((2, 24, WIDTH), f32), pltpu.VMEM((24, HALF), f32)]
        + [pltpu.SemaphoreType.DMA((n,)) for n in (8, 12, 8, 12)],
        compiler_params=pltpu.CompilerParams(collective_id=1, has_side_effects=True, vmem_limit_bytes=60 * 2**20),
        name="turn_around",
    )(parts, own)


def squares(value):
    sq = value * value
    folded = sq[0:8] + sq[8:16] + sq[16:24]
    lanes = folded[:, 0:128]
    for n in range(1, HALF // 128):
        lanes = lanes + folded[:, 128 * n:128 * n + 128]
    return lanes


def finish_kernel(parts, first, out_first, out_second, inbox, stage, box, send, recv, ssend, srecv):
    slab, sub = place()
    core = lax.rem(slab, 2)
    z = lax.rem(slab // 2, 4)
    y = slab // 8
    twin = slab + 1 - 2 * core
    groups = [[other(slab, sub + d) for d in range(1, 4)] + [other(twin, sub + d) for d in range(4)],
              [(y * 8 + lax.rem(z + d, 4) * 2 + core, sub) for d in range(1, 4)],
              [(lax.rem(y + d, 4) * 8 + z * 2 + core, sub) for d in range(1, 4)]]
    greet_near(slab, sub, groups[0][4:] + groups[1] + groups[2])
    copies, value = collect(slab, sub, parts, first, inbox, stage, send, recv)
    out_second[...] = value
    box[0, 0, 0:8, :] = squares(first[...])
    box[0, 0, 8:16, :] = squares(value)
    for n, group in enumerate(groups):
        turns = []
        for m, peer in enumerate(group):
            turns.append(push(box.at[n, 0], box.at[n, m + 1], ssend.at[7 * n + m], srecv.at[7 * n + m], peer))
        for copy in turns:
            copy.wait_recv()
        copies += turns
        now = box[n, 0]
        for m in range(len(group)):
            now = now + box[n, m + 1]
        box[n + 1, 0, :, :] = now
    total = jnp.sum(box[3, 0], axis=1, keepdims=True)
    per = 1.0 / (3.0 * BLOCK * SPAN * N_SUB * N_SLAB)
    one, two = total[0:8], total[8:16]
    one = (one + pltpu.roll(jnp.broadcast_to(one, (8, 128)), 4, 0)) * per
    two = (two + pltpu.roll(jnp.broadcast_to(two, (8, 128)), 4, 0)) * per
    scale_one = lax.rsqrt(one + 1e-6)
    scale_two = scale_one * lax.rsqrt(scale_one * scale_one * two + 1e-6)
    for r in range(0, 24, 8):
        out_first[r:r + 8, :] = first[r:r + 8, :] * scale_one[:, 0:1]
        out_second[r:r + 8, :] = out_second[r:r + 8, :] * scale_two[:, 0:1]
    for copy in copies:
        copy.wait_send()


def finish_all(parts, first):
    return pl.pallas_call(
        finish_kernel,
        out_shape=(jax.ShapeDtypeStruct((24, HALF), f32),) * 2,
        in_specs=[VMEM, VMEM],
        out_specs=(VMEM, VMEM),
        scratch_shapes=[pltpu.VMEM((6, 24, HALF), f32), pltpu.VMEM((2, 24, WIDTH), f32), pltpu.VMEM((4, 8, 16, 128), f32)]
        + [pltpu.SemaphoreType.DMA((n,)) for n in (8, 12, 21, 21)],
        compiler_params=pltpu.CompilerParams(collective_id=2, has_side_effects=True, vmem_limit_bytes=60 * 2**20),
        name="finish_all",
    )(parts, first)


def body(positions, forces, tile_rows, tile_cols, tile_count):
    _, sub = place()
    values, spots, own, table = gather(forces, positions, tile_rows[None], tile_cols[None], tile_count)
    plan_list = plan(table, spots)
    parts, kept, least = first_sweep(plan_list, values, spots)
    near_second = turn(parts, own)
    parts = second_sweep(plan_list, near_second, spots, kept, least)
    first = lax.dynamic_index_in_dim(near_second, sub, 0, keepdims=False)
    outs = finish_all(parts, first)
    return tuple(o.reshape(3, 2, 4, HALF).transpose(2, 0, 1, 3).reshape(12, 2 * HALF) for o in outs)


def solution(mesh):
    placed = (
        P(None, ("slab", "sub")),
        P(None, ("slab", "sub")),
        P(("slab", "sub")),
        P(("slab", "sub")),
        P(("slab", "sub")),
    )
    return jax.shard_map(
        body,
        mesh=mesh,
        in_specs=placed,
        out_specs=(P(None, ("slab", "sub")), P(None, ("slab", "sub"))),
        check_vma=False,
    )
```

```python
import functools
import types

import jax
import jax.numpy as jnp
from jax import lax
from jax.experimental import pallas as pl
from jax.experimental.pallas import tpu as pltpu
from jax.sharding import PartitionSpec as P

f32, bf16, i32 = jnp.float32, jnp.bfloat16, jnp.int32
BLOCK = 192
WIDE = 256
CHUNK = 16
SPAN = 32
HALF = SPAN // 2 * BLOCK
NEAR = 6 * SPAN
N_SUB = 4
N_SLAB = 32
LIST = 6 * 128 + 128
MESH = pl.DeviceIdType.MESH
VMEM = pl.BlockSpec(memory_space=pltpu.VMEM)
SMEM = pl.BlockSpec(memory_space=pltpu.SMEM)


def place():
    return lax.axis_index("slab"), lax.axis_index("sub")


def other(slab, sub):
    return (lax.rem(slab + N_SLAB, N_SLAB), lax.rem(sub, N_SUB))


def push(src, dst, send, recv, to):
    copy = pltpu.make_async_remote_copy(
        src_ref=src, dst_ref=dst, send_sem=send, recv_sem=recv, device_id=to, device_id_type=MESH
    )
    copy.start()
    return copy


def greet(peers):
    barrier = pltpu.get_barrier_semaphore()
    for peer in peers:
        pl.semaphore_signal(barrier, inc=1, device_id=peer, device_id_type=MESH)
    pl.semaphore_wait(barrier, len(peers))


WIDTH = HALF // 2
EARLY, LATE = slice(0, WIDTH), slice(WIDTH, HALF)


def wait_for(ref, sem, me):
    pltpu.make_async_remote_copy(
        src_ref=ref, dst_ref=ref, send_sem=sem, recv_sem=sem, device_id=me, device_id_type=MESH
    ).wait_recv()


def spread(slab, sub, src, near, send, recv):
    right, left = other(slab, sub + 1), other(slab, sub + 3)
    one, two, three = (lax.rem(sub + d, N_SUB) for d in range(1, 4))
    copies = []

    def half(what, at, lanes, to, n):
        copies.append(push(what.at[:, lanes], near.at[at, :, lanes], send.at[n],
                           recv.at[2 * at + (lanes is LATE)], to))

    half(src, sub, EARLY, right, 0)
    half(src, sub, LATE, left, 1)
    copies.append(push(src, near.at[4], send.at[2], recv.at[8], other(slab + 1, sub)))
    copies.append(push(src, near.at[5], send.at[3], recv.at[10], other(slab - 1, sub)))
    half(src, sub, LATE, right, 4)
    half(src, sub, EARLY, left, 5)
    near[sub, :, :] = src[...]

    def wait_half(at, lanes):
        wait_for(near.at[at, :, lanes], recv.at[2 * at + (lanes is LATE)], (slab, sub))

    wait_half(three, EARLY)
    half(near.at[three], three, EARLY, right, 6)
    wait_half(one, LATE)
    half(near.at[one], one, LATE, left, 7)
    for at, lanes in ((three, LATE), (one, EARLY), (two, EARLY), (two, LATE)):
        wait_half(at, lanes)
    wait_for(near.at[4], recv.at[8], (slab, sub))
    wait_for(near.at[5], recv.at[10], (slab, sub))
    return copies


def gather_kernel(forces_far, positions_far, rows_far, cols_far, count, values, spots, own, table,
                  forces, positions, rows, cols, in_sem, near, x, mine, send, recv, tsend, trecv, wsend, wrecv):
    slab, sub = place()
    fetches = [pltpu.make_async_copy(src, dst, in_sem.at[n]) for n, (src, dst) in enumerate(
        ((forces_far, forces), (positions_far, positions), (rows_far, rows), (cols_far, cols)))]
    for fetch in fetches:
        fetch.start()
    x[30:32, :] = jnp.zeros((2, HALF), f32)
    for fetch in fetches:
        fetch.wait()
    col = (cols[...] - (slab - 1) * (N_SUB * SPAN)).astype(f32)
    live = jnp.where(lax.broadcasted_iota(i32, (1, 128), 1) < count[0], 1.0, 0.0)
    x[30:31, 0:128] = (rows[...] - (slab * N_SUB + sub) * SPAN).astype(f32)
    x[30:31, 128:256] = col
    x[30:31, 256:384] = live
    upper = jnp.sum(jnp.where(col >= 256.0, live, 0.0), axis=1, keepdims=True)
    lower = jnp.sum(jnp.where(col < 128.0, live, 0.0), axis=1, keepdims=True)
    whole = jnp.sum(live, axis=1, keepdims=True)
    row = lax.broadcasted_iota(i32, (8, 128), 0)
    mine[...] = jnp.where(row == 0, upper, jnp.where(row == 1, lower, jnp.where(row == 2, whole, 0.0)))
    for a in range(3):
        for half in range(2):
            lanes = slice(half * HALF, half * HALF + HALF)
            for k in range(4):
                x[a * 8 + half * 4 + k:a * 8 + half * 4 + k + 1, :] = forces[3 * k + a:3 * k + a + 1, lanes]
            x[24 + 2 * a + half:25 + 2 * a + half, :] = positions[a:a + 1, lanes]
    greet([other(slab, sub + d) for d in range(1, N_SUB)]
          + [other(slab + d, sub) for d in (1, -1, 2, -2)])
    at_own = pl.ds(pl.multiple_of(sub * 8, 8), 8)
    copies = [push(mine, table.at[2, at_own], tsend.at[d - 1], trecv.at[sub], other(slab, sub + d))
              for d in range(1, N_SUB)]
    table[2, at_own, :] = mine[...]
    for d in range(1, N_SUB):
        at = lax.rem(sub + d, N_SUB)
        wait_for(table.at[2, pl.ds(pl.multiple_of(at * 8, 8), 8)], trecv.at[at], (slab, sub))
    turns = [push(table.at[2], table.at[2 - d], wsend.at[n], wrecv.at[n], other(slab + d, sub))
             for n, d in enumerate((1, -1, 2, -2))]
    own[...] = x[0:24, :]
    copies += spread(slab, sub, x, near, send, recv)
    for n in range(6):
        values[n, :, :] = near[n, 0:24, :]
        spots[n, :, :] = near[n, 24:32, :]
    for copy in turns:
        copy.wait_recv()
    for copy in copies + turns:
        copy.wait_send()


def gather(forces, positions, rows, cols, count):
    return pl.pallas_call(
        gather_kernel,
        out_shape=(jax.ShapeDtypeStruct((6, 24, HALF), f32), jax.ShapeDtypeStruct((6, 8, HALF), f32),
                   jax.ShapeDtypeStruct((24, HALF), f32), jax.ShapeDtypeStruct((5, 32, 128), f32)),
        in_specs=[pl.BlockSpec(memory_space=pltpu.HBM)] * 4 + [SMEM],
        out_specs=(VMEM,) * 4,
        scratch_shapes=[pltpu.VMEM((12, 2 * HALF), f32), pltpu.VMEM((3, 2 * HALF), f32), pltpu.VMEM((1, 128), i32),
                        pltpu.VMEM((1, 128), i32), pltpu.SemaphoreType.DMA((4,)), pltpu.VMEM((6, 32, HALF), f32), pltpu.VMEM((32, HALF), f32), pltpu.VMEM((8, 128), f32)]
        + [pltpu.SemaphoreType.DMA((n,)) for n in (8, 12, 3, 4, 4, 4)],
        compiler_params=pltpu.CompilerParams(collective_id=0, has_side_effects=True, vmem_limit_bytes=40 * 2**20),
        name="gather_all",
    )(forces, positions, rows, cols, count)


def given(flow, counts):
    total = counts[0] + counts[1] + counts[2] + counts[3]
    whole = jnp.minimum(jnp.floor(jnp.maximum(flow, 0.0)), total)
    part = whole / jnp.maximum(total, 1.0)
    return [jnp.minimum(jnp.floor(part * n), n) for n in counts]


def plan_kernel(table, spots, out):
    slab, sub = place()
    lists = jnp.concatenate([spots[n, 6:7, 0:384] for n in range(6)] + [jnp.zeros((2, 384), f32)], axis=0)
    at = lambda rel, sub_at, kind: table[rel + 2, 8 * sub_at + kind:8 * sub_at + kind + 1, :]
    subs = range(N_SUB)
    total = {rel: sum(at(rel, v, 2) for v in subs) for rel in range(-2, 3)}
    first, last = slab == 0, slab == N_SLAB - 1

    def flow(a, b, c, d):
        return (a - d + 2.0 * (b - c)) * 0.2

    before = flow(jnp.where(slab == 1, total[-1], total[-2]), total[-1], total[0],
                  jnp.where(last, total[0], total[1]))
    after = flow(jnp.where(first, total[0], total[-1]), total[0], total[1],
                 jnp.where(slab == N_SLAB - 2, total[1], total[2]))
    before = jnp.where(first, 0.0, before)
    after = jnp.where(last, 0.0, after)
    ups = [at(0, v, 0) for v in subs]
    downs = [at(0, v, 1) for v in subs]
    up_given = given(after, ups)
    down_given = given(-before, downs)
    from_before = given(before, [at(-1, v, 0) for v in subs])
    from_after = given(-after, [at(1, v, 1) for v in subs])

    col = lists[:, 128:256]
    alive = lists[:, 256:384] > 0.5
    row_local = lists[:, :128]
    is_up = alive & (col >= 256.0)
    is_down = alive & (col < 128.0)
    is_own = alive & (col >= 128.0) & (col < 256.0)
    within = col - jnp.where(col >= 256.0, 256.0, jnp.where(col >= 128.0, 128.0, 0.0))
    col_sub = jnp.floor(within * (1.0 / SPAN))
    col_local = within - SPAN * col_sub
    masks = jnp.concatenate([m.astype(f32) for m in (is_up, is_down, is_own)], axis=0)
    lane_a = lax.broadcasted_iota(i32, (128, 128), 0)
    lane_b = lax.broadcasted_iota(i32, (128, 128), 1)
    ahead = (lane_a < lane_b).astype(bf16)
    rank = jnp.dot(masks.astype(bf16), ahead, preferred_element_type=f32)
    up_rank, down_rank, own_rank = rank[0:8], rank[8:16], rank[16:24]

    seat = lax.broadcasted_iota(i32, (8, 128), 0)

    def rows(values):
        full = jnp.zeros((8, 128), f32)
        for n, value in enumerate(values):
            full = jnp.where(seat == n, value, full)
        return full

    pick = lambda values: sum(jnp.where(sub == v, values[v], 0.0) for v in subs)
    up_limit = rows(up_given + [pick(from_before), jnp.zeros((1, 128), f32)])
    down_limit = rows(down_given + [jnp.zeros((1, 128), f32), pick(from_after)])
    up_sent = is_up & (up_rank < up_limit)
    down_sent = is_down & (down_rank < down_limit)
    in_slab = seat < 4
    crossing = in_slab & ((is_up & ~up_sent) | (is_down & ~down_sent))
    fixed = []
    for v in subs:
        kept = jnp.where(crossing & (col_sub == float(v)), 1.0, 0.0)
        fixed.append(jnp.sum(jnp.sum(kept, axis=0, keepdims=True), axis=1, keepdims=True)
                     + from_before[v] + from_after[v])
    own_counts = [at(0, v, 2) - ups[v] - downs[v] for v in subs]
    own_total = sum(own_counts)
    level = (sum(fixed) + own_total) * 0.25
    wish = [jnp.maximum(level - have, 0.0) for have in fixed]
    scale = own_total / jnp.maximum(sum(wish), 1.0)
    edges = [jnp.zeros((1, 128), f32)]
    run = jnp.zeros((1, 128), f32)
    for v in range(3):
        run = run + wish[v] * scale
        edges.append(jnp.minimum(jnp.floor(run + 0.5), own_total))
    edges.append(own_total)
    begin = pick(edges[:4])
    end = pick(edges[1:])
    start, offsets = jnp.zeros((1, 128), f32), []
    for v in subs:
        offsets.append(start)
        start = start + own_counts[v]
    place_own = own_rank + rows(offsets)
    mine = (crossing & (col_sub == sub.astype(f32))) | (
        in_slab & is_own & (place_own >= begin) & (place_own < end))
    mine = mine | ((seat == 4) & up_sent) | ((seat == 5) & down_sent)
    mine_value = mine.astype(f32)
    slot = jnp.dot(mine_value.astype(bf16), ahead, preferred_element_type=f32)
    counted = jnp.sum(mine_value, axis=1, keepdims=True)
    start, offsets = jnp.zeros((1, 1), f32), []
    for n in range(6):
        offsets.append(start)
        start = start + counted[n:n + 1]
    slot = slot + rows(offsets)
    slot = jnp.where(mine, slot, -1.0)
    row_near = row_local + SPAN * seat.astype(f32)
    inside = SPAN * col_sub + col_local
    col_near = jnp.where(in_slab, jnp.where(is_up, 160.0 + col_local, jnp.where(is_down, 128.0 + col_local, inside)),
                         inside)
    slot_t = jnp.transpose(slot, (1, 0))
    target = lax.broadcasted_iota(i32, (128, LIST), 1).astype(f32)
    result = jnp.zeros((16, LIST), f32)
    pad = jnp.zeros((14, 128), f32)
    for n in range(6):
        chosen = (slot_t[:, n:n + 1] == target).astype(bf16)
        values = jnp.concatenate([row_near[n:n + 1], col_near[n:n + 1], pad], axis=0).astype(bf16)
        result = result + jnp.dot(values, chosen, preferred_element_type=f32)
    lane_wide = lax.broadcasted_iota(i32, (1, LIST), 1).astype(f32)
    packed = jnp.where(lane_wide < start, result[0:1] * 256.0 + result[1:2], NEAR * 257.0)
    last_row = jnp.where(lane_b[0:1] == 0, start, 4.0 * slab.astype(f32) + 2.0)
    out[...] = jnp.concatenate([packed[:, 128 * n:128 * n + 128] for n in range(7)] + [last_row], axis=0).astype(i32)


def plan(table, spots):
    return pl.pallas_call(
        plan_kernel,
        out_shape=jax.ShapeDtypeStruct((8, 128), i32),
        in_specs=[VMEM, VMEM],
        out_specs=VMEM,
        compiler_params=pltpu.CompilerParams(vmem_limit_bytes=40 * 2**20),
        name="plan_tiles",
    )(table, spots)


UNIT = 0.5 ** 0.5
ISO = 0.25 * UNIT / (64.0 * UNIT**2) ** 2
DYAD = 3.0 * ISO


def mobility(xi, yi, zi, xj, yj, zj):
    dx, dy, dz = xi - xj, yi - yj, zi - zj
    q = jnp.maximum(dx * dx + dy * dy + dz * dz, 1e-12 * UNIT**2)
    inverse = lax.rsqrt(q)
    taper = jnp.maximum(64.0 * UNIT**2 - q, 0.0)
    weight = taper * taper
    square = inverse * inverse
    near = 4.0 / UNIT - 9.0 / 8.0 / UNIT**2 * (q * inverse)
    far = inverse * (3.0 + square)
    iso = weight * jnp.where(q < 4.0 * UNIT**2, near, far)
    capped = jnp.minimum(square, 0.5)
    dyad = weight * (capped * (1.0 - capped))
    return iso, dyad, (dx, dy, dz), inverse, q


CLOSE = 1.0 / (2e-3 * UNIT)


def two_parts(value):
    high = value.astype(bf16)
    return high, (value - high.astype(f32)).astype(bf16)


def block_store(ref, block, r, j, value, lane):
    if j == 0:
        ref[block, r:r + 8, 0:128] = value
    elif j == 2:
        ref[block + 1, r:r + 8, 0:128] = value
    else:
        swapped = pltpu.roll(value, 64, 1)
        ref[block, r:r + 8, 128:256] = jnp.where(lane < 64, value, swapped)
        ref[block + 1, r:r + 8, 128:256] = jnp.where(lane < 64, swapped, value)


def unpack_spots(spots, pos, centre):
    row = lax.broadcasted_iota(i32, (8, 128), 0)
    lane = lax.broadcasted_iota(i32, (8, 128), 1)
    middle = jnp.where(row < 2, centre, 3.0)
    pos[NEAR, :, :] = jnp.zeros((8, WIDE), f32)

    def pair_body(pair, _):
        start = pl.multiple_of(pair * 2 * BLOCK, 128)
        for at in range(6):
            for j in range(3):
                spot = (spots[at, :, pl.ds(start + 128 * j, 128)] - middle) * UNIT
                for half in range(2):
                    block = at * SPAN + half * 16 + pair * 2
                    block_store(pos, block, 0, j, spot if half == 0 else pltpu.roll(spot, 7, 0), lane)
        return 0

    lax.fori_loop(0, 8, pair_body, 0)


def unpack_values(sources, raw):
    row = lax.broadcasted_iota(i32, (8, 128), 0)
    lane = lax.broadcasted_iota(i32, (8, 128), 1)
    raw[NEAR, :, :] = jnp.zeros((16, WIDE), f32)

    def pair_body(pair, _):
        start = pl.multiple_of(pair * 2 * BLOCK, 128)
        for view, at in sources:
            for j in range(3):
                x, y, z = (view[8 * a:8 * a + 8, pl.ds(start + 128 * j, 128)] for a in range(3))
                for half in range(2):
                    if half == 0:
                        first, second = jnp.where(row < 4, x, pltpu.roll(y, 4, 0)), z
                    else:
                        first, second = jnp.where(row < 4, pltpu.roll(x, 4, 0), y), pltpu.roll(z, 4, 0)
                    block = at * SPAN + half * 16 + pair * 2
                    block_store(raw, block, 0, j, first, lane)
                    block_store(raw, block, 8, j, second, lane)
        return 0

    lax.fori_loop(0, 8, pair_body, 0)


def repack(acc, out):
    row = lax.broadcasted_iota(i32, (8, 128), 0)
    lane = lax.broadcasted_iota(i32, (8, 128), 1)

    def pair_body(pair, _):
        start = pl.multiple_of(pair * 2 * BLOCK, 128)
        for at in range(6):
            for j in range(3):
                got = []
                for half in range(2):
                    block = at * SPAN + half * 16 + pair * 2
                    for r in (0, 8):
                        if j == 0:
                            got.append(acc[block, r:r + 8, 0:128])
                        elif j == 2:
                            got.append(acc[block + 1, r:r + 8, 0:128])
                        else:
                            even, odd = acc[block, r:r + 8, 128:256], acc[block + 1, r:r + 8, 128:256]
                            got.append(jnp.where(lane < 64, even, odd)
                                       + pltpu.roll(jnp.where(lane < 64, odd, even), 64, 1))
                a0, a1, b0, b1 = got
                lanes = pl.ds(start + 128 * j, 128)
                out[at, 0:8, lanes] = jnp.where(row < 4, a0, pltpu.roll(b0, 4, 0))
                out[at, 8:16, lanes] = jnp.where(row < 4, pltpu.roll(a0, 4, 0), b0)
                out[at, 16:24, lanes] = jnp.where(row < 4, a1, pltpu.roll(b1, 4, 0))
        return 0

    lax.fori_loop(0, 8, pair_body, 0)


def worker(plan_ref, pos, nearest, turned, raw=None, acc=None, sides=None, extra=None):
    row = lax.broadcasted_iota(i32, (8, WIDE), 0)
    across = (((1,), (1,)), ((), ()))

    def tile_of(t):
        packed = plan_ref[t // 128, t % 128]
        return packed // 256, packed % 256

    def build(t, turn_ref, matrices):
        p, c = tile_of(t)
        xj, yj, zj = (pos[c, n:n + 1, :] for n in (0, 2, 4))
        least = jnp.full((8, 128), 64.0, f32)
        side = lax.broadcasted_iota(i32, (CHUNK, 128), 1) < BLOCK - 128
        main, rest = slice(0, 128), slice(128, WIDE)

        for u in range(0, BLOCK // 2, CHUNK):
            w = u + BLOCK // 2
            there = [[jnp.broadcast_to(turn_ref[v:v + CHUNK, n:n + 1], (CHUNK, 128)) for n in (0, 2, 4)]
                     for v in (u, w)]
            there.append([jnp.where(side, one, two) for one, two in zip(*there)])
            for r, at, lanes in zip((u, w, u + BLOCK), there, (main, main, rest)):
                iso, dyad, _, inverse, q = mobility(*at, xj[:, lanes], yj[:, lanes], zj[:, lanes])
                for m, value in enumerate((iso, dyad * jnp.minimum(inverse, CLOSE))):
                    high, low = two_parts(value)
                    matrices[2 * m, r:r + CHUNK, :] = high
                    matrices[2 * m + 1, r:r + CHUNK, :] = low
                least = jnp.minimum(least, jnp.minimum(q[:8], q[8:]))
                yield
        nearest[...] = jnp.minimum(nearest[...], jnp.where(p == c, 64.0, least))

    def patterns(block):
        x, y, z = (pos[block, n:n + 1, :] for n in (0, 2, 4))
        return x, y, z, jnp.where(row < 4, x, y)

    def columns(block):
        x, y, z, both = patterns(block)
        first, second = raw[block, 0:8, :], raw[block, 8:16, :]
        t = first * both
        s = t + pltpu.roll(t, 4, 0) + pltpu.roll(second * z, 4, 0)
        second = jnp.where(row < 4, second, s)
        full = jnp.concatenate([first, second] + [part * scale for scale in (x, y, z) for part in (first, second)], axis=0)
        high = full.astype(bf16)
        rest = full - high.astype(f32)
        middle, low = two_parts(rest)
        return high, middle, low

    def finish(iso, dyad, block):
        x, y, z, both = patterns(block)
        last = jnp.where(row < 4, z, -1.0)

        def folded(r):
            t = dyad[r:r + 8] * both + dyad[r + 8:r + 16] * last
            return t + pltpu.roll(t, 4, 0)

        along = folded(0)
        upper = both * along - jnp.where(row < 4, folded(16), folded(32))
        under = z * along - folded(48)
        return ISO * iso[0:8] + DYAD * upper, ISO * iso[8:16] + DYAD * under

    def ready(t, slot):
        for side, block in zip(sides[slot], reversed(tile_of(t))):
            for n, part in enumerate(columns(block)):
                side[64 * n:64 * n + 64, :] = part
                yield

    def turn_rows(t, turn_ref):
        turn_ref[...] = jnp.transpose(pos[tile_of(t)[0]], (1, 0))
        yield

    def summed(by_high, by_low):
        return (by_high[0:64] + by_low[0:64]) + (by_high[64:128] + by_low[64:128]) + by_high[128:192]

    def apply(t, slot, matrices):
        p, c = tile_of(t)
        side = lax.broadcasted_iota(i32, (1, 128), 1) < BLOCK - 128
        none = jnp.zeros((BLOCK // 2, 128), bf16)

        def whole(m):
            rest = matrices[m, BLOCK:, :]
            rest = jnp.concatenate([jnp.where(side, rest, none), jnp.where(side, none, rest)], axis=0)
            return jnp.concatenate([matrices[m, 0:BLOCK, :], rest], axis=1)

        iso_high, iso_low, dyad_high, dyad_low = (whole(m) for m in range(4))
        dot = lambda a, b: jnp.dot(a, b, preferred_element_type=f32)
        dot_across = lambda a, b: lax.dot_general(a, b, across, preferred_element_type=f32)
        wide = sides[slot][0][...]
        slim = jnp.concatenate([wide[n:n + 16] for n in (0, 64)], axis=0)
        pad = jnp.zeros((64, WIDE - BLOCK), f32)
        dyad = dot_across(wide, dyad_high)
        yield
        dyad = summed(dyad, dot_across(wide[:128], dyad_low))
        yield
        iso = dot_across(slim, iso_high) + dot_across(slim, iso_low)
        yield
        upper, under = finish(jnp.concatenate([iso[:16] + iso[16:], pad[:16]], axis=1), jnp.concatenate([dyad, pad], axis=1), p)
        acc[p, 0:8, :] += upper
        acc[p, 8:16, :] += under
        yield
        wide = sides[slot][1][:, :BLOCK]
        slim = jnp.concatenate([wide[n:n + 16] for n in (0, 64)], axis=0)
        dyad = dot(wide, dyad_high)
        yield
        dyad = summed(dyad, dot(wide[:128], dyad_low))
        yield
        iso = dot(slim, iso_high) + dot(slim, iso_low)
        yield
        upper, under = finish(iso[:16] + iso[16:], dyad, c)
        acc[c, 0:8, :] += upper
        acc[c, 8:16, :] += under
        yield

    def any_close(t):
        p, c = tile_of(t)
        turned[0][...] = jnp.transpose(pos[p], (1, 0))
        xj, yj, zj = (pos[c, n:n + 1, :] for n in (0, 2, 4))
        least = jnp.full((8, WIDE), 64.0, f32)
        for r in range(0, BLOCK, 8):
            xi, yi, zi = (turned[0][r:r + 8, m:m + 1] for m in (0, 2, 4))
            dx, dy, dz = xi - xj, yi - yj, zi - zj
            apart = dx * dx + dy * dy + dz * dz
            least = jnp.minimum(least, jnp.where(apart > 0.0, apart, 64.0))
        return jnp.min(least) < 1.01 / CLOSE**2

    def close_pairs(t):
        p, c = tile_of(t)
        turned[0][...] = jnp.transpose(pos[p], (1, 0))
        single = lax.broadcasted_iota(i32, (1, WIDE), 1) < BLOCK
        xj, yj, zj = (pos[c, n:n + 1, :] for n in (0, 2, 4))
        col_parts, row_parts = columns(c), columns(p)
        col_vec = jnp.concatenate([col_parts[0][:16], col_parts[1][:16]], axis=0)
        row_vec = jnp.concatenate([row_parts[0][:16], row_parts[1][:16]], axis=0)[:, :BLOCK]

        col_vec = jnp.where(single, col_vec, jnp.zeros_like(col_vec))

        def one(n, _):
            for r in range(0, BLOCK, CHUNK):
                xi, yi, zi = (turned[0][r:r + CHUNK, m:m + 1] for m in (0, 2, 4))
                _, dyad, offset, inverse, _ = mobility(xi, yi, zi, xj, yj, zj)
                rest = dyad * jnp.maximum(inverse - CLOSE, 0.0)
                along = jnp.where(n == 0, offset[0], jnp.where(n == 1, offset[1], offset[2]))
                high, low = two_parts(rest * along)
                extra[0][r:r + CHUNK, :] = high
                extra[1][r:r + CHUNK, :] = low
            h, l = extra[0][...], extra[1][...]
            to_row = (lax.dot_general(col_vec, h, across, preferred_element_type=f32)
                      + lax.dot_general(col_vec, l, across, preferred_element_type=f32))
            to_row = jnp.concatenate([to_row, jnp.zeros((32, WIDE - BLOCK), f32)], axis=1)
            to_col = (jnp.dot(row_vec, h, preferred_element_type=f32)
                      + jnp.dot(row_vec, l, preferred_element_type=f32))
            for block, got, sign in ((p, to_row, 1.0), (c, to_col, -1.0)):
                x, y, z, both = patterns(block)
                last = jnp.where(row < 4, z, -1.0)
                got = got[:16] + got[16:]
                folded = got[:8] * both + got[8:] * last
                folded = sign * DYAD * (folded + pltpu.roll(folded, 4, 0)) * single
                acc[block, 0:8, :] += jnp.where(row // 4 == n, folded, 0.0)
                acc[block, 8:16, :] += jnp.where(row // 4 + 2 == n, folded, 0.0)
            return 0

        lax.fori_loop(0, 3, one, 0)

    def drain(*steps):
        steps = list(steps)
        while steps:
            for step in list(steps):
                if next(step, steps) is steps:
                    steps.remove(step)

    return types.SimpleNamespace(tile_of=tile_of, build=build, ready=ready, turn_rows=turn_rows, apply=apply,
                                 close_pairs=close_pairs, any_close=any_close, drain=drain)


KEPT = 128
DEEP = 8


def finish_sweep(work, plan_ref, nearest, selves, acc, out):
    count = plan_ref[7, 0]
    found = jnp.min(nearest[...]) < 1.01 / CLOSE**2

    def look(t, _):
        p, c = work.tile_of(t)

        @pl.when(found | (p == c))
        def _():
            @pl.when(found | work.any_close(t))
            def _():
                work.close_pairs(t)
        return 0

    lax.fori_loop(0, jnp.where(found | (selves > 0) | (count > KEPT), count, 0), look, 0)
    repack(acc, out)


def begin_sweep(values, raw, acc):
    unpack_values([(values.at[n], n) for n in range(6)], raw)
    acc[...] = jnp.zeros_like(acc)


def first_kernel(plan_ref, values, spots, out, kept, nearest, pos, raw, acc, store, sem, *scratch):
    turned, sides, extra = scratch[0:2], (scratch[2:4], scratch[4:6]), scratch[6:8]
    work = worker(plan_ref, pos, nearest, turned, raw, acc, sides, extra)
    nearest[...] = jnp.full((8, 128), 64.0, f32)
    begin_sweep(values, raw, acc)
    unpack_spots(spots, pos, plan_ref[7, 1].astype(f32))
    count = plan_ref[7, 0]
    pairs = (count + 1) // 2

    def out_copy(t):
        slot = lax.rem(t, DEEP)
        return pltpu.make_async_copy(store.at[slot], kept.at[t], sem.at[slot])

    def wait_out(t):
        @pl.when((t >= 0) & (t < KEPT))
        def _():
            out_copy(t).wait()

    work.drain(work.turn_rows(0, turned[0]), work.turn_rows(1, turned[1]))
    work.drain(work.build(0, turned[0], store.at[0]), work.ready(0, 0))
    out_copy(0).start()

    def body(n, selves):
        t = 2 * n
        for k in range(2):
            wait_out(t + 1 + k - DEEP)
        for k in range(2):
            p, c = work.tile_of(t + k)
            selves = selves + (p == c).astype(i32)
            work.drain(work.apply(t + k, k, store.at[lax.rem(t + k, DEEP)]),
                       work.build(t + k + 1, turned[1 - k], store.at[lax.rem(t + k + 1, DEEP)]),
                       work.turn_rows(t + k + 2, turned[k]), work.ready(t + k + 1, 1 - k))
        for k in range(2):
            @pl.when(t + 1 + k < KEPT)
            def _():
                out_copy(t + 1 + k).start()
        return selves

    selves = lax.fori_loop(0, pairs, body, 0)
    finish_sweep(work, plan_ref, nearest, selves, acc, out)
    for k in range(DEEP):
        wait_out(2 * pairs + 1 - DEEP + k)


TILE = (4, BLOCK + BLOCK // 2, 128)


def first_sweep(plan_list, values, spots):
    side = pltpu.VMEM((BLOCK, WIDE), bf16)
    return pl.pallas_call(
        first_kernel,
        out_shape=(jax.ShapeDtypeStruct((6, 24, HALF), f32), jax.ShapeDtypeStruct((KEPT,) + TILE, bf16),
                   jax.ShapeDtypeStruct((8, 128), f32), jax.ShapeDtypeStruct((NEAR + 1, 8, WIDE), f32)),
        in_specs=[SMEM, VMEM, VMEM],
        out_specs=(VMEM, pl.BlockSpec(memory_space=pl.ANY), VMEM, VMEM),
        scratch_shapes=[
            pltpu.VMEM((NEAR + 1, 16, WIDE), f32),
            pltpu.VMEM((NEAR + 1, 16, WIDE), f32),
            pltpu.VMEM((DEEP,) + TILE, bf16),
            pltpu.SemaphoreType.DMA((DEEP,)),
        ]
        + [pltpu.VMEM((WIDE, 8), f32)] * 2
        + [side] * 6,
        compiler_params=pltpu.CompilerParams(vmem_limit_bytes=48 * 2**20),
        name="first_sweep",
    )(plan_list, values, spots)


def second_kernel(plan_ref, values, pos, kept, least, out, raw, acc, store, sem, *scratch):
    turned, sides, extra, nearest = scratch[0:2], (scratch[2:4], scratch[4:6]), scratch[6:8], scratch[8]
    work = worker(plan_ref, pos, nearest, turned, raw, acc, sides, extra)
    count = plan_ref[7, 0]
    pairs = (jnp.minimum(count, KEPT) + 1) // 2

    def in_copy(t):
        slot = lax.rem(t, DEEP)
        return pltpu.make_async_copy(kept.at[t], store.at[slot], sem.at[slot])

    for t in range(DEEP):
        @pl.when(t < 2 * pairs)
        def _():
            in_copy(t).start()

    nearest[...] = least[...]
    begin_sweep(values, raw, acc)
    work.drain(work.ready(0, 0))

    def body(n, selves):
        t = 2 * n
        for k in range(2):
            in_copy(t + k).wait()
        for k in range(2):
            p, c = work.tile_of(t + k)
            selves = selves + (p == c).astype(i32)
            work.drain(work.apply(t + k, k, store.at[lax.rem(t + k, DEEP)]), work.ready(t + k + 1, 1 - k))

        @pl.when(n + DEEP // 2 < pairs)
        def _():
            for k in range(2):
                in_copy(t + k + DEEP).start()
        return selves

    selves = lax.fori_loop(0, pairs, body, 0)

    @pl.when(count > KEPT)
    def _():
        def more(t, _):
            work.drain(work.turn_rows(t, turned[0]), work.ready(t, 0))
            work.drain(work.build(t, turned[0], store.at[0]))
            work.drain(work.apply(t, 0, store.at[0]))
            return 0

        lax.fori_loop(KEPT, count, more, 0)

    finish_sweep(work, plan_ref, nearest, selves, acc, out)


def second_sweep(plan_list, values, pos, kept, least):
    side = pltpu.VMEM((BLOCK, WIDE), bf16)
    return pl.pallas_call(
        second_kernel,
        out_shape=jax.ShapeDtypeStruct((6, 24, HALF), f32),
        in_specs=[SMEM, VMEM, VMEM, pl.BlockSpec(memory_space=pl.ANY), VMEM],
        out_specs=VMEM,
        scratch_shapes=[
            pltpu.VMEM((NEAR + 1, 16, WIDE), f32),
            pltpu.VMEM((NEAR + 1, 16, WIDE), f32),
            pltpu.VMEM((DEEP,) + TILE, bf16),
            pltpu.SemaphoreType.DMA((DEEP,)),
        ]
        + [pltpu.VMEM((WIDE, 8), f32)] * 2
        + [side] * 6
        + [pltpu.VMEM((8, 128), f32)],
        compiler_params=pltpu.CompilerParams(vmem_limit_bytes=48 * 2**20),
        name="second_sweep",
    )(plan_list, values, pos, kept, least)


def collect(slab, sub, parts, own, inbox, stage, send, recv):
    right, left = other(slab, sub + 1), other(slab, sub + 3)
    one, two, three = (lax.rem(sub + d, N_SUB) for d in range(1, 4))
    copies = []

    def half(what, at, lanes, to, n):
        copies.append(push(what, inbox.at[at, :, lanes], send.at[n], recv.at[2 * at + (lanes is LATE)], to))

    def wait_half(at, lanes):
        wait_for(inbox.at[at, :, lanes], recv.at[2 * at + (lanes is LATE)], (slab, sub))

    half(parts.at[two, :, EARLY], 0, EARLY, right, 0)
    half(parts.at[two, :, LATE], 1, LATE, left, 1)
    copies.append(push(parts.at[4], inbox.at[5], send.at[2], recv.at[10], other(slab - 1, sub)))
    copies.append(push(parts.at[5], inbox.at[4], send.at[3], recv.at[8], other(slab + 1, sub)))
    half(parts.at[one, :, LATE], 2, LATE, right, 4)
    half(parts.at[three, :, EARLY], 3, EARLY, left, 5)
    wait_half(0, EARLY)
    stage[0, :, :] = parts[one, :, EARLY] + inbox[0, :, EARLY]
    half(stage.at[0], 2, EARLY, right, 6)
    wait_half(1, LATE)
    stage[1, :, :] = parts[three, :, LATE] + inbox[1, :, LATE]
    half(stage.at[1], 3, LATE, left, 7)
    wait_for(inbox.at[4], recv.at[8], (slab, sub))
    wait_for(inbox.at[5], recv.at[10], (slab, sub))
    total = own[...] + parts[sub] + inbox[4] + inbox[5]
    for at in (2, 3):
        for lanes in (EARLY, LATE):
            wait_half(at, lanes)
    return copies, total + inbox[2] + inbox[3]


def greet_near(slab, sub, more=()):
    greet([other(slab, sub + d) for d in range(1, N_SUB)] + [other(slab + d, sub) for d in (1, -1)] + list(more))


def turn_kernel(parts, own, near, inbox, stage, total, send, recv, gsend, grecv):
    slab, sub = place()
    greet_near(slab, sub)
    copies, value = collect(slab, sub, parts, own, inbox, stage, send, recv)
    total[...] = value
    copies += spread(slab, sub, total, near, gsend, grecv)
    for copy in copies:
        copy.wait_send()


def turn(parts, own):
    return pl.pallas_call(
        turn_kernel,
        out_shape=jax.ShapeDtypeStruct((6, 24, HALF), f32),
        in_specs=[VMEM, VMEM],
        out_specs=VMEM,
        scratch_shapes=[pltpu.VMEM((6, 24, HALF), f32), pltpu.VMEM((2, 24, WIDTH), f32), pltpu.VMEM((24, HALF), f32)]
        + [pltpu.SemaphoreType.DMA((n,)) for n in (8, 12, 8, 12)],
        compiler_params=pltpu.CompilerParams(collective_id=1, has_side_effects=True, vmem_limit_bytes=40 * 2**20),
        name="turn_around",
    )(parts, own)


def squares(value):
    sq = value * value
    folded = sq[0:8] + sq[8:16] + sq[16:24]
    lanes = folded[:, 0:128]
    for n in range(1, HALF // 128):
        lanes = lanes + folded[:, 128 * n:128 * n + 128]
    return lanes


def finish_kernel(parts, first, out_first, out_second, inbox, stage, box, send, recv, ssend, srecv):
    slab, sub = place()
    core = lax.rem(slab, 2)
    z = lax.rem(slab // 2, 4)
    y = slab // 8
    twin = slab + 1 - 2 * core
    groups = [[other(slab, sub + d) for d in range(1, 4)] + [other(twin, sub + d) for d in range(4)],
              [(y * 8 + lax.rem(z + d, 4) * 2 + core, sub) for d in range(1, 4)],
              [(lax.rem(y + d, 4) * 8 + z * 2 + core, sub) for d in range(1, 4)]]
    greet_near(slab, sub, groups[0][4:] + groups[1] + groups[2])
    copies, value = collect(slab, sub, parts, first, inbox, stage, send, recv)
    out_second[...] = value
    box[0, 0, 0:8, :] = squares(first[...])
    box[0, 0, 8:16, :] = squares(value)
    for n, group in enumerate(groups):
        turns = []
        for m, peer in enumerate(group):
            turns.append(push(box.at[n, 0], box.at[n, m + 1], ssend.at[7 * n + m], srecv.at[7 * n + m], peer))
        for copy in turns:
            copy.wait_recv()
        copies += turns
        now = box[n, 0]
        for m in range(len(group)):
            now = now + box[n, m + 1]
        box[n + 1, 0, :, :] = now
    total = jnp.sum(box[3, 0], axis=1, keepdims=True)
    per = 1.0 / (3.0 * BLOCK * SPAN * N_SUB * N_SLAB)
    one, two = total[0:8], total[8:16]
    one = (one + pltpu.roll(jnp.broadcast_to(one, (8, 128)), 4, 0)) * per
    two = (two + pltpu.roll(jnp.broadcast_to(two, (8, 128)), 4, 0)) * per
    scale_one = lax.rsqrt(one + 1e-6)
    scale_two = scale_one * lax.rsqrt(scale_one * scale_one * two + 1e-6)
    for r in range(0, 24, 8):
        out_first[r:r + 8, :] = first[r:r + 8, :] * scale_one[:, 0:1]
        out_second[r:r + 8, :] = out_second[r:r + 8, :] * scale_two[:, 0:1]
    for copy in copies:
        copy.wait_send()


def finish_all(parts, first):
    return pl.pallas_call(
        finish_kernel,
        out_shape=(jax.ShapeDtypeStruct((24, HALF), f32),) * 2,
        in_specs=[VMEM, VMEM],
        out_specs=(VMEM, VMEM),
        scratch_shapes=[pltpu.VMEM((6, 24, HALF), f32), pltpu.VMEM((2, 24, WIDTH), f32), pltpu.VMEM((4, 8, 16, 128), f32)]
        + [pltpu.SemaphoreType.DMA((n,)) for n in (8, 12, 21, 21)],
        compiler_params=pltpu.CompilerParams(collective_id=2, has_side_effects=True, vmem_limit_bytes=40 * 2**20),
        name="finish_all",
    )(parts, first)


def body(positions, forces, tile_rows, tile_cols, tile_count):
    _, sub = place()
    values, spots, own, table = gather(forces, positions, tile_rows[None], tile_cols[None], tile_count)
    plan_list = plan(table, spots)
    parts, kept, least, pos = first_sweep(plan_list, values, spots)
    near_second = turn(parts, own)
    parts = second_sweep(plan_list, near_second, pos, kept, least)
    first = lax.dynamic_index_in_dim(near_second, sub, 0, keepdims=False)
    outs = finish_all(parts, first)
    return tuple(o.reshape(3, 2, 4, HALF).transpose(2, 0, 1, 3).reshape(12, 2 * HALF) for o in outs)


def solution(mesh):
    placed = (
        P(None, ("slab", "sub")),
        P(None, ("slab", "sub")),
        P(("slab", "sub")),
        P(("slab", "sub")),
        P(("slab", "sub")),
    )
    return jax.shard_map(
        body,
        mesh=mesh,
        in_specs=placed,
        out_specs=(P(None, ("slab", "sub")), P(None, ("slab", "sub"))),
        check_vma=False,
    )
```

```python
import functools
import types

import jax
import jax.numpy as jnp
from jax import lax
from jax.experimental import pallas as pl
from jax.experimental.pallas import tpu as pltpu
from jax.sharding import PartitionSpec as P

f32, bf16, i32 = jnp.float32, jnp.bfloat16, jnp.int32
BLOCK = 192
WIDE = 256
CHUNK = 16
SPAN = 32
HALF = SPAN // 2 * BLOCK
NEAR = 6 * SPAN
N_SUB = 4
N_SLAB = 32
LIST = 6 * 128 + 128
MESH = pl.DeviceIdType.MESH
VMEM = pl.BlockSpec(memory_space=pltpu.VMEM)
SMEM = pl.BlockSpec(memory_space=pltpu.SMEM)


def place():
    return lax.axis_index("slab"), lax.axis_index("sub")


def other(slab, sub):
    return (lax.rem(slab + N_SLAB, N_SLAB), lax.rem(sub, N_SUB))


def push(src, dst, send, recv, to):
    copy = pltpu.make_async_remote_copy(
        src_ref=src, dst_ref=dst, send_sem=send, recv_sem=recv, device_id=to, device_id_type=MESH
    )
    copy.start()
    return copy


def greet(peers):
    barrier = pltpu.get_barrier_semaphore()
    for peer in peers:
        pl.semaphore_signal(barrier, inc=1, device_id=peer, device_id_type=MESH)
    pl.semaphore_wait(barrier, len(peers))


WIDTH = HALF // 2
EARLY, LATE = slice(0, WIDTH), slice(WIDTH, HALF)


def wait_for(ref, sem, me):
    pltpu.make_async_remote_copy(
        src_ref=ref, dst_ref=ref, send_sem=sem, recv_sem=sem, device_id=me, device_id_type=MESH
    ).wait_recv()


def spread(slab, sub, src, near, send, recv):
    right, left = other(slab, sub + 1), other(slab, sub + 3)
    one, two, three = (lax.rem(sub + d, N_SUB) for d in range(1, 4))
    copies = []

    def half(what, at, lanes, to, n):
        copies.append(push(what.at[:, lanes], near.at[at, :, lanes], send.at[n],
                           recv.at[2 * at + (lanes is LATE)], to))

    half(src, sub, EARLY, right, 0)
    half(src, sub, LATE, left, 1)
    copies.append(push(src, near.at[4], send.at[2], recv.at[8], other(slab + 1, sub)))
    copies.append(push(src, near.at[5], send.at[3], recv.at[10], other(slab - 1, sub)))
    half(src, sub, LATE, right, 4)
    half(src, sub, EARLY, left, 5)
    near[sub, :, :] = src[...]

    def wait_half(at, lanes):
        wait_for(near.at[at, :, lanes], recv.at[2 * at + (lanes is LATE)], (slab, sub))

    wait_half(three, EARLY)
    half(near.at[three], three, EARLY, right, 6)
    wait_half(one, LATE)
    half(near.at[one], one, LATE, left, 7)
    for at, lanes in ((three, LATE), (one, EARLY), (two, EARLY), (two, LATE)):
        wait_half(at, lanes)
    wait_for(near.at[4], recv.at[8], (slab, sub))
    wait_for(near.at[5], recv.at[10], (slab, sub))
    return copies


def gather_kernel(forces_far, positions_far, rows_far, cols_far, count, values, spots, own, table,
                  forces, positions, rows, cols, in_sem, near, x, mine, send, recv, tsend, trecv, wsend, wrecv):
    slab, sub = place()
    fetches = [pltpu.make_async_copy(src, dst, in_sem.at[n]) for n, (src, dst) in enumerate(
        ((forces_far, forces), (positions_far, positions), (rows_far, rows), (cols_far, cols)))]
    for fetch in fetches:
        fetch.start()
    x[30:32, :] = jnp.zeros((2, HALF), f32)
    for fetch in fetches:
        fetch.wait()
    col = (cols[...] - (slab - 1) * (N_SUB * SPAN)).astype(f32)
    live = jnp.where(lax.broadcasted_iota(i32, (1, 128), 1) < count[0], 1.0, 0.0)
    x[30:31, 0:128] = (rows[...] - (slab * N_SUB + sub) * SPAN).astype(f32)
    x[30:31, 128:256] = col
    x[30:31, 256:384] = live
    upper = jnp.sum(jnp.where(col >= 256.0, live, 0.0), axis=1, keepdims=True)
    lower = jnp.sum(jnp.where(col < 128.0, live, 0.0), axis=1, keepdims=True)
    whole = jnp.sum(live, axis=1, keepdims=True)
    row = lax.broadcasted_iota(i32, (8, 128), 0)
    mine[...] = jnp.where(row == 0, upper, jnp.where(row == 1, lower, jnp.where(row == 2, whole, 0.0)))
    for a in range(3):
        for half in range(2):
            lanes = slice(half * HALF, half * HALF + HALF)
            for k in range(4):
                x[a * 8 + half * 4 + k:a * 8 + half * 4 + k + 1, :] = forces[3 * k + a:3 * k + a + 1, lanes]
            x[24 + 2 * a + half:25 + 2 * a + half, :] = positions[a:a + 1, lanes]
    greet([other(slab, sub + d) for d in range(1, N_SUB)]
          + [other(slab + d, sub) for d in (1, -1, 2, -2)])
    at_own = pl.ds(pl.multiple_of(sub * 8, 8), 8)
    copies = [push(mine, table.at[2, at_own], tsend.at[d - 1], trecv.at[sub], other(slab, sub + d))
              for d in range(1, N_SUB)]
    table[2, at_own, :] = mine[...]
    for d in range(1, N_SUB):
        at = lax.rem(sub + d, N_SUB)
        wait_for(table.at[2, pl.ds(pl.multiple_of(at * 8, 8), 8)], trecv.at[at], (slab, sub))
    turns = [push(table.at[2], table.at[2 - d], wsend.at[n], wrecv.at[n], other(slab + d, sub))
             for n, d in enumerate((1, -1, 2, -2))]
    own[...] = x[0:24, :]
    copies += spread(slab, sub, x, near, send, recv)
    for n in range(6):
        values[n, :, :] = near[n, 0:24, :]
        spots[n, :, :] = near[n, 24:32, :]
    for copy in turns:
        copy.wait_recv()
    for copy in copies + turns:
        copy.wait_send()


def gather(forces, positions, rows, cols, count):
    return pl.pallas_call(
        gather_kernel,
        out_shape=(jax.ShapeDtypeStruct((6, 24, HALF), f32), jax.ShapeDtypeStruct((6, 8, HALF), f32),
                   jax.ShapeDtypeStruct((24, HALF), f32), jax.ShapeDtypeStruct((5, 32, 128), f32)),
        in_specs=[pl.BlockSpec(memory_space=pltpu.HBM)] * 4 + [SMEM],
        out_specs=(VMEM,) * 4,
        scratch_shapes=[pltpu.VMEM((12, 2 * HALF), f32), pltpu.VMEM((3, 2 * HALF), f32), pltpu.VMEM((1, 128), i32),
                        pltpu.VMEM((1, 128), i32), pltpu.SemaphoreType.DMA((4,)), pltpu.VMEM((6, 32, HALF), f32), pltpu.VMEM((32, HALF), f32), pltpu.VMEM((8, 128), f32)]
        + [pltpu.SemaphoreType.DMA((n,)) for n in (8, 12, 3, 4, 4, 4)],
        compiler_params=pltpu.CompilerParams(collective_id=0, has_side_effects=True, vmem_limit_bytes=40 * 2**20),
        name="gather_all",
    )(forces, positions, rows, cols, count)


def given(flow, counts):
    total = counts[0] + counts[1] + counts[2] + counts[3]
    whole = jnp.minimum(jnp.floor(jnp.maximum(flow, 0.0)), total)
    part = whole / jnp.maximum(total, 1.0)
    return [jnp.minimum(jnp.floor(part * n), n) for n in counts]


def plan_kernel(table, spots, out):
    slab, sub = place()
    lists = jnp.concatenate([spots[n, 6:7, 0:384] for n in range(6)] + [jnp.zeros((2, 384), f32)], axis=0)
    at = lambda rel, sub_at, kind: table[rel + 2, 8 * sub_at + kind:8 * sub_at + kind + 1, :]
    subs = range(N_SUB)
    total = {rel: sum(at(rel, v, 2) for v in subs) for rel in range(-2, 3)}
    first, last = slab == 0, slab == N_SLAB - 1

    def flow(a, b, c, d):
        return (a - d + 2.0 * (b - c)) * 0.2

    before = flow(jnp.where(slab == 1, total[-1], total[-2]), total[-1], total[0],
                  jnp.where(last, total[0], total[1]))
    after = flow(jnp.where(first, total[0], total[-1]), total[0], total[1],
                 jnp.where(slab == N_SLAB - 2, total[1], total[2]))
    before = jnp.where(first, 0.0, before)
    after = jnp.where(last, 0.0, after)
    ups = [at(0, v, 0) for v in subs]
    downs = [at(0, v, 1) for v in subs]
    up_given = given(after, ups)
    down_given = given(-before, downs)
    from_before = given(before, [at(-1, v, 0) for v in subs])
    from_after = given(-after, [at(1, v, 1) for v in subs])

    col = lists[:, 128:256]
    alive = lists[:, 256:384] > 0.5
    row_local = lists[:, :128]
    is_up = alive & (col >= 256.0)
    is_down = alive & (col < 128.0)
    is_own = alive & (col >= 128.0) & (col < 256.0)
    within = col - jnp.where(col >= 256.0, 256.0, jnp.where(col >= 128.0, 128.0, 0.0))
    col_sub = jnp.floor(within * (1.0 / SPAN))
    col_local = within - SPAN * col_sub
    masks = jnp.concatenate([m.astype(f32) for m in (is_up, is_down, is_own)], axis=0)
    lane_a = lax.broadcasted_iota(i32, (128, 128), 0)
    lane_b = lax.broadcasted_iota(i32, (128, 128), 1)
    ahead = (lane_a < lane_b).astype(bf16)
    rank = jnp.dot(masks.astype(bf16), ahead, preferred_element_type=f32)
    up_rank, down_rank, own_rank = rank[0:8], rank[8:16], rank[16:24]

    seat = lax.broadcasted_iota(i32, (8, 128), 0)

    def rows(values):
        full = jnp.zeros((8, 128), f32)
        for n, value in enumerate(values):
            full = jnp.where(seat == n, value, full)
        return full

    pick = lambda values: sum(jnp.where(sub == v, values[v], 0.0) for v in subs)
    up_limit = rows(up_given + [pick(from_before), jnp.zeros((1, 128), f32)])
    down_limit = rows(down_given + [jnp.zeros((1, 128), f32), pick(from_after)])
    up_sent = is_up & (up_rank < up_limit)
    down_sent = is_down & (down_rank < down_limit)
    in_slab = seat < 4
    crossing = in_slab & ((is_up & ~up_sent) | (is_down & ~down_sent))
    fixed = []
    for v in subs:
        kept = jnp.where(crossing & (col_sub == float(v)), 1.0, 0.0)
        fixed.append(jnp.sum(jnp.sum(kept, axis=0, keepdims=True), axis=1, keepdims=True)
                     + from_before[v] + from_after[v])
    own_counts = [at(0, v, 2) - ups[v] - downs[v] for v in subs]
    own_total = sum(own_counts)
    level = (sum(fixed) + own_total) * 0.25
    wish = [jnp.maximum(level - have, 0.0) for have in fixed]
    scale = own_total / jnp.maximum(sum(wish), 1.0)
    edges = [jnp.zeros((1, 128), f32)]
    run = jnp.zeros((1, 128), f32)
    for v in range(3):
        run = run + wish[v] * scale
        edges.append(jnp.minimum(jnp.floor(run + 0.5), own_total))
    edges.append(own_total)
    begin = pick(edges[:4])
    end = pick(edges[1:])
    start, offsets = jnp.zeros((1, 128), f32), []
    for v in subs:
        offsets.append(start)
        start = start + own_counts[v]
    place_own = own_rank + rows(offsets)
    mine = (crossing & (col_sub == sub.astype(f32))) | (
        in_slab & is_own & (place_own >= begin) & (place_own < end))
    mine = mine | ((seat == 4) & up_sent) | ((seat == 5) & down_sent)
    mine_value = mine.astype(f32)
    slot = jnp.dot(mine_value.astype(bf16), ahead, preferred_element_type=f32)
    counted = jnp.sum(mine_value, axis=1, keepdims=True)
    start, offsets = jnp.zeros((1, 1), f32), []
    for n in range(6):
        offsets.append(start)
        start = start + counted[n:n + 1]
    slot = slot + rows(offsets)
    slot = jnp.where(mine, slot, -1.0)
    row_near = row_local + SPAN * seat.astype(f32)
    inside = SPAN * col_sub + col_local
    col_near = jnp.where(in_slab, jnp.where(is_up, 160.0 + col_local, jnp.where(is_down, 128.0 + col_local, inside)),
                         inside)
    slot_t = jnp.transpose(slot, (1, 0))
    target = lax.broadcasted_iota(i32, (128, LIST), 1).astype(f32)
    result = jnp.zeros((16, LIST), f32)
    pad = jnp.zeros((14, 128), f32)
    for n in range(6):
        chosen = (slot_t[:, n:n + 1] == target).astype(bf16)
        values = jnp.concatenate([row_near[n:n + 1], col_near[n:n + 1], pad], axis=0).astype(bf16)
        result = result + jnp.dot(values, chosen, preferred_element_type=f32)
    lane_wide = lax.broadcasted_iota(i32, (1, LIST), 1).astype(f32)
    packed = jnp.where(lane_wide < start, result[0:1] * 256.0 + result[1:2], NEAR * 257.0)
    last_row = jnp.where(lane_b[0:1] == 0, start, 4.0 * slab.astype(f32) + 2.0)
    out[...] = jnp.concatenate([packed[:, 128 * n:128 * n + 128] for n in range(7)] + [last_row], axis=0).astype(i32)


def plan(table, spots):
    return pl.pallas_call(
        plan_kernel,
        out_shape=jax.ShapeDtypeStruct((8, 128), i32),
        in_specs=[VMEM, VMEM],
        out_specs=VMEM,
        compiler_params=pltpu.CompilerParams(vmem_limit_bytes=40 * 2**20),
        name="plan_tiles",
    )(table, spots)


UNIT = 0.5 ** 0.5
ISO = 0.25 * UNIT / (64.0 * UNIT**2) ** 2
DYAD = 3.0 * ISO


def mobility(xi, yi, zi, xj, yj, zj):
    dx, dy, dz = xi - xj, yi - yj, zi - zj
    q = jnp.maximum(dx * dx + dy * dy + dz * dz, 1e-12 * UNIT**2)
    inverse = lax.rsqrt(q)
    taper = jnp.maximum(64.0 * UNIT**2 - q, 0.0)
    weight = taper * taper
    square = inverse * inverse
    near = 4.0 / UNIT - 9.0 / 8.0 / UNIT**2 * (q * inverse)
    far = inverse * (3.0 + square)
    iso = weight * jnp.where(q < 4.0 * UNIT**2, near, far)
    capped = jnp.minimum(square, 0.5)
    dyad = weight * (capped * (1.0 - capped))
    return iso, dyad, (dx, dy, dz), inverse, q


CLOSE = 1.0 / (2e-3 * UNIT)


def two_parts(value):
    high = value.astype(bf16)
    return high, (value - high.astype(f32)).astype(bf16)


def block_store(ref, block, r, j, value, lane):
    if j == 0:
        ref[block, r:r + 8, 0:128] = value
    elif j == 2:
        ref[block + 1, r:r + 8, 0:128] = value
    else:
        swapped = pltpu.roll(value, 64, 1)
        ref[block, r:r + 8, 128:256] = jnp.where(lane < 64, value, swapped)
        ref[block + 1, r:r + 8, 128:256] = jnp.where(lane < 64, swapped, value)


def unpack_spots(spots, pos, centre):
    row = lax.broadcasted_iota(i32, (8, 128), 0)
    lane = lax.broadcasted_iota(i32, (8, 128), 1)
    middle = jnp.where(row < 2, centre, 3.0)
    pos[NEAR, :, :] = jnp.zeros((8, WIDE), f32)

    def pair_body(pair, _):
        start = pl.multiple_of(pair * 2 * BLOCK, 128)
        for at in range(6):
            for j in range(3):
                spot = (spots[at, :, pl.ds(start + 128 * j, 128)] - middle) * UNIT
                for half in range(2):
                    block = at * SPAN + half * 16 + pair * 2
                    block_store(pos, block, 0, j, spot if half == 0 else pltpu.roll(spot, 7, 0), lane)
        return 0

    lax.fori_loop(0, 8, pair_body, 0)


def unpack_values(sources, raw):
    row = lax.broadcasted_iota(i32, (8, 128), 0)
    lane = lax.broadcasted_iota(i32, (8, 128), 1)
    raw[NEAR, :, :] = jnp.zeros((16, WIDE), f32)

    def pair_body(pair, _):
        start = pl.multiple_of(pair * 2 * BLOCK, 128)
        for view, at in sources:
            for j in range(3):
                x, y, z = (view[8 * a:8 * a + 8, pl.ds(start + 128 * j, 128)] for a in range(3))
                for half in range(2):
                    if half == 0:
                        first, second = jnp.where(row < 4, x, pltpu.roll(y, 4, 0)), z
                    else:
                        first, second = jnp.where(row < 4, pltpu.roll(x, 4, 0), y), pltpu.roll(z, 4, 0)
                    block = at * SPAN + half * 16 + pair * 2
                    block_store(raw, block, 0, j, first, lane)
                    block_store(raw, block, 8, j, second, lane)
        return 0

    lax.fori_loop(0, 8, pair_body, 0)


def repack(acc, out):
    row = lax.broadcasted_iota(i32, (8, 128), 0)
    lane = lax.broadcasted_iota(i32, (8, 128), 1)

    def pair_body(pair, _):
        start = pl.multiple_of(pair * 2 * BLOCK, 128)
        for at in range(6):
            for j in range(3):
                got = []
                for half in range(2):
                    block = at * SPAN + half * 16 + pair * 2
                    for r in (0, 8):
                        if j == 0:
                            got.append(acc[block, r:r + 8, 0:128])
                        elif j == 2:
                            got.append(acc[block + 1, r:r + 8, 0:128])
                        else:
                            even, odd = acc[block, r:r + 8, 128:256], acc[block + 1, r:r + 8, 128:256]
                            got.append(jnp.where(lane < 64, even, odd)
                                       + pltpu.roll(jnp.where(lane < 64, odd, even), 64, 1))
                a0, a1, b0, b1 = got
                lanes = pl.ds(start + 128 * j, 128)
                out[at, 0:8, lanes] = jnp.where(row < 4, a0, pltpu.roll(b0, 4, 0))
                out[at, 8:16, lanes] = jnp.where(row < 4, pltpu.roll(a0, 4, 0), b0)
                out[at, 16:24, lanes] = jnp.where(row < 4, a1, pltpu.roll(b1, 4, 0))
        return 0

    lax.fori_loop(0, 8, pair_body, 0)


def worker(plan_ref, pos, nearest, turned, raw=None, acc=None, sides=None, extra=None):
    row = lax.broadcasted_iota(i32, (8, WIDE), 0)
    across = (((1,), (1,)), ((), ()))

    def tile_of(t):
        packed = plan_ref[t // 128, t % 128]
        return packed // 256, packed % 256

    def build(t, turn_ref, matrices):
        p, c = tile_of(t)
        xj, yj, zj = (pos[c, n:n + 1, :] for n in (0, 2, 4))
        least = jnp.full((8, 128), 64.0, f32)
        side = lax.broadcasted_iota(i32, (CHUNK, 128), 1) < BLOCK - 128
        main, rest = slice(0, 128), slice(128, WIDE)

        for u in range(0, BLOCK // 2, CHUNK):
            w = u + BLOCK // 2
            there = [[jnp.broadcast_to(turn_ref[v:v + CHUNK, n:n + 1], (CHUNK, 128)) for n in (0, 2, 4)]
                     for v in (u, w)]
            there.append([jnp.where(side, one, two) for one, two in zip(*there)])
            for r, at, lanes in zip((u, w, u + BLOCK), there, (main, main, rest)):
                iso, dyad, _, inverse, q = mobility(*at, xj[:, lanes], yj[:, lanes], zj[:, lanes])
                for m, value in enumerate((iso, dyad * jnp.minimum(inverse, CLOSE))):
                    high, low = two_parts(value)
                    matrices[2 * m, r:r + CHUNK, :] = high
                    matrices[2 * m + 1, r:r + CHUNK, :] = low
                least = jnp.minimum(least, jnp.minimum(q[:8], q[8:]))
                yield
        nearest[...] = jnp.minimum(nearest[...], jnp.where(p == c, 64.0, least))

    def patterns(block):
        x, y, z = (pos[block, n:n + 1, :] for n in (0, 2, 4))
        return x, y, z, jnp.where(row < 4, x, y)

    def columns(block):
        x, y, z, both = patterns(block)
        first, second = raw[block, 0:8, :], raw[block, 8:16, :]
        t = first * both
        s = t + pltpu.roll(t, 4, 0) + pltpu.roll(second * z, 4, 0)
        second = jnp.where(row < 4, second, s)
        full = jnp.concatenate([first, second] + [part * scale for scale in (x, y, z) for part in (first, second)], axis=0)
        high = full.astype(bf16)
        rest = full - high.astype(f32)
        middle, low = two_parts(rest)
        return high, middle, low

    def finish(iso, dyad, block):
        x, y, z, both = patterns(block)
        last = jnp.where(row < 4, z, -1.0)

        def folded(r):
            t = dyad[r:r + 8] * both + dyad[r + 8:r + 16] * last
            return t + pltpu.roll(t, 4, 0)

        along = folded(0)
        upper = both * along - jnp.where(row < 4, folded(16), folded(32))
        under = z * along - folded(48)
        return ISO * iso[0:8] + DYAD * upper, ISO * iso[8:16] + DYAD * under

    def ready(t, slot):
        for side, block in zip(sides[slot], reversed(tile_of(t))):
            for n, part in enumerate(columns(block)):
                side[64 * n:64 * n + 64, :] = part
                yield

    def turn_rows(t, turn_ref):
        turn_ref[...] = jnp.transpose(pos[tile_of(t)[0]], (1, 0))
        yield

    def summed(by_high, by_low):
        return (by_high[0:64] + by_low[0:64]) + (by_high[64:128] + by_low[64:128]) + by_high[128:192]

    def apply(t, slot, matrices):
        p, c = tile_of(t)
        side = lax.broadcasted_iota(i32, (1, 128), 1) < BLOCK - 128
        none = jnp.zeros((BLOCK // 2, 128), bf16)

        def whole(m):
            rest = matrices[m, BLOCK:, :]
            rest = jnp.concatenate([jnp.where(side, rest, none), jnp.where(side, none, rest)], axis=0)
            return jnp.concatenate([matrices[m, 0:BLOCK, :], rest], axis=1)

        iso_high, iso_low, dyad_high, dyad_low = (whole(m) for m in range(4))
        dot = lambda a, b: jnp.dot(a, b, preferred_element_type=f32)
        dot_across = lambda a, b: lax.dot_general(a, b, across, preferred_element_type=f32)
        wide = sides[slot][0][...]
        slim = jnp.concatenate([wide[n:n + 16] for n in (0, 64)], axis=0)
        pad = jnp.zeros((64, WIDE - BLOCK), f32)
        dyad = dot_across(wide, dyad_high)
        yield
        dyad = summed(dyad, dot_across(wide[:128], dyad_low))
        yield
        iso = dot_across(slim, iso_high) + dot_across(slim, iso_low)
        yield
        upper, under = finish(jnp.concatenate([iso[:16] + iso[16:], pad[:16]], axis=1), jnp.concatenate([dyad, pad], axis=1), p)
        acc[p, 0:8, :] += upper
        acc[p, 8:16, :] += under
        yield
        wide = sides[slot][1][:, :BLOCK]
        slim = jnp.concatenate([wide[n:n + 16] for n in (0, 64)], axis=0)
        dyad = dot(wide, dyad_high)
        yield
        dyad = summed(dyad, dot(wide[:128], dyad_low))
        yield
        iso = dot(slim, iso_high) + dot(slim, iso_low)
        yield
        upper, under = finish(iso[:16] + iso[16:], dyad, c)
        acc[c, 0:8, :] += upper
        acc[c, 8:16, :] += under
        yield

    def any_close(t):
        p, c = tile_of(t)
        turned[0][...] = jnp.transpose(pos[p], (1, 0))
        xj, yj, zj = (pos[c, n:n + 1, :] for n in (0, 2, 4))
        least = jnp.full((8, WIDE), 64.0, f32)
        for r in range(0, BLOCK, 8):
            xi, yi, zi = (turned[0][r:r + 8, m:m + 1] for m in (0, 2, 4))
            dx, dy, dz = xi - xj, yi - yj, zi - zj
            apart = dx * dx + dy * dy + dz * dz
            least = jnp.minimum(least, jnp.where(apart > 0.0, apart, 64.0))
        return jnp.min(least) < 1.01 / CLOSE**2

    def close_pairs(t):
        p, c = tile_of(t)
        turned[0][...] = jnp.transpose(pos[p], (1, 0))
        single = lax.broadcasted_iota(i32, (1, WIDE), 1) < BLOCK
        xj, yj, zj = (pos[c, n:n + 1, :] for n in (0, 2, 4))
        col_parts, row_parts = columns(c), columns(p)
        col_vec = jnp.concatenate([col_parts[0][:16], col_parts[1][:16]], axis=0)
        row_vec = jnp.concatenate([row_parts[0][:16], row_parts[1][:16]], axis=0)[:, :BLOCK]

        col_vec = jnp.where(single, col_vec, jnp.zeros_like(col_vec))

        def one(n, _):
            for r in range(0, BLOCK, CHUNK):
                xi, yi, zi = (turned[0][r:r + CHUNK, m:m + 1] for m in (0, 2, 4))
                _, dyad, offset, inverse, _ = mobility(xi, yi, zi, xj, yj, zj)
                rest = dyad * jnp.maximum(inverse - CLOSE, 0.0)
                along = jnp.where(n == 0, offset[0], jnp.where(n == 1, offset[1], offset[2]))
                high, low = two_parts(rest * along)
                extra[0][r:r + CHUNK, :] = high
                extra[1][r:r + CHUNK, :] = low
            h, l = extra[0][...], extra[1][...]
            to_row = (lax.dot_general(col_vec, h, across, preferred_element_type=f32)
                      + lax.dot_general(col_vec, l, across, preferred_element_type=f32))
            to_row = jnp.concatenate([to_row, jnp.zeros((32, WIDE - BLOCK), f32)], axis=1)
            to_col = (jnp.dot(row_vec, h, preferred_element_type=f32)
                      + jnp.dot(row_vec, l, preferred_element_type=f32))
            for block, got, sign in ((p, to_row, 1.0), (c, to_col, -1.0)):
                x, y, z, both = patterns(block)
                last = jnp.where(row < 4, z, -1.0)
                got = got[:16] + got[16:]
                folded = got[:8] * both + got[8:] * last
                folded = sign * DYAD * (folded + pltpu.roll(folded, 4, 0)) * single
                acc[block, 0:8, :] += jnp.where(row // 4 == n, folded, 0.0)
                acc[block, 8:16, :] += jnp.where(row // 4 + 2 == n, folded, 0.0)
            return 0

        lax.fori_loop(0, 3, one, 0)

    def drain(*steps):
        steps = list(steps)
        while steps:
            for step in list(steps):
                if next(step, steps) is steps:
                    steps.remove(step)

    return types.SimpleNamespace(tile_of=tile_of, build=build, ready=ready, turn_rows=turn_rows, apply=apply,
                                 close_pairs=close_pairs, any_close=any_close, drain=drain)


KEPT = 128
DEEP = 8


def finish_sweep(work, plan_ref, nearest, selves, acc, out):
    count = plan_ref[7, 0]
    found = jnp.min(nearest[...]) < 1.01 / CLOSE**2

    def look(t, _):
        p, c = work.tile_of(t)

        @pl.when(found | (p == c))
        def _():
            @pl.when(found | work.any_close(t))
            def _():
                work.close_pairs(t)
        return 0

    lax.fori_loop(0, jnp.where(found | (selves > 0) | (count > KEPT), count, 0), look, 0)
    repack(acc, out)


def begin_sweep(values, raw, acc):
    unpack_values([(values.at[n], n) for n in range(6)], raw)
    acc[...] = jnp.zeros_like(acc)


def first_kernel(plan_ref, values, spots, out, kept, nearest, pos, raw, acc, store, sem, *scratch):
    turned, sides, extra = scratch[0:2], (scratch[2:4], scratch[4:6]), scratch[6:8]
    work = worker(plan_ref, pos, nearest, turned, raw, acc, sides, extra)
    nearest[...] = jnp.full((8, 128), 64.0, f32)
    begin_sweep(values, raw, acc)
    unpack_spots(spots, pos, plan_ref[7, 1].astype(f32))
    count = plan_ref[7, 0]
    pairs = (count + 1) // 2

    def out_copy(t):
        slot = lax.rem(t, DEEP)
        return pltpu.make_async_copy(store.at[slot], kept.at[t], sem.at[slot])

    def wait_out(t):
        @pl.when((t >= 0) & (t < KEPT))
        def _():
            out_copy(t).wait()

    work.drain(work.turn_rows(0, turned[0]), work.turn_rows(1, turned[1]))
    work.drain(work.build(0, turned[0], store.at[0]), work.ready(0, 0))
    out_copy(0).start()

    def body(n, selves):
        t = 2 * n
        for k in range(2):
            wait_out(t + 1 + k - DEEP)
        for k in range(2):
            p, c = work.tile_of(t + k)
            selves = selves + (p == c).astype(i32)
            work.drain(work.apply(t + k, k, store.at[lax.rem(t + k, DEEP)]),
                       work.build(t + k + 1, turned[1 - k], store.at[lax.rem(t + k + 1, DEEP)]),
                       work.turn_rows(t + k + 2, turned[k]), work.ready(t + k + 1, 1 - k))
        for k in range(2):
            @pl.when(t + 1 + k < KEPT)
            def _():
                out_copy(t + 1 + k).start()
        return selves

    selves = lax.fori_loop(0, pairs, body, 0)
    finish_sweep(work, plan_ref, nearest, selves, acc, out)
    for k in range(DEEP):
        wait_out(2 * pairs + 1 - DEEP + k)


TILE = (4, BLOCK + BLOCK // 2, 128)


def first_sweep(plan_list, values, spots):
    side = pltpu.VMEM((BLOCK, WIDE), bf16)
    return pl.pallas_call(
        first_kernel,
        out_shape=(jax.ShapeDtypeStruct((6, 24, HALF), f32), jax.ShapeDtypeStruct((KEPT,) + TILE, bf16),
                   jax.ShapeDtypeStruct((8, 128), f32), jax.ShapeDtypeStruct((NEAR + 1, 8, WIDE), f32)),
        in_specs=[SMEM, VMEM, VMEM],
        out_specs=(VMEM, pl.BlockSpec(memory_space=pl.ANY), VMEM, VMEM),
        scratch_shapes=[
            pltpu.VMEM((NEAR + 1, 16, WIDE), f32),
            pltpu.VMEM((NEAR + 1, 16, WIDE), f32),
            pltpu.VMEM((DEEP,) + TILE, bf16),
            pltpu.SemaphoreType.DMA((DEEP,)),
        ]
        + [pltpu.VMEM((WIDE, 8), f32)] * 2
        + [side] * 6,
        compiler_params=pltpu.CompilerParams(vmem_limit_bytes=48 * 2**20),
        name="first_sweep",
    )(plan_list, values, spots)


def second_kernel(plan_ref, values, pos, kept, least, out, raw, acc, store, sem, *scratch):
    turned, sides, extra, nearest = scratch[0:2], (scratch[2:4], scratch[4:6]), scratch[6:8], scratch[8]
    work = worker(plan_ref, pos, nearest, turned, raw, acc, sides, extra)
    count = plan_ref[7, 0]
    pairs = (jnp.minimum(count, KEPT) + 1) // 2

    def in_copy(t):
        slot = lax.rem(t, DEEP)
        return pltpu.make_async_copy(kept.at[t], store.at[slot], sem.at[slot])

    for t in range(DEEP):
        @pl.when(t < 2 * pairs)
        def _():
            in_copy(t).start()

    nearest[...] = least[...]
    begin_sweep(values, raw, acc)
    work.drain(work.ready(0, 0))

    def body(n, selves):
        t = 2 * n
        for k in range(2):
            in_copy(t + k).wait()
        for k in range(2):
            p, c = work.tile_of(t + k)
            selves = selves + (p == c).astype(i32)
            work.drain(work.apply(t + k, k, store.at[lax.rem(t + k, DEEP)]), work.ready(t + k + 1, 1 - k))

        @pl.when(n + DEEP // 2 < pairs)
        def _():
            for k in range(2):
                in_copy(t + k + DEEP).start()
        return selves

    selves = lax.fori_loop(0, pairs, body, 0)

    @pl.when(count > KEPT)
    def _():
        def more(t, _):
            work.drain(work.turn_rows(t, turned[0]), work.ready(t, 0))
            work.drain(work.build(t, turned[0], store.at[0]))
            work.drain(work.apply(t, 0, store.at[0]))
            return 0

        lax.fori_loop(KEPT, count, more, 0)

    finish_sweep(work, plan_ref, nearest, selves, acc, out)


def second_sweep(plan_list, values, pos, kept, least):
    side = pltpu.VMEM((BLOCK, WIDE), bf16)
    return pl.pallas_call(
        second_kernel,
        out_shape=jax.ShapeDtypeStruct((6, 24, HALF), f32),
        in_specs=[SMEM, VMEM, VMEM, pl.BlockSpec(memory_space=pl.ANY), VMEM],
        out_specs=VMEM,
        scratch_shapes=[
            pltpu.VMEM((NEAR + 1, 16, WIDE), f32),
            pltpu.VMEM((NEAR + 1, 16, WIDE), f32),
            pltpu.VMEM((DEEP,) + TILE, bf16),
            pltpu.SemaphoreType.DMA((DEEP,)),
        ]
        + [pltpu.VMEM((WIDE, 8), f32)] * 2
        + [side] * 6
        + [pltpu.VMEM((8, 128), f32)],
        compiler_params=pltpu.CompilerParams(vmem_limit_bytes=48 * 2**20),
        name="second_sweep",
    )(plan_list, values, pos, kept, least)


def collect(slab, sub, parts, own, inbox, stage, send, recv):
    right, left = other(slab, sub + 1), other(slab, sub + 3)
    one, two, three = (lax.rem(sub + d, N_SUB) for d in range(1, 4))
    copies = []

    def half(what, at, lanes, to, n):
        copies.append(push(what, inbox.at[at, :, lanes], send.at[n], recv.at[2 * at + (lanes is LATE)], to))

    def wait_half(at, lanes):
        wait_for(inbox.at[at, :, lanes], recv.at[2 * at + (lanes is LATE)], (slab, sub))

    half(parts.at[two, :, EARLY], 0, EARLY, right, 0)
    half(parts.at[two, :, LATE], 1, LATE, left, 1)
    copies.append(push(parts.at[4], inbox.at[5], send.at[2], recv.at[10], other(slab - 1, sub)))
    copies.append(push(parts.at[5], inbox.at[4], send.at[3], recv.at[8], other(slab + 1, sub)))
    half(parts.at[one, :, LATE], 2, LATE, right, 4)
    half(parts.at[three, :, EARLY], 3, EARLY, left, 5)
    wait_half(0, EARLY)
    stage[0, :, :] = parts[one, :, EARLY] + inbox[0, :, EARLY]
    half(stage.at[0], 2, EARLY, right, 6)
    wait_half(1, LATE)
    stage[1, :, :] = parts[three, :, LATE] + inbox[1, :, LATE]
    half(stage.at[1], 3, LATE, left, 7)
    wait_for(inbox.at[4], recv.at[8], (slab, sub))
    wait_for(inbox.at[5], recv.at[10], (slab, sub))
    total = own[...] + parts[sub] + inbox[4] + inbox[5]
    for at in (2, 3):
        for lanes in (EARLY, LATE):
            wait_half(at, lanes)
    return copies, total + inbox[2] + inbox[3]


def greet_near(slab, sub, more=()):
    greet([other(slab, sub + d) for d in range(1, N_SUB)] + [other(slab + d, sub) for d in (1, -1)] + list(more))


def turn_kernel(parts, own, near, inbox, stage, total, send, recv, gsend, grecv):
    slab, sub = place()
    greet_near(slab, sub)
    copies, value = collect(slab, sub, parts, own, inbox, stage, send, recv)
    total[...] = value
    copies += spread(slab, sub, total, near, gsend, grecv)
    for copy in copies:
        copy.wait_send()


def turn(parts, own):
    return pl.pallas_call(
        turn_kernel,
        out_shape=jax.ShapeDtypeStruct((6, 24, HALF), f32),
        in_specs=[VMEM, VMEM],
        out_specs=VMEM,
        scratch_shapes=[pltpu.VMEM((6, 24, HALF), f32), pltpu.VMEM((2, 24, WIDTH), f32), pltpu.VMEM((24, HALF), f32)]
        + [pltpu.SemaphoreType.DMA((n,)) for n in (8, 12, 8, 12)],
        compiler_params=pltpu.CompilerParams(collective_id=1, has_side_effects=True, vmem_limit_bytes=40 * 2**20),
        name="turn_around",
    )(parts, own)


def squares(value):
    sq = value * value
    folded = sq[0:8] + sq[8:16] + sq[16:24]
    lanes = folded[:, 0:128]
    for n in range(1, HALF // 128):
        lanes = lanes + folded[:, 128 * n:128 * n + 128]
    return lanes


def finish_kernel(parts, first, out_first, out_second, inbox, stage, total_ref, box, send, recv, ssend, srecv):
    slab, sub = place()
    core = lax.rem(slab, 2)
    z = lax.rem(slab // 2, 4)
    y = slab // 8
    twin = slab + 1 - 2 * core
    groups = [[other(slab, sub + d) for d in range(1, 4)] + [other(twin, sub + d) for d in range(4)],
              [(y * 8 + lax.rem(z + d, 4) * 2 + core, sub) for d in range(1, 4)],
              [(lax.rem(y + d, 4) * 8 + z * 2 + core, sub) for d in range(1, 4)]]
    greet_near(slab, sub, groups[0][4:] + groups[1] + groups[2])
    copies, value = collect(slab, sub, parts, first, inbox, stage, send, recv)
    total_ref[...] = value
    box[0, 0, 0:8, :] = squares(first[...])
    box[0, 0, 8:16, :] = squares(value)
    for n, group in enumerate(groups):
        turns = []
        for m, peer in enumerate(group):
            turns.append(push(box.at[n, 0], box.at[n, m + 1], ssend.at[7 * n + m], srecv.at[7 * n + m], peer))
        for copy in turns:
            copy.wait_recv()
        copies += turns
        now = box[n, 0]
        for m in range(len(group)):
            now = now + box[n, m + 1]
        box[n + 1, 0, :, :] = now
    total = jnp.sum(box[3, 0], axis=1, keepdims=True)
    per = 1.0 / (3.0 * BLOCK * SPAN * N_SUB * N_SLAB)
    one, two = total[0:8], total[8:16]
    one = (one + pltpu.roll(jnp.broadcast_to(one, (8, 128)), 4, 0)) * per
    two = (two + pltpu.roll(jnp.broadcast_to(two, (8, 128)), 4, 0)) * per
    scale_one = lax.rsqrt(one + 1e-6)
    scale_two = scale_one * lax.rsqrt(scale_one * scale_one * two + 1e-6)
    for out, source, scale in ((out_first, first, scale_one), (out_second, total_ref, scale_two)):
        for a in range(3):
            value = source[8 * a:8 * a + 8, :] * scale[:, 0:1]
            for half in range(2):
                for k in range(4):
                    out[3 * k + a:3 * k + a + 1, half * HALF:half * HALF + HALF] = value[4 * half + k:4 * half + k + 1]
    for copy in copies:
        copy.wait_send()


def finish_all(parts, first):
    return pl.pallas_call(
        finish_kernel,
        out_shape=(jax.ShapeDtypeStruct((12, 2 * HALF), f32),) * 2,
        in_specs=[VMEM, VMEM],
        out_specs=(VMEM, VMEM),
        scratch_shapes=[pltpu.VMEM((6, 24, HALF), f32), pltpu.VMEM((2, 24, WIDTH), f32), pltpu.VMEM((24, HALF), f32),
                        pltpu.VMEM((4, 8, 16, 128), f32)]
        + [pltpu.SemaphoreType.DMA((n,)) for n in (8, 12, 21, 21)],
        compiler_params=pltpu.CompilerParams(collective_id=2, has_side_effects=True, vmem_limit_bytes=40 * 2**20),
        name="finish_all",
    )(parts, first)


def body(positions, forces, tile_rows, tile_cols, tile_count):
    _, sub = place()
    values, spots, own, table = gather(forces, positions, tile_rows[None], tile_cols[None], tile_count)
    plan_list = plan(table, spots)
    parts, kept, least, pos = first_sweep(plan_list, values, spots)
    near_second = turn(parts, own)
    parts = second_sweep(plan_list, near_second, pos, kept, least)
    first = lax.dynamic_index_in_dim(near_second, sub, 0, keepdims=False)
    return finish_all(parts, first)


def solution(mesh):
    placed = (
        P(None, ("slab", "sub")),
        P(None, ("slab", "sub")),
        P(("slab", "sub")),
        P(("slab", "sub")),
        P(("slab", "sub")),
    )
    return jax.shard_map(
        body,
        mesh=mesh,
        in_specs=placed,
        out_specs=(P(None, ("slab", "sub")), P(None, ("slab", "sub"))),
        check_vma=False,
    )
```

```python
import functools
import types

import jax
import jax.numpy as jnp
from jax import lax
from jax.experimental import pallas as pl
from jax.experimental.pallas import tpu as pltpu
from jax.sharding import PartitionSpec as P

f32, bf16, i32 = jnp.float32, jnp.bfloat16, jnp.int32
BLOCK = 192
WIDE = 256
CHUNK = 16
SPAN = 32
HALF = SPAN // 2 * BLOCK
NEAR = 6 * SPAN
N_SUB = 4
N_SLAB = 32
LIST = 6 * 128 + 128
MESH = pl.DeviceIdType.MESH
VMEM = pl.BlockSpec(memory_space=pltpu.VMEM)
SMEM = pl.BlockSpec(memory_space=pltpu.SMEM)


def place():
    return lax.axis_index("slab"), lax.axis_index("sub")


def other(slab, sub):
    return (lax.rem(slab + N_SLAB, N_SLAB), lax.rem(sub, N_SUB))


def push(src, dst, send, recv, to):
    copy = pltpu.make_async_remote_copy(
        src_ref=src, dst_ref=dst, send_sem=send, recv_sem=recv, device_id=to, device_id_type=MESH
    )
    copy.start()
    return copy


def hail(peers):
    for peer in peers:
        pl.semaphore_signal(pltpu.get_barrier_semaphore(), inc=1, device_id=peer, device_id_type=MESH)


def greet(peers):
    hail(peers)
    pl.semaphore_wait(pltpu.get_barrier_semaphore(), len(peers))


WIDTH = HALF // 2
EARLY, LATE = slice(0, WIDTH), slice(WIDTH, HALF)


def wait_for(ref, sem, me):
    pltpu.make_async_remote_copy(
        src_ref=ref, dst_ref=ref, send_sem=sem, recv_sem=sem, device_id=me, device_id_type=MESH
    ).wait_recv()


def spread(slab, sub, src, near, send, recv):
    right, left = other(slab, sub + 1), other(slab, sub + 3)
    one, two, three = (lax.rem(sub + d, N_SUB) for d in range(1, 4))
    copies = []

    def half(what, at, lanes, to, n):
        copies.append(push(what.at[:, lanes], near.at[at, :, lanes], send.at[n],
                           recv.at[2 * at + (lanes is LATE)], to))

    half(src, sub, EARLY, right, 0)
    half(src, sub, LATE, left, 1)
    copies.append(push(src, near.at[4], send.at[2], recv.at[8], other(slab + 1, sub)))
    copies.append(push(src, near.at[5], send.at[3], recv.at[10], other(slab - 1, sub)))
    half(src, sub, LATE, right, 4)
    half(src, sub, EARLY, left, 5)
    near[sub, :, :] = src[...]

    def wait_half(at, lanes):
        wait_for(near.at[at, :, lanes], recv.at[2 * at + (lanes is LATE)], (slab, sub))

    wait_half(three, EARLY)
    half(near.at[three], three, EARLY, right, 6)
    wait_half(one, LATE)
    half(near.at[one], one, LATE, left, 7)
    for at, lanes in ((three, LATE), (one, EARLY), (two, EARLY), (two, LATE)):
        wait_half(at, lanes)
    wait_for(near.at[4], recv.at[8], (slab, sub))
    wait_for(near.at[5], recv.at[10], (slab, sub))
    return copies


def gather_kernel(forces_far, positions_far, rows_far, cols_far, count, values, spots, own, table,
                  forces, positions, rows, cols, in_sem, near, x, mine, send, recv, tsend, trecv, wsend, wrecv):
    slab, sub = place()
    fetches = [pltpu.make_async_copy(src, dst, in_sem.at[n]) for n, (src, dst) in enumerate(
        ((forces_far, forces), (positions_far, positions), (rows_far, rows), (cols_far, cols)))]
    for fetch in fetches:
        fetch.start()
    peers = [other(slab, sub + d) for d in range(1, N_SUB)] + [other(slab + d, sub) for d in (1, -1, 2, -2)]
    hail(peers)
    x[30:32, :] = jnp.zeros((2, HALF), f32)
    for fetch in fetches:
        fetch.wait()
    col = (cols[...] - (slab - 1) * (N_SUB * SPAN)).astype(f32)
    live = jnp.where(lax.broadcasted_iota(i32, (1, 128), 1) < count[0], 1.0, 0.0)
    x[30:31, 0:128] = (rows[...] - (slab * N_SUB + sub) * SPAN).astype(f32)
    x[30:31, 128:256] = col
    x[30:31, 256:384] = live
    upper = jnp.sum(jnp.where(col >= 256.0, live, 0.0), axis=1, keepdims=True)
    lower = jnp.sum(jnp.where(col < 128.0, live, 0.0), axis=1, keepdims=True)
    whole = jnp.sum(live, axis=1, keepdims=True)
    row = lax.broadcasted_iota(i32, (8, 128), 0)
    mine[...] = jnp.where(row == 0, upper, jnp.where(row == 1, lower, jnp.where(row == 2, whole, 0.0)))
    for a in range(3):
        for half in range(2):
            lanes = slice(half * HALF, half * HALF + HALF)
            for k in range(4):
                x[a * 8 + half * 4 + k:a * 8 + half * 4 + k + 1, :] = forces[3 * k + a:3 * k + a + 1, lanes]
            x[24 + 2 * a + half:25 + 2 * a + half, :] = positions[a:a + 1, lanes]
    pl.semaphore_wait(pltpu.get_barrier_semaphore(), len(peers))
    at_own = pl.ds(pl.multiple_of(sub * 8, 8), 8)
    copies = [push(mine, table.at[2, at_own], tsend.at[d - 1], trecv.at[sub], other(slab, sub + d))
              for d in range(1, N_SUB)]
    table[2, at_own, :] = mine[...]
    for d in range(1, N_SUB):
        at = lax.rem(sub + d, N_SUB)
        wait_for(table.at[2, pl.ds(pl.multiple_of(at * 8, 8), 8)], trecv.at[at], (slab, sub))
    turns = [push(table.at[2], table.at[2 - d], wsend.at[n], wrecv.at[n], other(slab + d, sub))
             for n, d in enumerate((1, -1, 2, -2))]
    own[...] = x[0:24, :]
    copies += spread(slab, sub, x, near, send, recv)
    for n in range(6):
        values[n, :, :] = near[n, 0:24, :]
        spots[n, :, :] = near[n, 24:32, :]
    for copy in turns:
        copy.wait_recv()
    for copy in copies + turns:
        copy.wait_send()


def gather(forces, positions, rows, cols, count):
    return pl.pallas_call(
        gather_kernel,
        out_shape=(jax.ShapeDtypeStruct((6, 24, HALF), f32), jax.ShapeDtypeStruct((6, 8, HALF), f32),
                   jax.ShapeDtypeStruct((24, HALF), f32), jax.ShapeDtypeStruct((5, 32, 128), f32)),
        in_specs=[pl.BlockSpec(memory_space=pltpu.HBM)] * 4 + [SMEM],
        out_specs=(VMEM,) * 4,
        scratch_shapes=[pltpu.VMEM((12, 2 * HALF), f32), pltpu.VMEM((3, 2 * HALF), f32), pltpu.VMEM((1, 128), i32),
                        pltpu.VMEM((1, 128), i32), pltpu.SemaphoreType.DMA((4,)), pltpu.VMEM((6, 32, HALF), f32), pltpu.VMEM((32, HALF), f32), pltpu.VMEM((8, 128), f32)]
        + [pltpu.SemaphoreType.DMA((n,)) for n in (8, 12, 3, 4, 4, 4)],
        compiler_params=pltpu.CompilerParams(collective_id=0, has_side_effects=True, vmem_limit_bytes=40 * 2**20),
        name="gather_all",
    )(forces, positions, rows, cols, count)


def given(flow, counts):
    total = counts[0] + counts[1] + counts[2] + counts[3]
    whole = jnp.minimum(jnp.floor(jnp.maximum(flow, 0.0)), total)
    part = whole / jnp.maximum(total, 1.0)
    return [jnp.minimum(jnp.floor(part * n), n) for n in counts]


def plan_kernel(table, spots, out):
    slab, sub = place()
    lists = jnp.concatenate([spots[n, 6:7, 0:384] for n in range(6)] + [jnp.zeros((2, 384), f32)], axis=0)
    at = lambda rel, sub_at, kind: table[rel + 2, 8 * sub_at + kind:8 * sub_at + kind + 1, :]
    subs = range(N_SUB)
    total = {rel: sum(at(rel, v, 2) for v in subs) for rel in range(-2, 3)}
    first, last = slab == 0, slab == N_SLAB - 1

    def flow(a, b, c, d):
        return (a - d + 2.0 * (b - c)) * 0.2

    before = flow(jnp.where(slab == 1, total[-1], total[-2]), total[-1], total[0],
                  jnp.where(last, total[0], total[1]))
    after = flow(jnp.where(first, total[0], total[-1]), total[0], total[1],
                 jnp.where(slab == N_SLAB - 2, total[1], total[2]))
    before = jnp.where(first, 0.0, before)
    after = jnp.where(last, 0.0, after)
    ups = [at(0, v, 0) for v in subs]
    downs = [at(0, v, 1) for v in subs]
    up_given = given(after, ups)
    down_given = given(-before, downs)
    from_before = given(before, [at(-1, v, 0) for v in subs])
    from_after = given(-after, [at(1, v, 1) for v in subs])

    col = lists[:, 128:256]
    alive = lists[:, 256:384] > 0.5
    row_local = lists[:, :128]
    is_up = alive & (col >= 256.0)
    is_down = alive & (col < 128.0)
    is_own = alive & (col >= 128.0) & (col < 256.0)
    within = col - jnp.where(col >= 256.0, 256.0, jnp.where(col >= 128.0, 128.0, 0.0))
    col_sub = jnp.floor(within * (1.0 / SPAN))
    col_local = within - SPAN * col_sub
    masks = jnp.concatenate([m.astype(f32) for m in (is_up, is_down, is_own)], axis=0)
    lane_a = lax.broadcasted_iota(i32, (128, 128), 0)
    lane_b = lax.broadcasted_iota(i32, (128, 128), 1)
    ahead = (lane_a < lane_b).astype(bf16)
    rank = jnp.dot(masks.astype(bf16), ahead, preferred_element_type=f32)
    up_rank, down_rank, own_rank = rank[0:8], rank[8:16], rank[16:24]

    seat = lax.broadcasted_iota(i32, (8, 128), 0)

    def rows(values):
        full = jnp.zeros((8, 128), f32)
        for n, value in enumerate(values):
            full = jnp.where(seat == n, value, full)
        return full

    pick = lambda values: sum(jnp.where(sub == v, values[v], 0.0) for v in subs)
    up_limit = rows(up_given + [pick(from_before), jnp.zeros((1, 128), f32)])
    down_limit = rows(down_given + [jnp.zeros((1, 128), f32), pick(from_after)])
    up_sent = is_up & (up_rank < up_limit)
    down_sent = is_down & (down_rank < down_limit)
    in_slab = seat < 4
    crossing = in_slab & ((is_up & ~up_sent) | (is_down & ~down_sent))
    fixed = []
    for v in subs:
        kept = jnp.where(crossing & (col_sub == float(v)), 1.0, 0.0)
        fixed.append(jnp.sum(jnp.sum(kept, axis=0, keepdims=True), axis=1, keepdims=True)
                     + from_before[v] + from_after[v])
    own_counts = [at(0, v, 2) - ups[v] - downs[v] for v in subs]
    own_total = sum(own_counts)
    level = (sum(fixed) + own_total) * 0.25
    wish = [jnp.maximum(level - have, 0.0) for have in fixed]
    scale = own_total / jnp.maximum(sum(wish), 1.0)
    edges = [jnp.zeros((1, 128), f32)]
    run = jnp.zeros((1, 128), f32)
    for v in range(3):
        run = run + wish[v] * scale
        edges.append(jnp.minimum(jnp.floor(run + 0.5), own_total))
    edges.append(own_total)
    begin = pick(edges[:4])
    end = pick(edges[1:])
    start, offsets = jnp.zeros((1, 128), f32), []
    for v in subs:
        offsets.append(start)
        start = start + own_counts[v]
    place_own = own_rank + rows(offsets)
    mine = (crossing & (col_sub == sub.astype(f32))) | (
        in_slab & is_own & (place_own >= begin) & (place_own < end))
    mine = mine | ((seat == 4) & up_sent) | ((seat == 5) & down_sent)
    mine_value = mine.astype(f32)
    slot = jnp.dot(mine_value.astype(bf16), ahead, preferred_element_type=f32)
    counted = jnp.sum(mine_value, axis=1, keepdims=True)
    start, offsets = jnp.zeros((1, 1), f32), []
    for n in range(6):
        offsets.append(start)
        start = start + counted[n:n + 1]
    slot = slot + rows(offsets)
    slot = jnp.where(mine, slot, -1.0)
    row_near = row_local + SPAN * seat.astype(f32)
    inside = SPAN * col_sub + col_local
    col_near = jnp.where(in_slab, jnp.where(is_up, 160.0 + col_local, jnp.where(is_down, 128.0 + col_local, inside)),
                         inside)
    slot_t = jnp.transpose(slot, (1, 0))
    target = lax.broadcasted_iota(i32, (128, LIST), 1).astype(f32)
    result = jnp.zeros((16, LIST), f32)
    pad = jnp.zeros((14, 128), f32)
    for n in range(6):
        chosen = (slot_t[:, n:n + 1] == target).astype(bf16)
        values = jnp.concatenate([row_near[n:n + 1], col_near[n:n + 1], pad], axis=0).astype(bf16)
        result = result + jnp.dot(values, chosen, preferred_element_type=f32)
    lane_wide = lax.broadcasted_iota(i32, (1, LIST), 1).astype(f32)
    packed = jnp.where(lane_wide < start, result[0:1] * 256.0 + result[1:2], NEAR * 257.0)
    last_row = jnp.where(lane_b[0:1] == 0, start, 4.0 * slab.astype(f32) + 2.0)
    out[...] = jnp.concatenate([packed[:, 128 * n:128 * n + 128] for n in range(7)] + [last_row], axis=0).astype(i32)


def plan(table, spots):
    return pl.pallas_call(
        plan_kernel,
        out_shape=jax.ShapeDtypeStruct((8, 128), i32),
        in_specs=[VMEM, VMEM],
        out_specs=VMEM,
        compiler_params=pltpu.CompilerParams(vmem_limit_bytes=40 * 2**20),
        name="plan_tiles",
    )(table, spots)


UNIT = 0.5 ** 0.5
ISO = 0.25 * UNIT / (64.0 * UNIT**2) ** 2
DYAD = 3.0 * ISO


def mobility(xi, yi, zi, xj, yj, zj):
    dx, dy, dz = xi - xj, yi - yj, zi - zj
    q = jnp.maximum(dx * dx + dy * dy + dz * dz, 1e-12 * UNIT**2)
    inverse = lax.rsqrt(q)
    taper = jnp.maximum(64.0 * UNIT**2 - q, 0.0)
    weight = taper * taper
    square = inverse * inverse
    near = 4.0 / UNIT - 9.0 / 8.0 / UNIT**2 * (q * inverse)
    far = inverse * (3.0 + square)
    iso = weight * jnp.where(q < 4.0 * UNIT**2, near, far)
    capped = jnp.minimum(square, 0.5)
    dyad = weight * (capped * (1.0 - capped))
    return iso, dyad, (dx, dy, dz), inverse, q


CLOSE = 1.0 / (2e-3 * UNIT)


def two_parts(value):
    high = value.astype(bf16)
    return high, (value - high.astype(f32)).astype(bf16)


def block_store(ref, block, r, j, value, lane):
    if j == 0:
        ref[block, r:r + 8, 0:128] = value
    elif j == 2:
        ref[block + 1, r:r + 8, 0:128] = value
    else:
        swapped = pltpu.roll(value, 64, 1)
        ref[block, r:r + 8, 128:256] = jnp.where(lane < 64, value, swapped)
        ref[block + 1, r:r + 8, 128:256] = jnp.where(lane < 64, swapped, value)


def unpack_spots(spots, pos, centre):
    row = lax.broadcasted_iota(i32, (8, 128), 0)
    lane = lax.broadcasted_iota(i32, (8, 128), 1)
    middle = jnp.where(row < 2, centre, 3.0)
    pos[NEAR, :, :] = jnp.zeros((8, WIDE), f32)

    def pair_body(pair, _):
        start = pl.multiple_of(pair * 2 * BLOCK, 128)
        for at in range(6):
            for j in range(3):
                spot = (spots[at, :, pl.ds(start + 128 * j, 128)] - middle) * UNIT
                for half in range(2):
                    block = at * SPAN + half * 16 + pair * 2
                    block_store(pos, block, 0, j, spot if half == 0 else pltpu.roll(spot, 7, 0), lane)
        return 0

    lax.fori_loop(0, 8, pair_body, 0)


def unpack_values(sources, raw):
    row = lax.broadcasted_iota(i32, (8, 128), 0)
    lane = lax.broadcasted_iota(i32, (8, 128), 1)
    raw[NEAR, :, :] = jnp.zeros((16, WIDE), f32)

    def pair_body(pair, _):
        start = pl.multiple_of(pair * 2 * BLOCK, 128)
        for view, at in sources:
            for j in range(3):
                x, y, z = (view[8 * a:8 * a + 8, pl.ds(start + 128 * j, 128)] for a in range(3))
                for half in range(2):
                    if half == 0:
                        first, second = jnp.where(row < 4, x, pltpu.roll(y, 4, 0)), z
                    else:
                        first, second = jnp.where(row < 4, pltpu.roll(x, 4, 0), y), pltpu.roll(z, 4, 0)
                    block = at * SPAN + half * 16 + pair * 2
                    block_store(raw, block, 0, j, first, lane)
                    block_store(raw, block, 8, j, second, lane)
        return 0

    lax.fori_loop(0, 8, pair_body, 0)


def repack(acc, out):
    row = lax.broadcasted_iota(i32, (8, 128), 0)
    lane = lax.broadcasted_iota(i32, (8, 128), 1)

    def pair_body(pair, _):
        start = pl.multiple_of(pair * 2 * BLOCK, 128)
        for at in range(6):
            for j in range(3):
                got = []
                for half in range(2):
                    block = at * SPAN + half * 16 + pair * 2
                    for r in (0, 8):
                        if j == 0:
                            got.append(acc[block, r:r + 8, 0:128])
                        elif j == 2:
                            got.append(acc[block + 1, r:r + 8, 0:128])
                        else:
                            even, odd = acc[block, r:r + 8, 128:256], acc[block + 1, r:r + 8, 128:256]
                            got.append(jnp.where(lane < 64, even, odd)
                                       + pltpu.roll(jnp.where(lane < 64, odd, even), 64, 1))
                a0, a1, b0, b1 = got
                lanes = pl.ds(start + 128 * j, 128)
                out[at, 0:8, lanes] = jnp.where(row < 4, a0, pltpu.roll(b0, 4, 0))
                out[at, 8:16, lanes] = jnp.where(row < 4, pltpu.roll(a0, 4, 0), b0)
                out[at, 16:24, lanes] = jnp.where(row < 4, a1, pltpu.roll(b1, 4, 0))
        return 0

    lax.fori_loop(0, 8, pair_body, 0)


def worker(plan_ref, pos, nearest, turned, raw=None, acc=None, sides=None, extra=None):
    row = lax.broadcasted_iota(i32, (8, WIDE), 0)
    across = (((1,), (1,)), ((), ()))

    def tile_of(t):
        packed = plan_ref[t // 128, t % 128]
        return packed // 256, packed % 256

    def build(t, turn_ref, matrices):
        p, c = tile_of(t)
        xj, yj, zj = (pos[c, n:n + 1, :] for n in (0, 2, 4))
        least = jnp.full((8, 128), 64.0, f32)
        side = lax.broadcasted_iota(i32, (CHUNK, 128), 1) < BLOCK - 128
        main, rest = slice(0, 128), slice(128, WIDE)

        for u in range(0, BLOCK // 2, CHUNK):
            w = u + BLOCK // 2
            there = [[jnp.broadcast_to(turn_ref[v:v + CHUNK, n:n + 1], (CHUNK, 128)) for n in (0, 2, 4)]
                     for v in (u, w)]
            there.append([jnp.where(side, one, two) for one, two in zip(*there)])
            for r, at, lanes in zip((u, w, u + BLOCK), there, (main, main, rest)):
                iso, dyad, _, inverse, q = mobility(*at, xj[:, lanes], yj[:, lanes], zj[:, lanes])
                for m, value in enumerate((iso, dyad * jnp.minimum(inverse, CLOSE))):
                    high, low = two_parts(value)
                    matrices[2 * m, r:r + CHUNK, :] = high
                    matrices[2 * m + 1, r:r + CHUNK, :] = low
                least = jnp.minimum(least, jnp.minimum(q[:8], q[8:]))
                yield
        nearest[...] = jnp.minimum(nearest[...], jnp.where(p == c, 64.0, least))

    def patterns(block):
        x, y, z = (pos[block, n:n + 1, :] for n in (0, 2, 4))
        return x, y, z, jnp.where(row < 4, x, y)

    def columns(block):
        x, y, z, both = patterns(block)
        first, second = raw[block, 0:8, :], raw[block, 8:16, :]
        t = first * both
        s = t + pltpu.roll(t, 4, 0) + pltpu.roll(second * z, 4, 0)
        second = jnp.where(row < 4, second, s)
        full = jnp.concatenate([first, second] + [part * scale for scale in (x, y, z) for part in (first, second)], axis=0)
        high = full.astype(bf16)
        rest = full - high.astype(f32)
        middle, low = two_parts(rest)
        return high, middle, low

    def finish(iso, dyad, block):
        x, y, z, both = patterns(block)
        last = jnp.where(row < 4, z, -1.0)

        def folded(r):
            t = dyad[r:r + 8] * both + dyad[r + 8:r + 16] * last
            return t + pltpu.roll(t, 4, 0)

        along = folded(0)
        upper = both * along - jnp.where(row < 4, folded(16), folded(32))
        under = z * along - folded(48)
        return ISO * iso[0:8] + DYAD * upper, ISO * iso[8:16] + DYAD * under

    def ready(t, slot):
        for side, block in zip(sides[slot], reversed(tile_of(t))):
            for n, part in enumerate(columns(block)):
                side[64 * n:64 * n + 64, :] = part
                yield

    def turn_rows(t, turn_ref):
        turn_ref[...] = jnp.transpose(pos[tile_of(t)[0]], (1, 0))
        yield

    def summed(by_high, by_low):
        return (by_high[0:64] + by_low[0:64]) + (by_high[64:128] + by_low[64:128]) + by_high[128:192]

    def apply(t, slot, matrices):
        p, c = tile_of(t)
        side = lax.broadcasted_iota(i32, (1, 128), 1) < BLOCK - 128
        none = jnp.zeros((BLOCK // 2, 128), bf16)

        def whole(m):
            rest = matrices[m, BLOCK:, :]
            rest = jnp.concatenate([jnp.where(side, rest, none), jnp.where(side, none, rest)], axis=0)
            return jnp.concatenate([matrices[m, 0:BLOCK, :], rest], axis=1)

        iso_high, iso_low, dyad_high, dyad_low = (whole(m) for m in range(4))
        dot = lambda a, b: jnp.dot(a, b, preferred_element_type=f32)
        dot_across = lambda a, b: lax.dot_general(a, b, across, preferred_element_type=f32)
        wide = sides[slot][0][...]
        slim = jnp.concatenate([wide[n:n + 16] for n in (0, 64)], axis=0)
        pad = jnp.zeros((64, WIDE - BLOCK), f32)
        dyad = dot_across(wide, dyad_high)
        yield
        dyad = summed(dyad, dot_across(wide[:128], dyad_low))
        yield
        iso = dot_across(slim, iso_high) + dot_across(slim, iso_low)
        yield
        upper, under = finish(jnp.concatenate([iso[:16] + iso[16:], pad[:16]], axis=1), jnp.concatenate([dyad, pad], axis=1), p)
        acc[p, 0:8, :] += upper
        acc[p, 8:16, :] += under
        yield
        wide = sides[slot][1][:, :BLOCK]
        slim = jnp.concatenate([wide[n:n + 16] for n in (0, 64)], axis=0)
        dyad = dot(wide, dyad_high)
        yield
        dyad = summed(dyad, dot(wide[:128], dyad_low))
        yield
        iso = dot(slim, iso_high) + dot(slim, iso_low)
        yield
        upper, under = finish(iso[:16] + iso[16:], dyad, c)
        acc[c, 0:8, :] += upper
        acc[c, 8:16, :] += under
        yield

    def any_close(t):
        p, c = tile_of(t)
        turned[0][...] = jnp.transpose(pos[p], (1, 0))
        xj, yj, zj = (pos[c, n:n + 1, :] for n in (0, 2, 4))
        least = jnp.full((8, WIDE), 64.0, f32)
        for r in range(0, BLOCK, 8):
            xi, yi, zi = (turned[0][r:r + 8, m:m + 1] for m in (0, 2, 4))
            dx, dy, dz = xi - xj, yi - yj, zi - zj
            apart = dx * dx + dy * dy + dz * dz
            least = jnp.minimum(least, jnp.where(apart > 0.0, apart, 64.0))
        return jnp.min(least) < 1.01 / CLOSE**2

    def close_pairs(t):
        p, c = tile_of(t)
        turned[0][...] = jnp.transpose(pos[p], (1, 0))
        single = lax.broadcasted_iota(i32, (1, WIDE), 1) < BLOCK
        xj, yj, zj = (pos[c, n:n + 1, :] for n in (0, 2, 4))
        col_parts, row_parts = columns(c), columns(p)
        col_vec = jnp.concatenate([col_parts[0][:16], col_parts[1][:16]], axis=0)
        row_vec = jnp.concatenate([row_parts[0][:16], row_parts[1][:16]], axis=0)[:, :BLOCK]

        col_vec = jnp.where(single, col_vec, jnp.zeros_like(col_vec))

        def one(n, _):
            for r in range(0, BLOCK, CHUNK):
                xi, yi, zi = (turned[0][r:r + CHUNK, m:m + 1] for m in (0, 2, 4))
                _, dyad, offset, inverse, _ = mobility(xi, yi, zi, xj, yj, zj)
                rest = dyad * jnp.maximum(inverse - CLOSE, 0.0)
                along = jnp.where(n == 0, offset[0], jnp.where(n == 1, offset[1], offset[2]))
                high, low = two_parts(rest * along)
                extra[0][r:r + CHUNK, :] = high
                extra[1][r:r + CHUNK, :] = low
            h, l = extra[0][...], extra[1][...]
            to_row = (lax.dot_general(col_vec, h, across, preferred_element_type=f32)
                      + lax.dot_general(col_vec, l, across, preferred_element_type=f32))
            to_row = jnp.concatenate([to_row, jnp.zeros((32, WIDE - BLOCK), f32)], axis=1)
            to_col = (jnp.dot(row_vec, h, preferred_element_type=f32)
                      + jnp.dot(row_vec, l, preferred_element_type=f32))
            for block, got, sign in ((p, to_row, 1.0), (c, to_col, -1.0)):
                x, y, z, both = patterns(block)
                last = jnp.where(row < 4, z, -1.0)
                got = got[:16] + got[16:]
                folded = got[:8] * both + got[8:] * last
                folded = sign * DYAD * (folded + pltpu.roll(folded, 4, 0)) * single
                acc[block, 0:8, :] += jnp.where(row // 4 == n, folded, 0.0)
                acc[block, 8:16, :] += jnp.where(row // 4 + 2 == n, folded, 0.0)
            return 0

        lax.fori_loop(0, 3, one, 0)

    def drain(*steps):
        steps = list(steps)
        while steps:
            for step in list(steps):
                if next(step, steps) is steps:
                    steps.remove(step)

    return types.SimpleNamespace(tile_of=tile_of, build=build, ready=ready, turn_rows=turn_rows, apply=apply,
                                 close_pairs=close_pairs, any_close=any_close, drain=drain)


KEPT = 128
DEEP = 8


def finish_sweep(work, plan_ref, nearest, selves, acc, out):
    count = plan_ref[7, 0]
    found = jnp.min(nearest[...]) < 1.01 / CLOSE**2

    def look(t, _):
        p, c = work.tile_of(t)

        @pl.when(found | (p == c))
        def _():
            @pl.when(found | work.any_close(t))
            def _():
                work.close_pairs(t)
        return 0

    lax.fori_loop(0, jnp.where(found | (selves > 0) | (count > KEPT), count, 0), look, 0)
    repack(acc, out)


def begin_sweep(values, raw, acc):
    unpack_values([(values.at[n], n) for n in range(6)], raw)
    acc[...] = jnp.zeros_like(acc)


def first_kernel(plan_ref, values, spots, out, kept, nearest, pos, raw, acc, store, sem, *scratch):
    turned, sides, extra = scratch[0:2], (scratch[2:4], scratch[4:6]), scratch[6:8]
    work = worker(plan_ref, pos, nearest, turned, raw, acc, sides, extra)
    nearest[...] = jnp.full((8, 128), 64.0, f32)
    begin_sweep(values, raw, acc)
    unpack_spots(spots, pos, plan_ref[7, 1].astype(f32))
    count = plan_ref[7, 0]
    pairs = (count + 1) // 2

    def out_copy(t):
        slot = lax.rem(t, DEEP)
        return pltpu.make_async_copy(store.at[slot], kept.at[t], sem.at[slot])

    def wait_out(t):
        @pl.when((t >= 0) & (t < KEPT))
        def _():
            out_copy(t).wait()

    work.drain(work.turn_rows(0, turned[0]), work.turn_rows(1, turned[1]))
    work.drain(work.build(0, turned[0], store.at[0]), work.ready(0, 0))
    out_copy(0).start()

    def body(n, selves):
        t = 2 * n
        for k in range(2):
            wait_out(t + 1 + k - DEEP)
        for k in range(2):
            p, c = work.tile_of(t + k)
            selves = selves + (p == c).astype(i32)
            work.drain(work.apply(t + k, k, store.at[lax.rem(t + k, DEEP)]),
                       work.build(t + k + 1, turned[1 - k], store.at[lax.rem(t + k + 1, DEEP)]),
                       work.turn_rows(t + k + 2, turned[k]), work.ready(t + k + 1, 1 - k))
        for k in range(2):
            @pl.when(t + 1 + k < KEPT)
            def _():
                out_copy(t + 1 + k).start()
        return selves

    selves = lax.fori_loop(0, pairs, body, 0)
    finish_sweep(work, plan_ref, nearest, selves, acc, out)
    for k in range(DEEP):
        wait_out(2 * pairs + 1 - DEEP + k)


TILE = (4, BLOCK + BLOCK // 2, 128)


def first_sweep(plan_list, values, spots):
    side = pltpu.VMEM((BLOCK, WIDE), bf16)
    return pl.pallas_call(
        first_kernel,
        out_shape=(jax.ShapeDtypeStruct((6, 24, HALF), f32), jax.ShapeDtypeStruct((KEPT,) + TILE, bf16),
                   jax.ShapeDtypeStruct((8, 128), f32), jax.ShapeDtypeStruct((NEAR + 1, 8, WIDE), f32)),
        in_specs=[SMEM, VMEM, VMEM],
        out_specs=(VMEM, pl.BlockSpec(memory_space=pl.ANY), VMEM, VMEM),
        scratch_shapes=[
            pltpu.VMEM((NEAR + 1, 16, WIDE), f32),
            pltpu.VMEM((NEAR + 1, 16, WIDE), f32),
            pltpu.VMEM((DEEP,) + TILE, bf16),
            pltpu.SemaphoreType.DMA((DEEP,)),
        ]
        + [pltpu.VMEM((WIDE, 8), f32)] * 2
        + [side] * 6,
        compiler_params=pltpu.CompilerParams(vmem_limit_bytes=48 * 2**20),
        name="first_sweep",
    )(plan_list, values, spots)


def second_kernel(plan_ref, values, pos, kept, least, out, raw, acc, store, sem, *scratch):
    turned, sides, extra, nearest = scratch[0:2], (scratch[2:4], scratch[4:6]), scratch[6:8], scratch[8]
    work = worker(plan_ref, pos, nearest, turned, raw, acc, sides, extra)
    count = plan_ref[7, 0]
    pairs = (jnp.minimum(count, KEPT) + 1) // 2

    def in_copy(t):
        slot = lax.rem(t, DEEP)
        return pltpu.make_async_copy(kept.at[t], store.at[slot], sem.at[slot])

    for t in range(DEEP):
        @pl.when(t < 2 * pairs)
        def _():
            in_copy(t).start()

    nearest[...] = least[...]
    begin_sweep(values, raw, acc)
    work.drain(work.ready(0, 0))

    def body(n, selves):
        t = 2 * n
        for k in range(2):
            in_copy(t + k).wait()
        for k in range(2):
            p, c = work.tile_of(t + k)
            selves = selves + (p == c).astype(i32)
            work.drain(work.apply(t + k, k, store.at[lax.rem(t + k, DEEP)]), work.ready(t + k + 1, 1 - k))

        @pl.when(n + DEEP // 2 < pairs)
        def _():
            for k in range(2):
                in_copy(t + k + DEEP).start()
        return selves

    selves = lax.fori_loop(0, pairs, body, 0)

    @pl.when(count > KEPT)
    def _():
        def more(t, _):
            work.drain(work.turn_rows(t, turned[0]), work.ready(t, 0))
            work.drain(work.build(t, turned[0], store.at[0]))
            work.drain(work.apply(t, 0, store.at[0]))
            return 0

        lax.fori_loop(KEPT, count, more, 0)

    finish_sweep(work, plan_ref, nearest, selves, acc, out)


def second_sweep(plan_list, values, pos, kept, least):
    side = pltpu.VMEM((BLOCK, WIDE), bf16)
    return pl.pallas_call(
        second_kernel,
        out_shape=jax.ShapeDtypeStruct((6, 24, HALF), f32),
        in_specs=[SMEM, VMEM, VMEM, pl.BlockSpec(memory_space=pl.ANY), VMEM],
        out_specs=VMEM,
        scratch_shapes=[
            pltpu.VMEM((NEAR + 1, 16, WIDE), f32),
            pltpu.VMEM((NEAR + 1, 16, WIDE), f32),
            pltpu.VMEM((DEEP,) + TILE, bf16),
            pltpu.SemaphoreType.DMA((DEEP,)),
        ]
        + [pltpu.VMEM((WIDE, 8), f32)] * 2
        + [side] * 6
        + [pltpu.VMEM((8, 128), f32)],
        compiler_params=pltpu.CompilerParams(vmem_limit_bytes=48 * 2**20),
        name="second_sweep",
    )(plan_list, values, pos, kept, least)


def collect(slab, sub, parts, own, inbox, stage, send, recv):
    right, left = other(slab, sub + 1), other(slab, sub + 3)
    one, two, three = (lax.rem(sub + d, N_SUB) for d in range(1, 4))
    copies = []

    def half(what, at, lanes, to, n):
        copies.append(push(what, inbox.at[at, :, lanes], send.at[n], recv.at[2 * at + (lanes is LATE)], to))

    def wait_half(at, lanes):
        wait_for(inbox.at[at, :, lanes], recv.at[2 * at + (lanes is LATE)], (slab, sub))

    half(parts.at[two, :, EARLY], 0, EARLY, right, 0)
    half(parts.at[two, :, LATE], 1, LATE, left, 1)
    copies.append(push(parts.at[4], inbox.at[5], send.at[2], recv.at[10], other(slab - 1, sub)))
    copies.append(push(parts.at[5], inbox.at[4], send.at[3], recv.at[8], other(slab + 1, sub)))
    half(parts.at[one, :, LATE], 2, LATE, right, 4)
    half(parts.at[three, :, EARLY], 3, EARLY, left, 5)
    wait_half(0, EARLY)
    stage[0, :, :] = parts[one, :, EARLY] + inbox[0, :, EARLY]
    half(stage.at[0], 2, EARLY, right, 6)
    wait_half(1, LATE)
    stage[1, :, :] = parts[three, :, LATE] + inbox[1, :, LATE]
    half(stage.at[1], 3, LATE, left, 7)
    wait_for(inbox.at[4], recv.at[8], (slab, sub))
    wait_for(inbox.at[5], recv.at[10], (slab, sub))
    total = own[...] + parts[sub] + inbox[4] + inbox[5]
    for at in (2, 3):
        for lanes in (EARLY, LATE):
            wait_half(at, lanes)
    return copies, total + inbox[2] + inbox[3]


def greet_near(slab, sub, more=()):
    greet([other(slab, sub + d) for d in range(1, N_SUB)] + [other(slab + d, sub) for d in (1, -1)] + list(more))


def turn_kernel(parts, own, near, inbox, stage, total, send, recv, gsend, grecv):
    slab, sub = place()
    greet_near(slab, sub)
    copies, value = collect(slab, sub, parts, own, inbox, stage, send, recv)
    total[...] = value
    copies += spread(slab, sub, total, near, gsend, grecv)
    for copy in copies:
        copy.wait_send()


def turn(parts, own):
    return pl.pallas_call(
        turn_kernel,
        out_shape=jax.ShapeDtypeStruct((6, 24, HALF), f32),
        in_specs=[VMEM, VMEM],
        out_specs=VMEM,
        scratch_shapes=[pltpu.VMEM((6, 24, HALF), f32), pltpu.VMEM((2, 24, WIDTH), f32), pltpu.VMEM((24, HALF), f32)]
        + [pltpu.SemaphoreType.DMA((n,)) for n in (8, 12, 8, 12)],
        compiler_params=pltpu.CompilerParams(collective_id=1, has_side_effects=True, vmem_limit_bytes=40 * 2**20),
        name="turn_around",
    )(parts, own)


def squares(value):
    sq = value * value
    folded = sq[0:8] + sq[8:16] + sq[16:24]
    lanes = folded[:, 0:128]
    for n in range(1, HALF // 128):
        lanes = lanes + folded[:, 128 * n:128 * n + 128]
    return lanes


def finish_kernel(parts, first, out_first, out_second, inbox, stage, total_ref, box, send, recv, ssend, srecv):
    slab, sub = place()
    core = lax.rem(slab, 2)
    z = lax.rem(slab // 2, 4)
    y = slab // 8
    twin = slab + 1 - 2 * core
    groups = [[other(slab, sub + d) for d in range(1, 4)] + [other(twin, sub + d) for d in range(4)],
              [(y * 8 + lax.rem(z + d, 4) * 2 + core, sub) for d in range(1, 4)],
              [(lax.rem(y + d, 4) * 8 + z * 2 + core, sub) for d in range(1, 4)]]
    greet_near(slab, sub, groups[0][4:] + groups[1] + groups[2])
    copies, value = collect(slab, sub, parts, first, inbox, stage, send, recv)
    total_ref[...] = value
    box[0, 0, 0:8, :] = squares(first[...])
    box[0, 0, 8:16, :] = squares(value)
    for n, group in enumerate(groups):
        turns = []
        for m, peer in enumerate(group):
            turns.append(push(box.at[n, 0], box.at[n, m + 1], ssend.at[7 * n + m], srecv.at[7 * n + m], peer))
        for copy in turns:
            copy.wait_recv()
        copies += turns
        now = box[n, 0]
        for m in range(len(group)):
            now = now + box[n, m + 1]
        box[n + 1, 0, :, :] = now
    total = jnp.sum(box[3, 0], axis=1, keepdims=True)
    per = 1.0 / (3.0 * BLOCK * SPAN * N_SUB * N_SLAB)
    one, two = total[0:8], total[8:16]
    one = (one + pltpu.roll(jnp.broadcast_to(one, (8, 128)), 4, 0)) * per
    two = (two + pltpu.roll(jnp.broadcast_to(two, (8, 128)), 4, 0)) * per
    scale_one = lax.rsqrt(one + 1e-6)
    scale_two = scale_one * lax.rsqrt(scale_one * scale_one * two + 1e-6)
    for out, source, scale in ((out_first, first, scale_one), (out_second, total_ref, scale_two)):
        for a in range(3):
            value = source[8 * a:8 * a + 8, :] * scale[:, 0:1]
            for half in range(2):
                for k in range(4):
                    out[3 * k + a:3 * k + a + 1, half * HALF:half * HALF + HALF] = value[4 * half + k:4 * half + k + 1]
    for copy in copies:
        copy.wait_send()


def finish_all(parts, first):
    return pl.pallas_call(
        finish_kernel,
        out_shape=(jax.ShapeDtypeStruct((12, 2 * HALF), f32),) * 2,
        in_specs=[VMEM, VMEM],
        out_specs=(VMEM, VMEM),
        scratch_shapes=[pltpu.VMEM((6, 24, HALF), f32), pltpu.VMEM((2, 24, WIDTH), f32), pltpu.VMEM((24, HALF), f32),
                        pltpu.VMEM((4, 8, 16, 128), f32)]
        + [pltpu.SemaphoreType.DMA((n,)) for n in (8, 12, 21, 21)],
        compiler_params=pltpu.CompilerParams(collective_id=2, has_side_effects=True, vmem_limit_bytes=40 * 2**20),
        name="finish_all",
    )(parts, first)


def body(positions, forces, tile_rows, tile_cols, tile_count):
    _, sub = place()
    far = [pltpu.with_memory_space_constraint(v, pltpu.HBM)
           for v in (forces, positions, tile_rows[None], tile_cols[None])]
    values, spots, own, table = gather(*far, tile_count)
    plan_list = plan(table, spots)
    parts, kept, least, pos = first_sweep(plan_list, values, spots)
    near_second = turn(parts, own)
    parts = second_sweep(plan_list, near_second, pos, kept, least)
    first = lax.dynamic_index_in_dim(near_second, sub, 0, keepdims=False)
    return finish_all(parts, first)


def solution(mesh):
    placed = (
        P(None, ("slab", "sub")),
        P(None, ("slab", "sub")),
        P(("slab", "sub")),
        P(("slab", "sub")),
        P(("slab", "sub")),
    )
    return jax.shard_map(
        body,
        mesh=mesh,
        in_specs=placed,
        out_specs=(P(None, ("slab", "sub")), P(None, ("slab", "sub"))),
        check_vma=False,
    )
```

```python
import functools
import types

import jax
import jax.numpy as jnp
from jax import lax
from jax.experimental import pallas as pl
from jax.experimental.pallas import tpu as pltpu
from jax.sharding import PartitionSpec as P

f32, bf16, i32 = jnp.float32, jnp.bfloat16, jnp.int32
BLOCK = 192
WIDE = 256
CHUNK = 16
SPAN = 32
HALF = SPAN // 2 * BLOCK
NEAR = 6 * SPAN
N_SUB = 4
N_SLAB = 32
LIST = 6 * 128 + 128
MESH = pl.DeviceIdType.MESH
VMEM = pl.BlockSpec(memory_space=pltpu.VMEM)
SMEM = pl.BlockSpec(memory_space=pltpu.SMEM)


def place():
    return lax.axis_index("slab"), lax.axis_index("sub")


def other(slab, sub):
    return (lax.rem(slab + N_SLAB, N_SLAB), lax.rem(sub, N_SUB))


def push(src, dst, send, recv, to):
    copy = pltpu.make_async_remote_copy(
        src_ref=src, dst_ref=dst, send_sem=send, recv_sem=recv, device_id=to, device_id_type=MESH
    )
    copy.start()
    return copy


def hail(peers):
    for peer in peers:
        pl.semaphore_signal(pltpu.get_barrier_semaphore(), inc=1, device_id=peer, device_id_type=MESH)


def greet(peers):
    hail(peers)
    pl.semaphore_wait(pltpu.get_barrier_semaphore(), len(peers))


WIDTH = HALF // 2
EARLY, LATE = slice(0, WIDTH), slice(WIDTH, HALF)


def wait_for(ref, sem, me):
    pltpu.make_async_remote_copy(
        src_ref=ref, dst_ref=ref, send_sem=sem, recv_sem=sem, device_id=me, device_id_type=MESH
    ).wait_recv()


def spread(slab, sub, src, near, send, recv):
    right, left = other(slab, sub + 1), other(slab, sub + 3)
    one, two, three = (lax.rem(sub + d, N_SUB) for d in range(1, 4))
    copies = []

    def half(what, at, lanes, to, n):
        copies.append(push(what.at[:, lanes], near.at[at, :, lanes], send.at[n],
                           recv.at[2 * at + (lanes is LATE)], to))

    half(src, sub, EARLY, right, 0)
    half(src, sub, LATE, left, 1)
    copies.append(push(src, near.at[4], send.at[2], recv.at[8], other(slab + 1, sub)))
    copies.append(push(src, near.at[5], send.at[3], recv.at[10], other(slab - 1, sub)))
    half(src, sub, LATE, right, 4)
    half(src, sub, EARLY, left, 5)
    near[sub, :, :] = src[...]

    def wait_half(at, lanes):
        wait_for(near.at[at, :, lanes], recv.at[2 * at + (lanes is LATE)], (slab, sub))

    wait_half(three, EARLY)
    half(near.at[three], three, EARLY, right, 6)
    wait_half(one, LATE)
    half(near.at[one], one, LATE, left, 7)
    for at, lanes in ((three, LATE), (one, EARLY), (two, EARLY), (two, LATE)):
        wait_half(at, lanes)
    wait_for(near.at[4], recv.at[8], (slab, sub))
    wait_for(near.at[5], recv.at[10], (slab, sub))
    return copies


def gather_kernel(forces_far, positions_far, rows_far, cols_far, count, values, spots, own, table,
                  forces, positions, rows, cols, in_sem, near, x, mine, send, recv, tsend, trecv, wsend, wrecv):
    slab, sub = place()
    fetches = [pltpu.make_async_copy(src, dst, in_sem.at[n]) for n, (src, dst) in enumerate(
        ((forces_far, forces), (positions_far, positions), (rows_far, rows), (cols_far, cols)))]
    for fetch in fetches:
        fetch.start()
    peers = [other(slab, sub + d) for d in range(1, N_SUB)] + [other(slab + d, sub) for d in (1, -1, 2, -2)]
    hail(peers)
    x[30:32, :] = jnp.zeros((2, HALF), f32)
    for fetch in fetches:
        fetch.wait()
    col = (cols[...] - (slab - 1) * (N_SUB * SPAN)).astype(f32)
    live = jnp.where(lax.broadcasted_iota(i32, (1, 128), 1) < count[0], 1.0, 0.0)
    x[30:31, 0:128] = (rows[...] - (slab * N_SUB + sub) * SPAN).astype(f32)
    x[30:31, 128:256] = col
    x[30:31, 256:384] = live
    upper = jnp.sum(jnp.where(col >= 256.0, live, 0.0), axis=1, keepdims=True)
    lower = jnp.sum(jnp.where(col < 128.0, live, 0.0), axis=1, keepdims=True)
    whole = jnp.sum(live, axis=1, keepdims=True)
    row = lax.broadcasted_iota(i32, (8, 128), 0)
    mine[...] = jnp.where(row == 0, upper, jnp.where(row == 1, lower, jnp.where(row == 2, whole, 0.0)))
    for a in range(3):
        for half in range(2):
            lanes = slice(half * HALF, half * HALF + HALF)
            for k in range(4):
                x[a * 8 + half * 4 + k:a * 8 + half * 4 + k + 1, :] = forces[3 * k + a:3 * k + a + 1, lanes]
            x[24 + 2 * a + half:25 + 2 * a + half, :] = positions[a:a + 1, lanes]
    pl.semaphore_wait(pltpu.get_barrier_semaphore(), len(peers))
    at_own = pl.ds(pl.multiple_of(sub * 8, 8), 8)
    copies = [push(mine, table.at[2, at_own], tsend.at[d - 1], trecv.at[sub], other(slab, sub + d))
              for d in range(1, N_SUB)]
    table[2, at_own, :] = mine[...]
    for d in range(1, N_SUB):
        at = lax.rem(sub + d, N_SUB)
        wait_for(table.at[2, pl.ds(pl.multiple_of(at * 8, 8), 8)], trecv.at[at], (slab, sub))
    turns = [push(table.at[2], table.at[2 - d], wsend.at[n], wrecv.at[n], other(slab + d, sub))
             for n, d in enumerate((1, -1, 2, -2))]
    own[...] = x[0:24, :]
    copies += spread(slab, sub, x, near, send, recv)
    for n in range(6):
        values[n, :, :] = near[n, 0:24, :]
        spots[n, :, :] = near[n, 24:32, :]
    for copy in turns:
        copy.wait_recv()
    for copy in copies + turns:
        copy.wait_send()


def gather(forces, positions, rows, cols, count):
    return pl.pallas_call(
        gather_kernel,
        out_shape=(jax.ShapeDtypeStruct((6, 24, HALF), f32), jax.ShapeDtypeStruct((6, 8, HALF), f32),
                   jax.ShapeDtypeStruct((24, HALF), f32), jax.ShapeDtypeStruct((5, 32, 128), f32)),
        in_specs=[pl.BlockSpec(memory_space=pltpu.HBM)] * 4 + [SMEM],
        out_specs=(VMEM,) * 4,
        scratch_shapes=[pltpu.VMEM((12, 2 * HALF), f32), pltpu.VMEM((3, 2 * HALF), f32), pltpu.VMEM((1, 128), i32),
                        pltpu.VMEM((1, 128), i32), pltpu.SemaphoreType.DMA((4,)), pltpu.VMEM((6, 32, HALF), f32), pltpu.VMEM((32, HALF), f32), pltpu.VMEM((8, 128), f32)]
        + [pltpu.SemaphoreType.DMA((n,)) for n in (8, 12, 3, 4, 4, 4)],
        compiler_params=pltpu.CompilerParams(collective_id=0, has_side_effects=True, vmem_limit_bytes=40 * 2**20),
        name="gather_all",
    )(forces, positions, rows, cols, count)


def given(flow, counts):
    total = counts[0] + counts[1] + counts[2] + counts[3]
    whole = jnp.minimum(jnp.floor(jnp.maximum(flow, 0.0)), total)
    part = whole / jnp.maximum(total, 1.0)
    return [jnp.minimum(jnp.floor(part * n), n) for n in counts]


def plan_kernel(table, spots, out):
    slab, sub = place()
    lists = jnp.concatenate([spots[n, 6:7, 0:384] for n in range(6)] + [jnp.zeros((2, 384), f32)], axis=0)
    at = lambda rel, sub_at, kind: table[rel + 2, 8 * sub_at + kind:8 * sub_at + kind + 1, :]
    subs = range(N_SUB)
    total = {rel: sum(at(rel, v, 2) for v in subs) for rel in range(-2, 3)}
    first, last = slab == 0, slab == N_SLAB - 1

    def flow(a, b, c, d):
        return (a - d + 2.0 * (b - c)) * 0.2

    before = flow(jnp.where(slab == 1, total[-1], total[-2]), total[-1], total[0],
                  jnp.where(last, total[0], total[1]))
    after = flow(jnp.where(first, total[0], total[-1]), total[0], total[1],
                 jnp.where(slab == N_SLAB - 2, total[1], total[2]))
    before = jnp.where(first, 0.0, before)
    after = jnp.where(last, 0.0, after)
    ups = [at(0, v, 0) for v in subs]
    downs = [at(0, v, 1) for v in subs]
    up_given = given(after, ups)
    down_given = given(-before, downs)
    from_before = given(before, [at(-1, v, 0) for v in subs])
    from_after = given(-after, [at(1, v, 1) for v in subs])

    col = lists[:, 128:256]
    alive = lists[:, 256:384] > 0.5
    row_local = lists[:, :128]
    is_up = alive & (col >= 256.0)
    is_down = alive & (col < 128.0)
    is_own = alive & (col >= 128.0) & (col < 256.0)
    within = col - jnp.where(col >= 256.0, 256.0, jnp.where(col >= 128.0, 128.0, 0.0))
    col_sub = jnp.floor(within * (1.0 / SPAN))
    col_local = within - SPAN * col_sub
    masks = jnp.concatenate([m.astype(f32) for m in (is_up, is_down, is_own)], axis=0)
    lane_a = lax.broadcasted_iota(i32, (128, 128), 0)
    lane_b = lax.broadcasted_iota(i32, (128, 128), 1)
    ahead = (lane_a < lane_b).astype(bf16)
    rank = jnp.dot(masks.astype(bf16), ahead, preferred_element_type=f32)
    up_rank, down_rank, own_rank = rank[0:8], rank[8:16], rank[16:24]

    seat = lax.broadcasted_iota(i32, (8, 128), 0)

    def rows(values):
        full = jnp.zeros((8, 128), f32)
        for n, value in enumerate(values):
            full = jnp.where(seat == n, value, full)
        return full

    pick = lambda values: sum(jnp.where(sub == v, values[v], 0.0) for v in subs)
    up_limit = rows(up_given + [pick(from_before), jnp.zeros((1, 128), f32)])
    down_limit = rows(down_given + [jnp.zeros((1, 128), f32), pick(from_after)])
    up_sent = is_up & (up_rank < up_limit)
    down_sent = is_down & (down_rank < down_limit)
    in_slab = seat < 4
    crossing = in_slab & ((is_up & ~up_sent) | (is_down & ~down_sent))
    fixed = []
    for v in subs:
        kept = jnp.where(crossing & (col_sub == float(v)), 1.0, 0.0)
        fixed.append(jnp.sum(jnp.sum(kept, axis=0, keepdims=True), axis=1, keepdims=True)
                     + from_before[v] + from_after[v])
    own_counts = [at(0, v, 2) - ups[v] - downs[v] for v in subs]
    own_total = sum(own_counts)
    level = (sum(fixed) + own_total) * 0.25
    wish = [jnp.maximum(level - have, 0.0) for have in fixed]
    scale = own_total / jnp.maximum(sum(wish), 1.0)
    edges = [jnp.zeros((1, 128), f32)]
    run = jnp.zeros((1, 128), f32)
    for v in range(3):
        run = run + wish[v] * scale
        edges.append(jnp.minimum(jnp.floor(run + 0.5), own_total))
    edges.append(own_total)
    begin = pick(edges[:4])
    end = pick(edges[1:])
    start, offsets = jnp.zeros((1, 128), f32), []
    for v in subs:
        offsets.append(start)
        start = start + own_counts[v]
    place_own = own_rank + rows(offsets)
    mine = (crossing & (col_sub == sub.astype(f32))) | (
        in_slab & is_own & (place_own >= begin) & (place_own < end))
    mine = mine | ((seat == 4) & up_sent) | ((seat == 5) & down_sent)
    mine_value = mine.astype(f32)
    slot = jnp.dot(mine_value.astype(bf16), ahead, preferred_element_type=f32)
    counted = jnp.sum(mine_value, axis=1, keepdims=True)
    start, offsets = jnp.zeros((1, 1), f32), []
    for n in range(6):
        offsets.append(start)
        start = start + counted[n:n + 1]
    slot = slot + rows(offsets)
    slot = jnp.where(mine, slot, -1.0)
    row_near = row_local + SPAN * seat.astype(f32)
    inside = SPAN * col_sub + col_local
    col_near = jnp.where(in_slab, jnp.where(is_up, 160.0 + col_local, jnp.where(is_down, 128.0 + col_local, inside)),
                         inside)
    slot_t = jnp.transpose(slot, (1, 0))
    target = lax.broadcasted_iota(i32, (128, LIST), 1).astype(f32)
    result = jnp.zeros((16, LIST), f32)
    pad = jnp.zeros((14, 128), f32)
    for n in range(6):
        chosen = (slot_t[:, n:n + 1] == target).astype(bf16)
        values = jnp.concatenate([row_near[n:n + 1], col_near[n:n + 1], pad], axis=0).astype(bf16)
        result = result + jnp.dot(values, chosen, preferred_element_type=f32)
    lane_wide = lax.broadcasted_iota(i32, (1, LIST), 1).astype(f32)
    packed = jnp.where(lane_wide < start, result[0:1] * 256.0 + result[1:2], NEAR * 257.0)
    last_row = jnp.where(lane_b[0:1] == 0, start, 4.0 * slab.astype(f32) + 2.0)
    out[...] = jnp.concatenate([packed[:, 128 * n:128 * n + 128] for n in range(7)] + [last_row], axis=0).astype(i32)


def plan(table, spots):
    return pl.pallas_call(
        plan_kernel,
        out_shape=jax.ShapeDtypeStruct((8, 128), i32),
        in_specs=[VMEM, VMEM],
        out_specs=VMEM,
        compiler_params=pltpu.CompilerParams(vmem_limit_bytes=40 * 2**20),
        name="plan_tiles",
    )(table, spots)


UNIT = 0.5 ** 0.5
ISO = 0.25 * UNIT / (64.0 * UNIT**2) ** 2
DYAD = 3.0 * ISO


def mobility(xi, yi, zi, xj, yj, zj):
    dx, dy, dz = xi - xj, yi - yj, zi - zj
    q = jnp.maximum(dx * dx + dy * dy + dz * dz, 1e-12 * UNIT**2)
    inverse = lax.rsqrt(q)
    taper = jnp.maximum(64.0 * UNIT**2 - q, 0.0)
    weight = taper * taper
    square = inverse * inverse
    near = 4.0 / UNIT - 9.0 / 8.0 / UNIT**2 * (q * inverse)
    far = inverse * (3.0 + square)
    iso = weight * jnp.where(q < 4.0 * UNIT**2, near, far)
    capped = jnp.minimum(square, 0.5)
    dyad = weight * (capped * (1.0 - capped))
    return iso, dyad, (dx, dy, dz), inverse, q


CLOSE = 1.0 / (2e-3 * UNIT)


def two_parts(value):
    high = value.astype(bf16)
    return high, (value - high.astype(f32)).astype(bf16)


def block_store(ref, block, r, j, value, lane):
    if j == 0:
        ref[block, r:r + 8, 0:128] = value
    elif j == 2:
        ref[block + 1, r:r + 8, 0:128] = value
    else:
        swapped = pltpu.roll(value, 64, 1)
        ref[block, r:r + 8, 128:256] = jnp.where(lane < 64, value, swapped)
        ref[block + 1, r:r + 8, 128:256] = jnp.where(lane < 64, swapped, value)


def unpack_spots(spots, pos, centre):
    row = lax.broadcasted_iota(i32, (8, 128), 0)
    lane = lax.broadcasted_iota(i32, (8, 128), 1)
    middle = jnp.where(row < 2, centre, 3.0)
    pos[NEAR, :, :] = jnp.zeros((8, WIDE), f32)

    def pair_body(pair, _):
        start = pl.multiple_of(pair * 2 * BLOCK, 128)
        for at in range(6):
            for j in range(3):
                spot = (spots[at, :, pl.ds(start + 128 * j, 128)] - middle) * UNIT
                for half in range(2):
                    block = at * SPAN + half * 16 + pair * 2
                    block_store(pos, block, 0, j, spot if half == 0 else pltpu.roll(spot, 7, 0), lane)
        return 0

    lax.fori_loop(0, 8, pair_body, 0)


def unpack_values(sources, raw):
    row = lax.broadcasted_iota(i32, (8, 128), 0)
    lane = lax.broadcasted_iota(i32, (8, 128), 1)
    raw[NEAR, :, :] = jnp.zeros((16, WIDE), f32)

    def pair_body(pair, _):
        start = pl.multiple_of(pair * 2 * BLOCK, 128)
        for view, at in sources:
            for j in range(3):
                x, y, z = (view[8 * a:8 * a + 8, pl.ds(start + 128 * j, 128)] for a in range(3))
                for half in range(2):
                    if half == 0:
                        first, second = jnp.where(row < 4, x, pltpu.roll(y, 4, 0)), z
                    else:
                        first, second = jnp.where(row < 4, pltpu.roll(x, 4, 0), y), pltpu.roll(z, 4, 0)
                    block = at * SPAN + half * 16 + pair * 2
                    block_store(raw, block, 0, j, first, lane)
                    block_store(raw, block, 8, j, second, lane)
        return 0

    lax.fori_loop(0, 8, pair_body, 0)


def repack(acc, out):
    row = lax.broadcasted_iota(i32, (8, 128), 0)
    lane = lax.broadcasted_iota(i32, (8, 128), 1)

    def pair_body(pair, _):
        start = pl.multiple_of(pair * 2 * BLOCK, 128)
        for at in range(6):
            for j in range(3):
                got = []
                for half in range(2):
                    block = at * SPAN + half * 16 + pair * 2
                    for r in (0, 8):
                        if j == 0:
                            got.append(acc[block, r:r + 8, 0:128])
                        elif j == 2:
                            got.append(acc[block + 1, r:r + 8, 0:128])
                        else:
                            even, odd = acc[block, r:r + 8, 128:256], acc[block + 1, r:r + 8, 128:256]
                            got.append(jnp.where(lane < 64, even, odd)
                                       + pltpu.roll(jnp.where(lane < 64, odd, even), 64, 1))
                a0, a1, b0, b1 = got
                lanes = pl.ds(start + 128 * j, 128)
                out[at, 0:8, lanes] = jnp.where(row < 4, a0, pltpu.roll(b0, 4, 0))
                out[at, 8:16, lanes] = jnp.where(row < 4, pltpu.roll(a0, 4, 0), b0)
                out[at, 16:24, lanes] = jnp.where(row < 4, a1, pltpu.roll(b1, 4, 0))
        return 0

    lax.fori_loop(0, 8, pair_body, 0)


def worker(plan_ref, pos, nearest, turned, raw=None, acc=None, sides=None, extra=None):
    row = lax.broadcasted_iota(i32, (8, WIDE), 0)
    across = (((1,), (1,)), ((), ()))

    def tile_of(t):
        packed = plan_ref[t // 128, t % 128]
        return packed // 256, packed % 256

    def build(t, turn_ref, matrices):
        p, c = tile_of(t)
        xj, yj, zj = (pos[c, n:n + 1, :] for n in (0, 2, 4))
        least = jnp.full((8, 128), 64.0, f32)
        side = lax.broadcasted_iota(i32, (CHUNK, 128), 1) < BLOCK - 128
        main, rest = slice(0, 128), slice(128, WIDE)

        for u in range(0, BLOCK // 2, CHUNK):
            w = u + BLOCK // 2
            there = [[jnp.broadcast_to(turn_ref[v:v + CHUNK, n:n + 1], (CHUNK, 128)) for n in (0, 2, 4)]
                     for v in (u, w)]
            there.append([jnp.where(side, one, two) for one, two in zip(*there)])
            for r, at, lanes in zip((u, w, u + BLOCK), there, (main, main, rest)):
                iso, dyad, _, inverse, q = mobility(*at, xj[:, lanes], yj[:, lanes], zj[:, lanes])
                for m, value in enumerate((iso, dyad * jnp.minimum(inverse, CLOSE))):
                    high, low = two_parts(value)
                    matrices[2 * m, r:r + CHUNK, :] = high
                    matrices[2 * m + 1, r:r + CHUNK, :] = low
                least = jnp.minimum(least, jnp.minimum(q[:8], q[8:]))
                yield
        nearest[...] = jnp.minimum(nearest[...], jnp.where(p == c, 64.0, least))

    def patterns(block):
        x, y, z = (pos[block, n:n + 1, :] for n in (0, 2, 4))
        return x, y, z, jnp.where(row < 4, x, y)

    def columns(block):
        x, y, z, both = patterns(block)
        first, second = raw[block, 0:8, :], raw[block, 8:16, :]
        t = first * both
        s = t + pltpu.roll(t, 4, 0) + pltpu.roll(second * z, 4, 0)
        second = jnp.where(row < 4, second, s)
        full = jnp.concatenate([first, second] + [part * scale for scale in (x, y, z) for part in (first, second)], axis=0)
        high = full.astype(bf16)
        rest = full - high.astype(f32)
        middle, low = two_parts(rest)
        return high, middle, low

    def finish(iso, dyad, block):
        x, y, z, both = patterns(block)
        last = jnp.where(row < 4, z, -1.0)

        def folded(r):
            t = dyad[r:r + 8] * both + dyad[r + 8:r + 16] * last
            return t + pltpu.roll(t, 4, 0)

        along = folded(0)
        upper = both * along - jnp.where(row < 4, folded(16), folded(32))
        under = z * along - folded(48)
        return ISO * iso[0:8] + DYAD * upper, ISO * iso[8:16] + DYAD * under

    def ready(t, slot):
        for side, block in zip(sides[slot], reversed(tile_of(t))):
            for n, part in enumerate(columns(block)):
                side[64 * n:64 * n + 64, :] = part
                yield

    def turn_rows(t, turn_ref):
        turn_ref[...] = jnp.transpose(pos[tile_of(t)[0]], (1, 0))
        yield

    def summed(by_high, by_low):
        return (by_high[0:64] + by_low[0:64]) + (by_high[64:128] + by_low[64:128]) + by_high[128:192]

    def apply(t, slot, matrices):
        p, c = tile_of(t)
        side = lax.broadcasted_iota(i32, (1, 128), 1) < BLOCK - 128
        none = jnp.zeros((BLOCK // 2, 128), bf16)

        def whole(m):
            rest = matrices[m, BLOCK:, :]
            rest = jnp.concatenate([jnp.where(side, rest, none), jnp.where(side, none, rest)], axis=0)
            return jnp.concatenate([matrices[m, 0:BLOCK, :], rest], axis=1)

        iso_high, iso_low, dyad_high, dyad_low = (whole(m) for m in range(4))
        dot = lambda a, b: jnp.dot(a, b, preferred_element_type=f32)
        dot_across = lambda a, b: lax.dot_general(a, b, across, preferred_element_type=f32)
        wide = sides[slot][0][...]
        slim = jnp.concatenate([wide[n:n + 16] for n in (0, 64)], axis=0)
        pad = jnp.zeros((64, WIDE - BLOCK), f32)
        dyad = dot_across(wide, dyad_high)
        yield
        dyad = summed(dyad, dot_across(wide[:128], dyad_low))
        yield
        iso = dot_across(slim, iso_high) + dot_across(slim, iso_low)
        yield
        upper, under = finish(jnp.concatenate([iso[:16] + iso[16:], pad[:16]], axis=1), jnp.concatenate([dyad, pad], axis=1), p)
        acc[p, 0:8, :] += upper
        acc[p, 8:16, :] += under
        yield
        wide = sides[slot][1][:, :BLOCK]
        slim = jnp.concatenate([wide[n:n + 16] for n in (0, 64)], axis=0)
        dyad = dot(wide, dyad_high)
        yield
        dyad = summed(dyad, dot(wide[:128], dyad_low))
        yield
        iso = dot(slim, iso_high) + dot(slim, iso_low)
        yield
        upper, under = finish(iso[:16] + iso[16:], dyad, c)
        acc[c, 0:8, :] += upper
        acc[c, 8:16, :] += under
        yield

    def any_close(t):
        p, c = tile_of(t)
        turned[0][...] = jnp.transpose(pos[p], (1, 0))
        xj, yj, zj = (pos[c, n:n + 1, :] for n in (0, 2, 4))
        least = jnp.full((8, WIDE), 64.0, f32)
        for r in range(0, BLOCK, 8):
            xi, yi, zi = (turned[0][r:r + 8, m:m + 1] for m in (0, 2, 4))
            dx, dy, dz = xi - xj, yi - yj, zi - zj
            apart = dx * dx + dy * dy + dz * dz
            least = jnp.minimum(least, jnp.where(apart > 0.0, apart, 64.0))
        return jnp.min(least) < 1.01 / CLOSE**2

    def close_pairs(t):
        p, c = tile_of(t)
        turned[0][...] = jnp.transpose(pos[p], (1, 0))
        single = lax.broadcasted_iota(i32, (1, WIDE), 1) < BLOCK
        xj, yj, zj = (pos[c, n:n + 1, :] for n in (0, 2, 4))
        col_parts, row_parts = columns(c), columns(p)
        col_vec = jnp.concatenate([col_parts[0][:16], col_parts[1][:16]], axis=0)
        row_vec = jnp.concatenate([row_parts[0][:16], row_parts[1][:16]], axis=0)[:, :BLOCK]

        col_vec = jnp.where(single, col_vec, jnp.zeros_like(col_vec))

        def one(n, _):
            for r in range(0, BLOCK, CHUNK):
                xi, yi, zi = (turned[0][r:r + CHUNK, m:m + 1] for m in (0, 2, 4))
                _, dyad, offset, inverse, _ = mobility(xi, yi, zi, xj, yj, zj)
                rest = dyad * jnp.maximum(inverse - CLOSE, 0.0)
                along = jnp.where(n == 0, offset[0], jnp.where(n == 1, offset[1], offset[2]))
                high, low = two_parts(rest * along)
                extra[0][r:r + CHUNK, :] = high
                extra[1][r:r + CHUNK, :] = low
            h, l = extra[0][...], extra[1][...]
            to_row = (lax.dot_general(col_vec, h, across, preferred_element_type=f32)
                      + lax.dot_general(col_vec, l, across, preferred_element_type=f32))
            to_row = jnp.concatenate([to_row, jnp.zeros((32, WIDE - BLOCK), f32)], axis=1)
            to_col = (jnp.dot(row_vec, h, preferred_element_type=f32)
                      + jnp.dot(row_vec, l, preferred_element_type=f32))
            for block, got, sign in ((p, to_row, 1.0), (c, to_col, -1.0)):
                x, y, z, both = patterns(block)
                last = jnp.where(row < 4, z, -1.0)
                got = got[:16] + got[16:]
                folded = got[:8] * both + got[8:] * last
                folded = sign * DYAD * (folded + pltpu.roll(folded, 4, 0)) * single
                acc[block, 0:8, :] += jnp.where(row // 4 == n, folded, 0.0)
                acc[block, 8:16, :] += jnp.where(row // 4 + 2 == n, folded, 0.0)
            return 0

        lax.fori_loop(0, 3, one, 0)

    def drain(*steps):
        steps = list(steps)
        while steps:
            for step in list(steps):
                if next(step, steps) is steps:
                    steps.remove(step)

    return types.SimpleNamespace(tile_of=tile_of, build=build, ready=ready, turn_rows=turn_rows, apply=apply,
                                 close_pairs=close_pairs, any_close=any_close, drain=drain)


KEPT = 128
DEEP = 8


def finish_sweep(work, plan_ref, nearest, selves, acc, out):
    count = plan_ref[7, 0]
    found = jnp.min(nearest[...]) < 1.01 / CLOSE**2

    def look(t, _):
        p, c = work.tile_of(t)

        @pl.when(found | (p == c))
        def _():
            @pl.when(found | work.any_close(t))
            def _():
                work.close_pairs(t)
        return 0

    lax.fori_loop(0, jnp.where(found | (selves > 0) | (count > KEPT), count, 0), look, 0)
    repack(acc, out)


def begin_sweep(values, raw, acc):
    unpack_values([(values.at[n], n) for n in range(6)], raw)
    acc[...] = jnp.zeros_like(acc)


def first_kernel(plan_ref, values, spots, out, kept, nearest, pos, raw, acc, store, sem, *scratch):
    turned, sides, extra = scratch[0:2], (scratch[2:4], scratch[4:6]), scratch[6:8]
    work = worker(plan_ref, pos, nearest, turned, raw, acc, sides, extra)
    nearest[...] = jnp.full((8, 128), 64.0, f32)
    begin_sweep(values, raw, acc)
    unpack_spots(spots, pos, plan_ref[7, 1].astype(f32))
    count = plan_ref[7, 0]
    pairs = (count + 1) // 2

    def out_copy(t):
        slot = lax.rem(t, DEEP)
        return pltpu.make_async_copy(store.at[slot], kept.at[t], sem.at[slot])

    def wait_out(t):
        @pl.when((t >= 0) & (t < KEPT))
        def _():
            out_copy(t).wait()

    work.drain(work.turn_rows(0, turned[0]), work.turn_rows(1, turned[1]))
    work.drain(work.build(0, turned[0], store.at[0]), work.ready(0, 0))
    out_copy(0).start()

    def body(n, selves):
        t = 2 * n
        for k in range(2):
            wait_out(t + 1 + k - DEEP)
        for k in range(2):
            p, c = work.tile_of(t + k)
            selves = selves + (p == c).astype(i32)
            work.drain(work.apply(t + k, k, store.at[lax.rem(t + k, DEEP)]),
                       work.build(t + k + 1, turned[1 - k], store.at[lax.rem(t + k + 1, DEEP)]),
                       work.turn_rows(t + k + 2, turned[k]), work.ready(t + k + 1, 1 - k))
        for k in range(2):
            @pl.when(t + 1 + k < KEPT)
            def _():
                out_copy(t + 1 + k).start()
        return selves

    selves = lax.fori_loop(0, pairs, body, 0)
    finish_sweep(work, plan_ref, nearest, selves, acc, out)
    for k in range(DEEP):
        wait_out(2 * pairs + 1 - DEEP + k)


TILE = (4, BLOCK + BLOCK // 2, 128)


def first_sweep(plan_list, values, spots):
    side = pltpu.VMEM((BLOCK, WIDE), bf16)
    return pl.pallas_call(
        first_kernel,
        out_shape=(jax.ShapeDtypeStruct((6, 24, HALF), f32), jax.ShapeDtypeStruct((KEPT,) + TILE, bf16),
                   jax.ShapeDtypeStruct((8, 128), f32), jax.ShapeDtypeStruct((NEAR + 1, 8, WIDE), f32)),
        in_specs=[SMEM, VMEM, VMEM],
        out_specs=(VMEM, pl.BlockSpec(memory_space=pl.ANY), VMEM, VMEM),
        scratch_shapes=[
            pltpu.VMEM((NEAR + 1, 16, WIDE), f32),
            pltpu.VMEM((NEAR + 1, 16, WIDE), f32),
            pltpu.VMEM((DEEP,) + TILE, bf16),
            pltpu.SemaphoreType.DMA((DEEP,)),
        ]
        + [pltpu.VMEM((WIDE, 8), f32)] * 2
        + [side] * 6,
        compiler_params=pltpu.CompilerParams(vmem_limit_bytes=48 * 2**20),
        name="first_sweep",
    )(plan_list, values, spots)


def second_kernel(plan_ref, values, pos, kept, least, out, raw, acc, store, sem, *scratch):
    turned, sides, extra, nearest = scratch[0:2], (scratch[2:4], scratch[4:6]), scratch[6:8], scratch[8]
    work = worker(plan_ref, pos, nearest, turned, raw, acc, sides, extra)
    count = plan_ref[7, 0]
    pairs = (jnp.minimum(count, KEPT) + 1) // 2

    def in_copy(t):
        slot = lax.rem(t, DEEP)
        return pltpu.make_async_copy(kept.at[t], store.at[slot], sem.at[slot])

    for t in range(DEEP):
        @pl.when(t < 2 * pairs)
        def _():
            in_copy(t).start()

    nearest[...] = least[...]
    begin_sweep(values, raw, acc)
    work.drain(work.ready(0, 0))

    def body(n, selves):
        t = 2 * n
        for k in range(2):
            in_copy(t + k).wait()
        for k in range(2):
            p, c = work.tile_of(t + k)
            selves = selves + (p == c).astype(i32)
            work.drain(work.apply(t + k, k, store.at[lax.rem(t + k, DEEP)]), work.ready(t + k + 1, 1 - k))

        @pl.when(n + DEEP // 2 < pairs)
        def _():
            for k in range(2):
                in_copy(t + k + DEEP).start()
        return selves

    selves = lax.fori_loop(0, pairs, body, 0)

    @pl.when(count > KEPT)
    def _():
        def more(t, _):
            work.drain(work.turn_rows(t, turned[0]), work.ready(t, 0))
            work.drain(work.build(t, turned[0], store.at[0]))
            work.drain(work.apply(t, 0, store.at[0]))
            return 0

        lax.fori_loop(KEPT, count, more, 0)

    finish_sweep(work, plan_ref, nearest, selves, acc, out)


def second_sweep(plan_list, values, pos, kept, least):
    side = pltpu.VMEM((BLOCK, WIDE), bf16)
    return pl.pallas_call(
        second_kernel,
        out_shape=jax.ShapeDtypeStruct((6, 24, HALF), f32),
        in_specs=[SMEM, VMEM, VMEM, pl.BlockSpec(memory_space=pl.ANY), VMEM],
        out_specs=VMEM,
        scratch_shapes=[
            pltpu.VMEM((NEAR + 1, 16, WIDE), f32),
            pltpu.VMEM((NEAR + 1, 16, WIDE), f32),
            pltpu.VMEM((DEEP,) + TILE, bf16),
            pltpu.SemaphoreType.DMA((DEEP,)),
        ]
        + [pltpu.VMEM((WIDE, 8), f32)] * 2
        + [side] * 6
        + [pltpu.VMEM((8, 128), f32)],
        compiler_params=pltpu.CompilerParams(vmem_limit_bytes=48 * 2**20),
        name="second_sweep",
    )(plan_list, values, pos, kept, least)


def collect(slab, sub, parts, own, inbox, stage, send, recv):
    right, left = other(slab, sub + 1), other(slab, sub + 3)
    one, two, three = (lax.rem(sub + d, N_SUB) for d in range(1, 4))
    copies = []

    def half(what, at, lanes, to, n):
        copies.append(push(what, inbox.at[at, :, lanes], send.at[n], recv.at[2 * at + (lanes is LATE)], to))

    def wait_half(at, lanes):
        wait_for(inbox.at[at, :, lanes], recv.at[2 * at + (lanes is LATE)], (slab, sub))

    half(parts.at[two, :, EARLY], 0, EARLY, right, 0)
    half(parts.at[two, :, LATE], 1, LATE, left, 1)
    copies.append(push(parts.at[4], inbox.at[5], send.at[2], recv.at[10], other(slab - 1, sub)))
    copies.append(push(parts.at[5], inbox.at[4], send.at[3], recv.at[8], other(slab + 1, sub)))
    half(parts.at[one, :, LATE], 2, LATE, right, 4)
    half(parts.at[three, :, EARLY], 3, EARLY, left, 5)
    wait_half(0, EARLY)
    stage[0, :, :] = parts[one, :, EARLY] + inbox[0, :, EARLY]
    half(stage.at[0], 2, EARLY, right, 6)
    wait_half(1, LATE)
    stage[1, :, :] = parts[three, :, LATE] + inbox[1, :, LATE]
    half(stage.at[1], 3, LATE, left, 7)
    wait_for(inbox.at[4], recv.at[8], (slab, sub))
    wait_for(inbox.at[5], recv.at[10], (slab, sub))
    total = own[...] + parts[sub] + inbox[4] + inbox[5]
    for at in (2, 3):
        for lanes in (EARLY, LATE):
            wait_half(at, lanes)
    return copies, total + inbox[2] + inbox[3]


def greet_near(slab, sub, more=()):
    greet([other(slab, sub + d) for d in range(1, N_SUB)] + [other(slab + d, sub) for d in (1, -1)] + list(more))


def turn_kernel(parts, own, near, inbox, stage, total, send, recv, gsend, grecv):
    slab, sub = place()
    greet_near(slab, sub)
    copies, value = collect(slab, sub, parts, own, inbox, stage, send, recv)
    total[...] = value
    copies += spread(slab, sub, total, near, gsend, grecv)
    for copy in copies:
        copy.wait_send()


def turn(parts, own):
    return pl.pallas_call(
        turn_kernel,
        out_shape=jax.ShapeDtypeStruct((6, 24, HALF), f32),
        in_specs=[VMEM, VMEM],
        out_specs=VMEM,
        scratch_shapes=[pltpu.VMEM((6, 24, HALF), f32), pltpu.VMEM((2, 24, WIDTH), f32), pltpu.VMEM((24, HALF), f32)]
        + [pltpu.SemaphoreType.DMA((n,)) for n in (8, 12, 8, 12)],
        compiler_params=pltpu.CompilerParams(collective_id=1, has_side_effects=True, vmem_limit_bytes=40 * 2**20),
        name="turn_around",
    )(parts, own)


def squares(value):
    sq = value * value
    folded = sq[0:8] + sq[8:16] + sq[16:24]
    lanes = folded[:, 0:128]
    for n in range(1, HALF // 128):
        lanes = lanes + folded[:, 128 * n:128 * n + 128]
    return lanes


def finish_kernel(parts, first, out_first, out_second, inbox, stage, total_ref, box, send, recv, ssend, srecv):
    slab, sub = place()
    core = lax.rem(slab, 2)
    z = lax.rem(slab // 2, 4)
    y = slab // 8
    twin = slab + 1 - 2 * core
    groups = [[other(slab, sub + d) for d in range(1, 4)] + [other(twin, sub + d) for d in range(4)],
              [(lax.rem(y + e, 4) * 8 + lax.rem(z + d, 4) * 2 + core, sub) for e in range(4) for d in range(4) if d or e]]
    greet_near(slab, sub, groups[0][4:] + groups[1])
    copies, value = collect(slab, sub, parts, first, inbox, stage, send, recv)
    total_ref[...] = value
    box[0, 0, 0:8, :] = squares(first[...])
    box[0, 0, 8:16, :] = squares(value)
    for n, group in enumerate(groups):
        turns = []
        for m, peer in enumerate(group):
            turns.append(push(box.at[n, 0], box.at[n, m + 1], ssend.at[7 * n + m], srecv.at[7 * n + m], peer))
        for copy in turns:
            copy.wait_recv()
        copies += turns
        now = box[n, 0]
        for m in range(len(group)):
            now = now + box[n, m + 1]
        box[n + 1, 0, :, :] = now
    total = jnp.sum(box[2, 0], axis=1, keepdims=True)
    per = 1.0 / (3.0 * BLOCK * SPAN * N_SUB * N_SLAB)
    one, two = total[0:8], total[8:16]
    one = (one + pltpu.roll(jnp.broadcast_to(one, (8, 128)), 4, 0)) * per
    two = (two + pltpu.roll(jnp.broadcast_to(two, (8, 128)), 4, 0)) * per
    scale_one = lax.rsqrt(one + 1e-6)
    scale_two = scale_one * lax.rsqrt(scale_one * scale_one * two + 1e-6)
    for out, source, scale in ((out_first, first, scale_one), (out_second, total_ref, scale_two)):
        for a in range(3):
            value = source[8 * a:8 * a + 8, :] * scale[:, 0:1]
            for half in range(2):
                for k in range(4):
                    out[3 * k + a:3 * k + a + 1, half * HALF:half * HALF + HALF] = value[4 * half + k:4 * half + k + 1]
    for copy in copies:
        copy.wait_send()


def finish_all(parts, first):
    return pl.pallas_call(
        finish_kernel,
        out_shape=(jax.ShapeDtypeStruct((12, 2 * HALF), f32),) * 2,
        in_specs=[VMEM, VMEM],
        out_specs=(VMEM, VMEM),
        scratch_shapes=[pltpu.VMEM((6, 24, HALF), f32), pltpu.VMEM((2, 24, WIDTH), f32), pltpu.VMEM((24, HALF), f32),
                        pltpu.VMEM((3, 16, 16, 128), f32)]
        + [pltpu.SemaphoreType.DMA((n,)) for n in (8, 12, 22, 22)],
        compiler_params=pltpu.CompilerParams(collective_id=2, has_side_effects=True, vmem_limit_bytes=40 * 2**20),
        name="finish_all",
    )(parts, first)


def body(positions, forces, tile_rows, tile_cols, tile_count):
    _, sub = place()
    far = [pltpu.with_memory_space_constraint(v, pltpu.HBM)
           for v in (forces, positions, tile_rows[None], tile_cols[None])]
    values, spots, own, table = gather(*far, tile_count)
    plan_list = plan(table, spots)
    parts, kept, least, pos = first_sweep(plan_list, values, spots)
    near_second = turn(parts, own)
    parts = second_sweep(plan_list, near_second, pos, kept, least)
    first = lax.dynamic_index_in_dim(near_second, sub, 0, keepdims=False)
    return finish_all(parts, first)


def solution(mesh):
    placed = (
        P(None, ("slab", "sub")),
        P(None, ("slab", "sub")),
        P(("slab", "sub")),
        P(("slab", "sub")),
        P(("slab", "sub")),
    )
    return jax.shard_map(
        body,
        mesh=mesh,
        in_specs=placed,
        out_specs=(P(None, ("slab", "sub")), P(None, ("slab", "sub"))),
        check_vma=False,
    )
```
